128 devices in a mesh: grid: 8 (over x_lo, z), band: 16 (over y, x_hi, core).
Axes of the slice: x: 4 (x_hi: 2, x_lo: 2; x = x_hi * 2 + x_lo), y: 4, z: 4, core: 2. Of those that a mesh axis runs over, the one named last changes fastest.
Arguments:
- virtual_field: bfloat16 [2048, 64, 4096], P('band', 'grid'), may hold values from -6 to 6
- occupied_field: bfloat16 [256, 64, 4096], P('band', 'grid'), may hold values from -6 to 6
- amplitudes: bfloat16 [1, 2048, 2048], P(None, 'band', 'grid'), may hold values from -0.1875 to 0.1875
- ablock: int32 [1], replicated, may hold values from 0 to 31
- pairs: int32 [1, 2], replicated, may hold values from 0 to 255
- kept_cells: int32 [128, 512], P(('grid', 'band')), may hold values from 0 to 1023, as said below
Outputs:
- ladder: float32 [1, 2048, 64], P(None, ('grid', 'band'))
The draws below stay inside these ranges and needn't reach their ends.
Inputs may be any that keep to these rules, and one draw needn't show every extreme that they name: `kept_cells`: each row holds 512 distinct cells in rising order, and always holds 0 and 1023.
All inputs are finite; a program needn't handle non-finite values.
Results may differ from the reference program's by a relative error of at most 0.018.
Values may be sent and summed in bfloat16 or wider, within the bound.
No kernel may reach another device: no remote copies, remote signals or barrier semaphores. Data moves between devices by JAX's collectives and lax.ppermute only.
A program may use at most 256 MiB of HBM per device.

```python
import math
import jax
import jax.numpy as jnp
from jax import lax

NX = 64
NY = 64
NZ = 64
NV = 2048
NO = 256
ABLK = 64
PAIRS = 1
SHARDS = 128
CPD = 16
KEEP = 512


def draw_kept_cells(key, part):
    key = jax.random.fold_in(key, 7)
    cell_count = NX * CPD

    def one_row(row_key):
        shuffled = jax.random.permutation(row_key, cell_count - 2).astype(jnp.int32) + 1
        interior = shuffled[:KEEP - 2]
        ends = jnp.array([0, cell_count - 1], dtype=jnp.int32)
        return jnp.sort(jnp.concatenate([ends, interior]))
    row_keys = jax.random.split(key, SHARDS)
    return jax.vmap(one_row)(row_keys)


def spiked(entries, rng, source, target, blocks, factor):
    def block_of(dim):
        return (jnp.arange(entries.shape[dim]) // (entries.shape[dim] // blocks)).reshape((-1,) + (1,) * (entries.ndim - 1 - dim))

    near = jax.random.permutation(rng, blocks)[block_of(target)]
    other_side = (block_of(target) + blocks // 2) % blocks
    return jnp.where((block_of(source) == near) | (block_of(source) == other_side), factor * entries, entries)


def block_levels(rng, shape, shards, least, high):
    level = 1.0
    for position, blocks in shards:
        steps = jax.random.uniform(jax.random.fold_in(jax.random.fold_in(rng, 6), position), (blocks,), jnp.float32, least / len(shards), high / len(shards))
        level = level * jnp.repeat(jnp.exp(steps), shape[position] // blocks).reshape((-1,) + (1,) * (len(shape) - 1 - position))
    return level


def centred(stream_key, shape, width, limit, cuts=(), kind=jnp.bfloat16):
    entries = jax.random.normal(stream_key, shape, jnp.float32) * width
    if len(cuts) > 0:
        entries = block_levels(stream_key, shape, cuts, -0.22, 0.18) * entries
    return jnp.clip(entries, min=-limit, max=limit).astype(kind)


def noise_with(rng, dims, width, bound, cuts, heavy, kind=jnp.bfloat16):
    values = width * jax.random.normal(rng, dims, jnp.float32)
    if cuts:
        values = values * block_levels(rng, dims, cuts, -0.22, 0.18)
    return jnp.clip(spiked(values, jax.random.fold_in(rng, 3), *heavy), -bound, bound).astype(kind)


def setup_inputs(seed: int = 0) -> dict:
    keys = jax.random.split(jax.random.key(seed), 7)
    return {
        "virtual_field": centred(keys[0], (NV, NX, NY * NZ), 1.0, 6.0, ((0, 16), (1, 8))),
        "occupied_field": centred(keys[1], (NO, NX, NY * NZ), 1.0, 6.0, ((0, 16), (1, 8))),
        "amplitudes": noise_with(keys[2], (PAIRS, NV, NV), NV ** -0.5, 0.1875, ((1, 16), (2, 8)), (1, 2, 16, 2.0)),
        "ablock": jax.random.randint(keys[3], (1,), 0, NV // ABLK).astype(jnp.int32),
        "pairs": jax.random.randint(keys[4], (PAIRS, 2), 0, NO).astype(jnp.int32),
        "kept_cells": draw_kept_cells(jax.random.fold_in(keys[6], 71), 0),
    }


def twiddle_tables(length):
    wave_index = jnp.arange(length, dtype=jnp.int32)
    phase_index = wave_index[:, None] * wave_index[None, :] % length
    phase_angle = 2.0 * math.pi / length * phase_index.astype(jnp.float32)
    return (jnp.cos(phase_angle).astype(jnp.bfloat16), jnp.sin(phase_angle).astype(jnp.bfloat16))

def z_section(density):
    z_count = density.shape[-1]
    half_z = z_count // 2
    cosine_table, sine_table = twiddle_tables(z_count)
    z_table = jnp.concatenate([cosine_table[:half_z].T, -sine_table[:half_z].T], axis=1)
    result = jnp.einsum('bxyz,zq->bxyq', density.astype(jnp.float32), z_table.astype(jnp.float32), precision=lax.Precision.HIGHEST)
    return result.astype(jnp.bfloat16)

def y_section(zfreq):
    batch, x_count, y_count, z_count = zfreq.shape
    half_z = z_count // 2
    cosine_table, sine_table = twiddle_tables(y_count)
    source = zfreq.astype(jnp.float32)
    with_cosine = jnp.einsum('bxyq,ky->bxkq', source, cosine_table.astype(jnp.float32), precision=lax.Precision.HIGHEST)
    with_sine = jnp.einsum('bxyq,ky->bxkq', source, sine_table.astype(jnp.float32), precision=lax.Precision.HIGHEST)
    real_part = with_cosine[..., :half_z] + with_sine[..., half_z:]
    imag_part = with_cosine[..., half_z:] - with_sine[..., :half_z]
    stacked = jnp.stack([real_part, imag_part], axis=2)
    return stacked.reshape(batch, x_count, 2, y_count * half_z).astype(jnp.bfloat16)

def signed_freq(index, length):
    return (index + length // 2) % length - length // 2

def vertex_rows(fields, orbital, flat_cells, weights):
    density = (fields.astype(jnp.float32) * orbital.astype(jnp.float32)[None]).astype(jnp.bfloat16)
    yfreq = y_section(z_section(density)).astype(jnp.float32)
    cosine_table, sine_table = twiddle_tables(NX)
    with_cosine = jnp.einsum('bxtc,kx->bktc', yfreq, cosine_table.astype(jnp.float32), precision=lax.Precision.HIGHEST)
    with_sine = jnp.einsum('bxtc,kx->bktc', yfreq, sine_table.astype(jnp.float32), precision=lax.Precision.HIGHEST)
    real_part = with_cosine[:, :, 0] + with_sine[:, :, 1]
    imag_part = with_cosine[:, :, 1] - with_sine[:, :, 0]
    batch = fields.shape[0]
    real_kept = jnp.take(real_part.reshape(batch, -1), flat_cells, axis=1) * weights[None]
    imag_kept = jnp.take(imag_part.reshape(batch, -1), flat_cells, axis=1) * weights[None]
    return jnp.stack([real_kept, imag_kept], axis=1).astype(jnp.bfloat16).reshape(batch, -1)

def reference(virtual_field, occupied_field, amplitudes, ablock, pairs, kept_cells):
    virtual_field = virtual_field.reshape(NV, NX, NY, NZ)
    occupied_field = occupied_field.reshape(NO, NX, NY, NZ)
    half_z = NZ // 2
    shard_ids = jnp.arange(SHARDS, dtype=jnp.int32)[:, None]
    freq_x = kept_cells // CPD
    cell_flat = shard_ids * CPD + kept_cells % CPD
    flat_cells = (freq_x * (NY * half_z) + cell_flat).reshape(-1).astype(jnp.int32)
    freq_y = cell_flat // half_z
    freq_z = cell_flat % half_z
    squared = signed_freq(freq_x, NX) ** 2 + signed_freq(freq_y, NY) ** 2 + freq_z ** 2
    weights = (1.0 / jnp.sqrt(float(NX * NY * NZ) * (squared.astype(jnp.float32) + 1.0))).reshape(-1)
    block_start = (ablock[0] * ABLK).astype(jnp.int32)
    block_fields = lax.dynamic_slice_in_dim(virtual_field, block_start, ABLK, 0)
    band_rows = 128
    grouped = virtual_field.reshape(NV // band_rows, band_rows, NX, NY, NZ)
    results = []
    for pair_index in range(PAIRS):
        first_orbital = lax.dynamic_index_in_dim(occupied_field, pairs[pair_index, 0].astype(jnp.int32), 0, keepdims=False)
        second_orbital = lax.dynamic_index_in_dim(occupied_field, pairs[pair_index, 1].astype(jnp.int32), 0, keepdims=False)
        block_vertex = vertex_rows(block_fields, first_orbital, flat_cells, weights)

        def slab_part(fields):
            band_vertex = vertex_rows(fields, second_orbital, flat_cells, weights)
            return jnp.dot(block_vertex, band_vertex.T, preferred_element_type=jnp.float32)
        pieces = lax.map(slab_part, grouped)
        slab = jnp.transpose(pieces, (1, 0, 2)).reshape(ABLK, NV)
        slab_rounded = slab.astype(jnp.bfloat16)
        results.append(jnp.dot(amplitudes[pair_index].T, slab_rounded.T, preferred_element_type=jnp.float32))
    return jnp.stack(results)
```

```python
import functools
import math

import jax
import jax.numpy as jnp
import numpy as np
from jax import lax
from jax.experimental import pallas as pl
from jax.experimental.pallas import tpu as pltpu
from jax.sharding import PartitionSpec as P


N = 64
HALF = 32
ABLK = 64
GRID = 8
BAND = 16
XL = 8
SHARE = ABLK // BAND
PAIRS_Y = 32
F32 = jnp.float32
BF16 = jnp.bfloat16
VMEM_LIMIT = 56 * 1024 * 1024


@functools.cache
def tables():
    index = np.arange(N)
    phase = (index[:, None] * index[None, :]) % N
    angle = np.float32(2.0 * math.pi / N) * phase.astype(np.float32)
    cosine = np.cos(angle).astype(np.float32)
    sine = np.sin(angle).astype(np.float32)
    eye_x = np.eye(XL, dtype=np.float32)
    z_plain = np.concatenate([cosine[:HALF].T, -sine[:HALF].T], axis=1)
    z_turned = np.concatenate([z_plain[:, HALF:], -z_plain[:, :HALF]], axis=1)
    mz = np.zeros((SHARE, 2, N, 2, 2, SHARE, N), np.float32)
    for a in range(SHARE):
        for p in range(2):
            mz[a, p, :, 0, p, a, :] = z_plain
            mz[a, p, :, 1, p, a, :] = z_turned
    mzt = np.zeros((2, SHARE, N, SHARE, 2, N), np.float32)
    for a in range(SHARE):
        for p in range(2):
            mzt[p, a, :, a, p, :] = z_plain.T
    by_parity = np.stack([cosine, sine], axis=1).reshape(N, 2, PAIRS_Y, 2)
    ky = np.einsum("ktjp,xw->kxtpjw", by_parity, eye_x)
    signed = np.stack([cosine, -sine], axis=1).reshape(N, 2, PAIRS_Y, 2)
    kyt = np.einsum("ktjp,xw->pjxtkw", signed, eye_x)
    by_slab = np.stack([cosine, sine], axis=1).reshape(N, 2, GRID, XL)
    kx = np.einsum("ktgx,lm->kltgmx", by_slab, eye_x)
    signed_slab = np.stack([cosine, -sine], axis=1).reshape(N, 2, GRID, XL)
    kxt = np.einsum("ktgx,lm->gmxtkl", signed_slab, eye_x)
    turn = np.zeros((SHARE, 2, HALF, SHARE, 2, HALF), np.float32)
    for a in range(SHARE):
        turn[a, 1, :, a, 0, :] = np.eye(HALF)
        turn[a, 0, :, a, 1, :] = -np.eye(HALF)
    shapes = {
        "mz": (mz, 512, 1024),
        "mzt": (mzt, 512, 512),
        "ky": (ky, 512, 1024),
        "kyt": (kyt, 512, 1024),
        "kx": (kx, 512, 1024),
        "kxt": (kxt, 512, 1024),
        "turn": (turn, 256, 256),
    }
    return {n: v.reshape(r, c).astype(BF16) for n, (v, r, c) in shapes.items()}


def dot(a, b):
    return jnp.dot(a, b, preferred_element_type=F32)


def forward_body(u_ref, o_ref, mz_ref, ky_ref, out_ref):
    orbital = o_ref[...].astype(F32)
    columns = []
    for a in range(SHARE):
        density = u_ref[a].astype(F32) * orbital
        columns.append(
            jnp.concatenate([density[:, 128 * j : 128 * (j + 1)] for j in range(PAIRS_Y)], axis=0)
        )
    density = jnp.concatenate(columns, axis=1).astype(BF16)
    zfreq = dot(density, mz_ref[...]).astype(BF16)
    stacked = jnp.concatenate([zfreq[:, 256 * i : 256 * (i + 1)] for i in range(4)], axis=0)
    out_ref[...] = dot(ky_ref[...], stacked).astype(BF16)


def middle_body(y_ref, w_ref, turn_ref, kx_ref, kxt_ref, out_ref):
    turn = turn_ref[...]
    yfreq = y_ref[...]
    both = jnp.concatenate([yfreq, dot(yfreq, turn).astype(BF16)], axis=0)
    potential = (dot(kx_ref[...], both) * w_ref[...]).astype(BF16)
    both = jnp.concatenate([potential, dot(potential, turn).astype(BF16)], axis=0)
    out_ref[...] = dot(kxt_ref[...], both).astype(BF16)


def backward_body(h_ref, o_ref, turn_ref, kyt_ref, mzt_ref, out_ref):
    orbital = o_ref[...].astype(F32)
    freq = h_ref[...]
    both = jnp.concatenate([freq, dot(freq, turn_ref[...]).astype(BF16)], axis=0)
    zfreq = dot(kyt_ref[...], both).astype(BF16)
    zfreq = jnp.concatenate([zfreq[:256], zfreq[256:]], axis=1)
    value = dot(zfreq, mzt_ref[...])
    for a in range(SHARE):
        rows = [value[8 * j : 8 * (j + 1), 128 * a : 128 * (a + 1)] for j in range(PAIRS_Y)]
        out_ref[a] = (jnp.concatenate(rows, axis=1) * orbital).astype(BF16)


def whole_call(body, shape, dtype, *args):
    return pl.pallas_call(
        body,
        out_shape=jax.ShapeDtypeStruct(shape, dtype),
        in_specs=[pl.BlockSpec(memory_space=pltpu.VMEM)] * len(args),
        out_specs=pl.BlockSpec(memory_space=pltpu.VMEM),
        compiler_params=pltpu.CompilerParams(vmem_limit_bytes=VMEM_LIMIT),
    )(*args)


def slab_body(steps, pieces, *refs):
    place_ref, u_ref, amp_ref = refs[:3]
    w_refs = refs[3 : 3 + pieces]
    out_ref, total = refs[3 + pieces :]
    step = pl.program_id(0)

    @pl.when(step == 0)
    def _():
        total[...] = jnp.zeros_like(total)

    bands, _, lanes = u_ref.shape
    left = u_ref[...].reshape(bands * XL, lanes)
    right = jnp.concatenate([w[...].reshape(-1, lanes) for w in w_refs], axis=0)
    total[...] += lax.dot_general(left, right, (((1,), (1,)), ((), ())), preferred_element_type=F32)

    @pl.when(step == steps - 1)
    def _():
        gram = total[...]
        row = lax.broadcasted_iota(jnp.int32, gram.shape, 0) % XL
        col = lax.broadcasted_iota(jnp.int32, gram.shape, 1) % XL
        gram = jnp.where(row == col, gram, 0.0)
        gram = jnp.sum(gram.reshape(bands, XL, ABLK * XL), axis=1)
        halves = []
        for half in range(2):
            spot = place_ref[...] + ABLK * half
            lane = lax.broadcasted_iota(jnp.int32, (ABLK * XL, 128), 1)
            pick = (lane == spot).astype(F32)
            halves.append(jnp.dot(gram, pick, precision=lax.Precision.HIGHEST, preferred_element_type=F32))
        slab = jnp.concatenate(halves, axis=0)
        high = slab.astype(BF16)
        low = (slab - high.astype(F32)).astype(BF16)
        amp = amp_ref[...]
        out_ref[...] = (dot(amp, high) + dot(amp, low)).astype(BF16)


def slab_call(place, fields, amp, parts):
    bands = fields.shape[0]
    lanes = 512
    steps = N * N // lanes
    counts = [p.shape[0] for p in parts]
    return pl.pallas_call(
        functools.partial(slab_body, steps, len(parts)),
        out_shape=jax.ShapeDtypeStruct((1024, 128), BF16),
        grid=(steps,),
        in_specs=[
            pl.BlockSpec((ABLK * XL, 1), lambda s: (0, 0)),
            pl.BlockSpec((bands, XL, lanes), lambda s: (0, 0, s)),
            pl.BlockSpec((1024, 256), lambda s: (0, 0)),
        ]
        + [pl.BlockSpec((n, XL, lanes), lambda s: (0, 0, s)) for n in counts],
        out_specs=pl.BlockSpec((1024, 128), lambda s: (0, 0)),
        scratch_shapes=[pltpu.VMEM((bands * XL, ABLK * XL), F32)],
        compiler_params=pltpu.CompilerParams(vmem_limit_bytes=VMEM_LIMIT),
    )(place, fields, amp, *parts)


def band_shift(value, dy, dh, dc):
    pairs = []
    for y in range(4):
        for h in range(2):
            for c in range(2):
                pairs.append((4 * y + 2 * h + c, 4 * ((y + dy) % 4) + 2 * ((h + dh) % 2) + (c + dc) % 2))
    return lax.ppermute(value, "band", pairs)


def rows(value, start, count):
    return lax.dynamic_slice_in_dim(value, start, count, 0)


def signed_freq(index):
    return (index + N // 2) % N - N // 2


def per_device(virtual_field, occupied_field, amplitudes, ablock, pairs, kept_cells):
    const = {n: jnp.asarray(v) for n, v in tables().items()}
    band = lax.axis_index("band")
    grid = lax.axis_index("grid")
    my_y, my_h, my_c = band // 4, (band // 2) % 2, band % 2
    local_bands = virtual_field.shape[0]
    occ_local = occupied_field.shape[0]
    block_start = ablock[0] * ABLK
    owner = block_start // local_bands
    own_y, own_h, own_c = owner // 4, (owner // 2) % 2, owner % 2
    first = block_start % local_bands

    with jax.named_scope("block_scatter"):
        got = band_shift(rows(virtual_field, first + 32 * (1 - my_c), 32), 0, 0, 1)
        mine = rows(virtual_field, first + 32 * my_c, 32)
        mine = jnp.where(own_c == my_c, mine, got)
        cand = [rows(mine, 8 * my_y, 8)]
        for k in (1, 3, 2):
            cand.append(band_shift(rows(mine, 8 * ((my_y + k) % 4), 8), k, 0, 0))
        away = (my_y - own_y) % 4
        mine = jnp.where(
            away == 0, cand[0], jnp.where(away == 1, cand[1], jnp.where(away == 3, cand[2], cand[3]))
        )
        got = band_shift(rows(mine, 4 * (1 - my_h), 4), 0, 1, 0)
        mine = jnp.where(own_h == my_h, rows(mine, 4 * my_h, 4), got)

    with jax.named_scope("orbitals"):
        index = pairs[0]
        local = jnp.clip(index - band * occ_local, 0, occ_local - 1)
        chosen = jnp.concatenate([rows(occupied_field, local[k], 1) for k in range(2)], axis=0)
        chosen = chosen.reshape(2, XL, BAND, 256).transpose(2, 0, 1, 3)
        chosen = lax.all_to_all(chosen, "band", 0, 0, tiled=True)
        piece = [rows(chosen, index[k] // occ_local, 1)[0, k] for k in range(2)]
        kept = kept_cells[0]
        in_x = (kept[None, :] // 16 == jnp.arange(N, dtype=jnp.int32)[:, None]).astype(BF16)
        in_c = (kept[:, None] % 16 == jnp.arange(16, dtype=jnp.int32)[None, :]).astype(BF16)
        mask = dot(in_x, in_c).astype(BF16).reshape(XL, 128)
        mask = jnp.concatenate([mask, jnp.zeros_like(mask)], axis=1)
        piece = jnp.stack(piece + [mask])
        spread = lax.all_to_all(
            jnp.broadcast_to(piece[None], (BAND,) + piece.shape), "band", 0, 0, tiled=True
        )
        orbitals = spread[:, :2].transpose(1, 2, 0, 3).reshape(2, XL, N * N)
        masks = spread[:, 2, :, :128].reshape(BAND, N, 16).transpose(1, 0, 2).reshape(N * GRID, HALF)
        cell = jnp.arange(N * GRID, dtype=jnp.int32)[:, None]
        freq_x = signed_freq(cell // GRID)
        freq_y = signed_freq(grid * GRID + cell % GRID)
        freq_z = jnp.arange(HALF, dtype=jnp.int32)[None, :]
        squared = (freq_x**2 + freq_y**2 + freq_z**2).astype(F32)
        weights = masks.astype(F32) / (float(N * N * N) * (squared + 1.0))
        weights = jnp.tile(weights, (1, 2 * SHARE))

    with jax.named_scope("amplitudes"):
        amp = amplitudes[0].T.reshape(128, 256)
        amp = lax.all_gather(amp, "grid", axis=0, tiled=True)

    with jax.named_scope("transform"):
        freq = whole_call(forward_body, (512, 256), BF16, mine, orbitals[0], const["mz"], const["ky"])
        freq = lax.all_to_all(freq, "grid", 0, 0, tiled=True)
        freq = whole_call(
            middle_body, (512, 256), BF16, freq, weights, const["turn"], const["kx"], const["kxt"]
        )
        freq = lax.all_to_all(freq, "grid", 0, 0, tiled=True)
        potential = whole_call(
            backward_body,
            (SHARE, XL, N * N),
            BF16,
            freq,
            orbitals[1],
            const["turn"],
            const["kyt"],
            const["mzt"],
        )

    with jax.named_scope("block_gather"):
        near = [potential, band_shift(potential, 0, 1, 0)]
        parts = [(0, h, 0, v) for h, v in enumerate(near)]
        for h in range(2):
            for k in (1, 3, 2):
                parts.append((k, h, 0, band_shift(near[h], k, 0, 0)))
        parts += [(k, h, 1, band_shift(v, 0, 0, 1)) for k, h, _, v in parts]
        row = jnp.arange(SHARE * XL, dtype=jnp.int32) // XL
        place = jnp.concatenate(
            [32 * (my_c ^ c) + 8 * ((my_y - k) % 4) + 4 * (my_h ^ h) + row for k, h, c, _ in parts]
        )

    with jax.named_scope("slab_ladder"):
        terms = slab_call(place[:, None], virtual_field, amp, [v for *_, v in parts])
        terms = lax.all_to_all(
            terms.reshape(GRID * BAND, XL, 128), ("grid", "band"), 0, 0, tiled=True
        )
        ladder = jnp.sum(terms.astype(F32), axis=0)
        return ladder.reshape(1, 16, ABLK)


def solution(mesh):
    in_specs = (
        P("band", "grid", None),
        P("band", "grid", None),
        P(None, "band", "grid"),
        P(),
        P(),
        P(("grid", "band"), None),
    )
    out_specs = P(None, ("grid", "band"), None)
    return jax.shard_map(
        per_device, mesh=mesh, in_specs=in_specs, out_specs=out_specs, check_vma=False
    )
```

```python
import functools
import math

import jax
import jax.numpy as jnp
import numpy as np
from jax import lax
from jax.experimental import pallas as pl
from jax.experimental.pallas import tpu as pltpu
from jax.sharding import PartitionSpec as P


N = 64
HALF = 32
ABLK = 64
GRID = 8
BAND = 16
XL = 8
SHARE = ABLK // BAND
PAIRS_Y = 32
F32 = jnp.float32
BF16 = jnp.bfloat16
VMEM_LIMIT = 16 * 1024 * 1024


@functools.cache
def tables():
    index = np.arange(N)
    phase = (index[:, None] * index[None, :]) % N
    angle = np.float32(2.0 * math.pi / N) * phase.astype(np.float32)
    cosine = np.cos(angle).astype(np.float32)
    sine = np.sin(angle).astype(np.float32)
    eye_x = np.eye(XL, dtype=np.float32)
    z_plain = np.concatenate([cosine[:HALF].T, -sine[:HALF].T], axis=1)
    z_turned = np.concatenate([z_plain[:, HALF:], -z_plain[:, :HALF]], axis=1)
    mz = np.zeros((SHARE, 2, N, 2, 2, SHARE, N), np.float32)
    for a in range(SHARE):
        for p in range(2):
            mz[a, p, :, 0, p, a, :] = z_plain
            mz[a, p, :, 1, p, a, :] = z_turned
    mzt = np.zeros((2, SHARE, N, SHARE, 2, N), np.float32)
    for a in range(SHARE):
        for p in range(2):
            mzt[p, a, :, a, p, :] = z_plain.T
    by_parity = np.stack([cosine, sine], axis=1).reshape(N, 2, PAIRS_Y, 2)
    ky = np.einsum("ktjp,xw->kxtpjw", by_parity, eye_x)
    signed = np.stack([cosine, -sine], axis=1).reshape(N, 2, PAIRS_Y, 2)
    kyt = np.einsum("ktjp,xw->pjxtkw", signed, eye_x)
    by_slab = np.stack([cosine, sine], axis=1).reshape(N, 2, GRID, XL)
    kx = np.einsum("ktgx,lm->lktgmx", by_slab, eye_x)
    signed_slab = np.stack([cosine, -sine], axis=1).reshape(N, 2, GRID, XL)
    kxt = np.einsum("ktgx,lm->gmxtlk", signed_slab, eye_x)
    turn = np.zeros((SHARE, 2, HALF, SHARE, 2, HALF), np.float32)
    for a in range(SHARE):
        turn[a, 1, :, a, 0, :] = np.eye(HALF)
        turn[a, 0, :, a, 1, :] = -np.eye(HALF)
    shapes = {
        "mz": (mz, 512, 1024),
        "mzt": (mzt, 512, 512),
        "ky": (ky, 512, 1024),
        "kyt": (kyt, 512, 1024),
        "kx": (kx, 512, 1024),
        "kxt": (kxt, 512, 1024),
        "turn": (turn, 256, 256),
    }
    return {n: v.reshape(r, c).astype(BF16) for n, (v, r, c) in shapes.items()}


def dot(a, b):
    return jnp.dot(a, b, preferred_element_type=F32)


def signed_freq(index):
    return (index + N // 2) % N - N // 2


def position():
    band = lax.axis_index("band")
    return band // 4, (band // 2) % 2, band % 2


def root_of(device):
    return device // 4, (device // 2) % 2, device % 2


def copies(sems, jobs):
    waits = []
    for slot, (target, choices) in enumerate(jobs):
        for condition, source in choices:
            move = pltpu.make_async_copy(source, target, sems.at[slot])
            if condition is None:
                move.start()
            else:
                pl.when(condition)(move.start)
        waits.append(pltpu.make_async_copy(target, target, sems.at[slot]))
    return waits


def through(bounce, sems, jobs, between=None):
    inner, row = [], 0
    for target, choices in jobs:
        inner.append((bounce.at[row : row + target.shape[0]], choices))
        row += target.shape[0]
    moves = copies(sems, inner)
    out = between() if between else []
    for slot, move in enumerate(moves):
        move.wait()
        target = jobs[slot][0]
        out.append(pltpu.make_async_copy(inner[slot][0], target, sems.at[len(jobs) + slot]))
        out[-1].start()
    wait_all(out)


def added(marks, sems, groups):
    def between():
        moves, slot = [], 0
        for sources, _ in groups:
            part = [(marks.at[slot + i : slot + i + 1], [(None, v)]) for i, v in enumerate(sources)]
            moves.append((slot, copies(sems.at[slot : slot + len(part)], part)))
            slot += len(part)
        out = []
        for (first, waits), (sources, targets) in zip(moves, groups, strict=True):
            wait_all(waits)
            total = marks[first].astype(F32)
            for i in range(1, len(sources)):
                total += marks[first + i].astype(F32)
            marks[first] = total.astype(BF16)
            for target in targets:
                out.append(pltpu.make_async_copy(marks.at[first : first + 1], target, sems.at[slot]))
                out[-1].start()
                slot += 1
        return out

    return between


def wait_all(waits):
    for move in waits:
        move.wait()


class Roots:
    def __init__(self, ablock_ref, pairs_ref, fields, occupied):
        self.y, self.h, self.c = position()
        self.fields, self.occupied = fields, occupied
        start = ablock_ref[0] * ABLK
        self.first = start % fields.shape[0]
        devices = [start // fields.shape[0]]
        self.local = []
        for k in range(2):
            index = pairs_ref[0, k]
            devices.append(index // occupied.shape[0])
            self.local.append(index % occupied.shape[0])
        roots = [root_of(d) for d in devices]
        self.away = [(self.y - y + 4) % 4 for y, _, _ in roots]
        self.same_h = [h == self.h for _, h, _ in roots]
        self.same_c = [c == self.c for _, _, c in roots]

    def block(self, core, dy, h, count):
        start = self.first + 32 * core + 8 * ((self.y + dy) % 4) + 4 * h
        return self.fields.at[pl.ds(start, count)]

    def orbital(self, k):
        return self.occupied.at[pl.ds(self.local[k], 1)]


def send_core_body(
    ablock_ref, pairs_ref, kept_ref, fields, occupied, up, down, across, stay, orbitals, bounce, marks, sems
):
    def between():
        kept = kept_ref[...]
        in_x = (lax.broadcasted_iota(jnp.int32, (N, kept.shape[1]), 0) == kept // 16).astype(BF16)
        in_c = lax.broadcasted_iota(jnp.int32, (128, kept.shape[1]), 0) % 16 == kept % 16
        mask = lax.dot_general(
            in_x, in_c.astype(BF16), (((1,), (1,)), ((), ())), preferred_element_type=F32
        )
        row = lax.broadcasted_iota(jnp.int32, mask.shape, 0)
        lane = lax.broadcasted_iota(jnp.int32, mask.shape, 1)
        mask = jnp.where(row % XL == lane // 16, mask, 0.0)
        tile = jnp.sum(mask.reshape(XL, XL, 128), axis=1)
        here = lax.axis_index("band")
        tiles = [jnp.where(here == n, tile, 0.0) for n in range(2 * BAND)]
        marks[0] = jnp.concatenate(tiles, axis=1).astype(BF16)
        move = pltpu.make_async_copy(marks, orbitals.at[2:], sems.at[16])
        move.start()
        return [move]

    at = Roots(ablock_ref, pairs_ref, fields, occupied)
    other, here, there = 1 - at.c, at.h, 1 - at.h
    jobs = [
        (up, at.block(other, 1, 0, 8)),
        (down, at.block(other, 3, 0, 8)),
        (across.at[:4], at.block(other, 0, there, 4)),
        (across.at[4:], at.block(other, 2, there, 4)),
        (orbitals.at[:1], at.orbital(0)),
        (orbitals.at[1:2], at.orbital(1)),
        (stay.at[:4], at.block(other, 0, here, 4)),
        (stay.at[4:], at.block(other, 2, here, 4)),
    ]
    through(bounce, sems, [(t, [(None, v)]) for t, v in jobs], between)


def send_first_body(
    ablock_ref,
    pairs_ref,
    fields,
    occupied,
    got_up,
    got_down,
    got_across,
    sent_orbitals,
    got_orbitals,
    up,
    down,
    across,
    bounce,
    marks,
    sems,
):
    at = Roots(ablock_ref, pairs_ref, fields, occupied)
    there = 1 - at.h
    mine, theirs = at.same_c[0], jnp.logical_not(at.same_c[0])
    jobs = [
        (up.at[:8], [(mine, at.block(at.c, 1, 0, 8)), (theirs, got_up)]),
        (down.at[:8], [(mine, at.block(at.c, 3, 0, 8)), (theirs, got_down)]),
        (across.at[:4], [(mine, at.block(at.c, 0, there, 4)), (theirs, got_across.at[:4])]),
        (across.at[4:8], [(mine, at.block(at.c, 2, there, 4)), (theirs, got_across.at[4:])]),
    ]
    for target in (up, down, across):
        for k in range(2):
            own = at.same_c[1 + k]
            jobs.append(
                (
                    target.at[8 + k : 9 + k],
                    [(own, at.orbital(k)), (jnp.logical_not(own), got_orbitals.at[k : k + 1])],
                )
            )
    groups = [([sent_orbitals.at[2:], got_orbitals.at[2:]], [v.at[10:] for v in (up, down, across)])]
    through(bounce, sems, jobs, added(marks, sems.at[20:], groups))


def send_second_body(
    ablock_ref,
    pairs_ref,
    fields,
    occupied,
    got_stay,
    sent_orbitals,
    got_orbitals,
    crossed,
    below,
    above,
    far,
    turn,
    bounce,
    marks,
    sems,
):
    at = Roots(ablock_ref, pairs_ref, fields, occupied)
    not_ = jnp.logical_not
    here, there = at.h, 1 - at.h
    same_h, same_c = at.same_h[0], at.same_c[0]
    jobs = [
        (
            far.at[:4],
            [
                (same_h & same_c, at.block(at.c, 2, here, 4)),
                (same_h & not_(same_c), got_stay.at[4:]),
                (not_(same_h), crossed.at[4:8]),
            ],
        ),
        (
            turn.at[:4],
            [
                (at.away[0] == 1, below.at[pl.ds(4 * there, 4)]),
                (at.away[0] != 1, above.at[pl.ds(4 * there, 4)]),
            ],
        ),
    ]
    for k in range(2):
        same_h, same_c, away = at.same_h[1 + k], at.same_c[1 + k], at.away[1 + k]
        row = slice(8 + k, 9 + k)
        jobs.append(
            (
                far.at[4 + k : 5 + k],
                [
                    (same_h & same_c, at.orbital(k)),
                    (same_h & not_(same_c), got_orbitals.at[k : k + 1]),
                    (not_(same_h), crossed.at[row]),
                ],
            )
        )
        jobs.append((turn.at[4 + k : 5 + k], [(away == 1, below.at[row]), (away != 1, above.at[row])]))
    groups = [
        ([sent_orbitals.at[2:], got_orbitals.at[2:], crossed.at[10:]], [far.at[6:]]),
        ([below.at[10:], above.at[10:]], [turn.at[6:]]),
    ]
    through(bounce, sems, jobs, added(marks, sems.at[12:], groups))


def forward_body(
    ablock_ref,
    pairs_ref,
    fields,
    occupied,
    got_stay,
    got_orbitals,
    crossed,
    below,
    above,
    far,
    turned,
    mz_hbm,
    ky_hbm,
    out_ref,
    second_ref,
    u_ref,
    o_ref,
    mz_ref,
    ky_ref,
    sems,
):
    at = Roots(ablock_ref, pairs_ref, fields, occupied)
    not_ = jnp.logical_not

    def arrived(k, rows_far, near_own, near_core, near_cross, side, side_turned):
        away, same_h, same_c = at.away[k], at.same_h[k], at.same_c[k]
        return [
            ((away == 0) & same_h & same_c, near_own),
            ((away == 0) & same_h & not_(same_c), near_core),
            ((away == 0) & not_(same_h), near_cross),
            (away == 2, rows_far),
            ((away == 1) & same_h, below.at[side]),
            ((away == 3) & same_h, above.at[side]),
            ((away % 2 == 1) & not_(same_h), side_turned),
        ]

    jobs = [
        (
            u_ref,
            arrived(
                0,
                far.at[:4],
                at.block(at.c, 0, at.h, 4),
                got_stay.at[:4],
                crossed.at[:4],
                pl.ds(4 * at.h, 4),
                turned.at[:4],
            ),
        )
    ]
    for k, target in enumerate((o_ref, second_ref)):
        jobs.append(
            (
                target,
                arrived(
                    1 + k,
                    far.at[4 + k : 5 + k],
                    at.orbital(k),
                    got_orbitals.at[k : k + 1],
                    crossed.at[8 + k : 9 + k],
                    pl.ds(8 + k, 1),
                    turned.at[4 + k : 5 + k],
                ),
            )
        )
    jobs += [(mz_ref, [(None, mz_hbm)]), (ky_ref, [(None, ky_hbm)])]
    u_wait, o_wait, second_wait, mz_wait, ky_wait = copies(sems, jobs)
    u_wait.wait()
    o_wait.wait()
    orbital = o_ref[0].astype(F32)
    columns = []
    for a in range(SHARE):
        density = u_ref[a].astype(F32) * orbital
        columns.append(
            jnp.concatenate([density[:, 128 * j : 128 * (j + 1)] for j in range(PAIRS_Y)], axis=0)
        )
    density = jnp.concatenate(columns, axis=1).astype(BF16)
    mz_wait.wait()
    zfreq = dot(density, mz_ref[...]).astype(BF16)
    stacked = jnp.concatenate([zfreq[:, 256 * i : 256 * (i + 1)] for i in range(4)], axis=0)
    ky_wait.wait()
    out_ref[...] = dot(ky_ref[...], stacked).astype(BF16)
    second_wait.wait()


def middle_body(y_ref, weight_ref, turn_ref, kx_hbm, kxt_hbm, out_ref, kx_ref, kxt_ref, sems):
    kx_wait, kxt_wait = copies(sems, [(kx_ref, [(None, kx_hbm)]), (kxt_ref, [(None, kxt_hbm)])])
    turn = turn_ref[...]
    yfreq = y_ref[...]
    both = jnp.concatenate([yfreq, dot(yfreq, turn).astype(BF16)], axis=0)
    weights = jnp.concatenate([weight_ref[...], weight_ref[...]], axis=1)
    kx_wait.wait()
    potential = (dot(kx_ref[...], both) * weights).astype(BF16)
    both = jnp.concatenate([potential, dot(potential, turn).astype(BF16)], axis=0)
    kxt_wait.wait()
    out_ref[...] = dot(kxt_ref[...], both).astype(BF16)


def backward_body(h_ref, o_ref, turn_ref, kyt_hbm, mzt_hbm, out_ref, kyt_ref, mzt_ref, sems):
    kyt_wait, mzt_wait = copies(sems, [(kyt_ref, [(None, kyt_hbm)]), (mzt_ref, [(None, mzt_hbm)])])
    orbital = o_ref[0].astype(F32)
    freq = h_ref[...]
    both = jnp.concatenate([freq, dot(freq, turn_ref[...]).astype(BF16)], axis=0)
    kyt_wait.wait()
    zfreq = dot(kyt_ref[...], both).astype(BF16)
    zfreq = jnp.concatenate([zfreq[:256], zfreq[256:]], axis=1)
    mzt_wait.wait()
    value = dot(zfreq, mzt_ref[...])
    for a in range(SHARE):
        rows = [value[8 * j : 8 * (j + 1), 128 * a : 128 * (a + 1)] for j in range(PAIRS_Y)]
        out_ref[a] = (jnp.concatenate(rows, axis=1) * orbital).astype(BF16)


def weight_body(sent_orbitals, got_orbitals, crossed, below, above, far, turned, out_ref, marks, sems):
    sources = [sent_orbitals.at[2:], got_orbitals.at[2:], crossed.at[10:], below.at[10:], above.at[10:]]
    sources += [far.at[6:], turned.at[6:]]
    wait_all(copies(sems, [(marks.at[i : i + 1], [(None, v)]) for i, v in enumerate(sources)]))
    total = sum(marks[i].astype(F32) for i in range(len(sources)))
    tiles = jnp.concatenate([total[:, 128 * n : 128 * (n + 1)] for n in range(BAND)], axis=0).astype(BF16)
    shape = (BAND * N, BAND * XL)
    row = lax.broadcasted_iota(jnp.int32, shape, 0)
    lane = lax.broadcasted_iota(jnp.int32, shape, 1)
    spread = dot((row // XL == lane).astype(BF16), tiles)
    spread = jnp.where(row % XL == lane // 16, spread, 0.0).astype(BF16)
    row = lax.broadcasted_iota(jnp.int32, (128, 128), 0)
    lane = lax.broadcasted_iota(jnp.int32, (128, 128), 1)
    spread = dot(spread, (row % 16 == lane % 16).astype(BF16))
    low = lax.broadcasted_iota(jnp.int32, (N, 128), 1) % HALF < 16
    blocks = [spread[N * n : N * (n + 1)] for n in range(BAND)]
    kept = jnp.concatenate([jnp.where(low, blocks[2 * m], blocks[2 * m + 1]) for m in range(XL)], axis=0)
    shape = (N * XL, 128)
    row = lax.broadcasted_iota(jnp.int32, shape, 0)
    lane = lax.broadcasted_iota(jnp.int32, shape, 1)
    freq_x = signed_freq(row % N)
    freq_y = signed_freq(lax.axis_index("grid") * XL + row // N)
    freq_z = lane % HALF
    squared = (freq_x * freq_x + freq_y * freq_y + freq_z * freq_z).astype(F32)
    out_ref[...] = kept / (float(N * N * N) * (squared + 1.0))


def copy_body(source, target, sems):
    wait_all(copies(sems, [(target, [(None, source)])]))


SMEM, VMEM, HBM = pltpu.SMEM, pltpu.VMEM, pltpu.HBM
PLANE = (XL, N * N)


def call(body, spaces, outs, out_spaces, scratch, args, dtype=BF16):
    many = len(outs) > 1
    shapes = [jax.ShapeDtypeStruct(o, dtype) for o in outs]
    specs = [pl.BlockSpec(memory_space=m) for m in out_spaces]
    return pl.pallas_call(
        body,
        out_shape=shapes if many else shapes[0],
        in_specs=[pl.BlockSpec(memory_space=m) for m in spaces],
        out_specs=specs if many else specs[0],
        scratch_shapes=scratch,
        compiler_params=pltpu.CompilerParams(vmem_limit_bytes=VMEM_LIMIT),
    )(*args)


def slab_body(last, names, u_ref, *refs):
    pieces = 2 * len(names)
    w_refs, extra = refs[:pieces], refs[pieces:-2]
    out_ref, total = refs[-2:]
    lanes = 2048
    for s in range(N * N // lanes):
        part = pl.ds(s * lanes, lanes)
        right = jnp.concatenate([w[:, part] for w in w_refs], axis=0)
        gram = lax.dot_general(u_ref[:, part], right, (((1,), (1,)), ((), ())), preferred_element_type=F32)
        if s == 0:
            total[...] = gram
        else:
            total[...] += gram
    gram = total[...]
    wide = gram.shape[1]
    row = lax.broadcasted_iota(jnp.int32, gram.shape, 0) % XL
    col = lax.broadcasted_iota(jnp.int32, gram.shape, 1) % XL
    gram = jnp.where(row == col, gram, 0.0)
    gram = jnp.sum(gram.reshape(gram.shape[0] // XL, XL, wide), axis=1)
    y, h, c = position()
    row = lax.broadcasted_iota(jnp.int32, (SHARE * XL, 128), 0) // XL
    lane = lax.broadcasted_iota(jnp.int32, (SHARE * XL, 128), 1) % ABLK
    pick = []
    for dy, dh in names:
        for dc in range(2):
            first = 32 * ((c + dc) % 2) + 8 * ((y - dy + 4) % 4) + 4 * ((h + dh) % 2)
            pick.append((lane == first + row).astype(F32))
    pick = jnp.concatenate(pick, axis=0)
    slab = jnp.dot(gram, pick, precision=lax.Precision.HIGHEST, preferred_element_type=F32)
    if extra:
        slab = slab + extra[0][...]
    if not last:
        out_ref[...] = slab
    else:
        lane = lax.broadcasted_iota(jnp.int32, slab.shape, 1)
        zero = jnp.zeros_like(slab)
        slab = jnp.concatenate(
            [jnp.where(lane < ABLK, slab, zero), jnp.where(lane < ABLK, zero, slab)], axis=0
        )
        high = slab.astype(BF16)
        low = (slab - high.astype(F32)).astype(BF16)
        amp = extra[1][...].reshape(1024, 256)
        out_ref[...] = (dot(amp, high) + dot(amp, low)).astype(BF16)


def slab_call(names, fields, parts, extra=()):
    last = len(extra) > 1
    tall = fields.shape[0]
    wide = sum(p.shape[0] for p in parts)
    out = (1024, 128) if last else (tall // XL, 128)
    args = (fields, *parts, *extra)
    return pl.pallas_call(
        functools.partial(slab_body, last, names),
        out_shape=jax.ShapeDtypeStruct(out, BF16 if last else F32),
        in_specs=[pl.BlockSpec(memory_space=VMEM)] * len(args),
        out_specs=pl.BlockSpec(memory_space=VMEM),
        scratch_shapes=[VMEM((tall, wide), F32)],
        compiler_params=pltpu.CompilerParams(vmem_limit_bytes=24 * 1024 * 1024),
        cost_estimate=pl.CostEstimate(
            flops=2 * tall * wide * N * N, bytes_accessed=2 * tall * N * N, transcendentals=0
        ),
    )(*args)


def band_shift(value, dy, dh, dc):
    pairs = []
    for y in range(4):
        for h in range(2):
            for c in range(2):
                pairs.append((4 * y + 2 * h + c, 4 * ((y + dy) % 4) + 2 * ((h + dh) % 2) + (c + dc) % 2))
    return lax.ppermute(value, "band", pairs)


def per_device(virtual_field, occupied_field, amplitudes, ablock, pairs, kept_cells):
    far_memory = lambda v: pltpu.with_memory_space_constraint(v, HBM)
    const = {n: jnp.asarray(v) if n == "turn" else far_memory(jnp.asarray(v)) for n, v in tables().items()}
    roots = (ablock, pairs, far_memory(virtual_field), far_memory(occupied_field))
    root_spaces = [SMEM, SMEM, pl.ANY, pl.ANY]

    with jax.named_scope("block_scatter"):
        sems = lambda n: [pltpu.SemaphoreType.DMA((n,))]
        bounce = lambda n, marks, k: [VMEM((n,) + PLANE, BF16), VMEM((marks,) + PLANE, BF16)] + sems(k)
        eight = (8,) + PLANE
        sent = call(
            send_core_body,
            [SMEM, SMEM, VMEM, pl.ANY, pl.ANY],
            [eight] * 4 + [(3,) + PLANE],
            [pl.ANY] * 5,
            bounce(34, 1, 17),
            roots[:2] + (kept_cells,) + roots[2:],
        )
        order = (0, 1, 2, 4, 3)
        got = {k: band_shift(sent[k], 0, 0, 1) for k in order}
        sent_orbitals = sent[4]
        sent = call(
            send_first_body,
            root_spaces + [pl.ANY] * 5,
            [(11,) + PLANE] * 3,
            [pl.ANY] * 3,
            bounce(30, 2, 25),
            roots + (got[0], got[1], got[2], sent_orbitals, got[4]),
        )
        sent, amp = lax.optimization_barrier((sent, amplitudes[0]))
        amp = jnp.broadcast_to(amp.T.reshape(1, 128, 256), (GRID, 128, 256))
        crossed = band_shift(sent[2], 0, 1, 0)
        below = band_shift(sent[0], 1, 0, 0)
        above = band_shift(sent[1], 3, 0, 0)
        amp = lax.all_to_all(amp, "grid", 0, 0, tiled=True)
        sent = call(
            send_second_body,
            root_spaces + [pl.ANY] * 6,
            [(7,) + PLANE] * 2,
            [pl.ANY] * 2,
            bounce(12, 5, 19),
            roots + (got[3], sent_orbitals, got[4], crossed, below, above),
        )
        far = band_shift(sent[0], 2, 0, 0)
        turned = band_shift(sent[1], 0, 1, 0)
        far, turned, amp = lax.optimization_barrier((far, turned, amp))

    with jax.named_scope("transform"):
        big = VMEM((512, 1024), BF16)
        freq, second = call(
            forward_body,
            root_spaces + [pl.ANY] * 9,
            [(512, 256), (1,) + PLANE],
            [VMEM, VMEM],
            [VMEM((SHARE,) + PLANE, BF16), VMEM((1,) + PLANE, BF16), big, big] + sems(5),
            roots + (got[3], got[4], crossed, below, above, far, turned, const["mz"], const["ky"]),
        )
        freq = lax.all_to_all(freq, "grid", 0, 0, tiled=True)
        weights = call(
            weight_body,
            [pl.ANY] * 7,
            [(N * XL, 128)],
            [VMEM],
            [VMEM((7,) + PLANE, BF16)] + sems(7),
            (sent_orbitals, got[4], crossed, below, above, far, turned),
            F32,
        )
        freq = call(
            middle_body,
            [VMEM] * 3 + [pl.ANY] * 2,
            [(512, 256)],
            [VMEM],
            [big, big] + sems(2),
            (freq, weights, const["turn"], const["kx"], const["kxt"]),
        )
        freq = lax.all_to_all(freq, "grid", 0, 0, tiled=True)
        potential = call(
            backward_body,
            [VMEM] * 3 + [pl.ANY] * 2,
            [(SHARE,) + PLANE],
            [VMEM],
            [big, VMEM((512, 512), BF16)] + sems(2),
            (freq, second, const["turn"], const["kyt"], const["mzt"]),
        )

    with jax.named_scope("block_gather"):
        early, late = ((0, 0), (2, 0), (1, 0), (3, 0), (0, 1)), ((2, 1), (1, 1), (3, 1))
        shape = (virtual_field.shape[0] * XL, N * N)
        potential, fields = lax.optimization_barrier(
            (potential.reshape(SHARE * XL, N * N), virtual_field.reshape(shape))
        )
        fields = call(copy_body, [pl.ANY], [shape], [pl.ANY], sems(1), (far_memory(fields),))
        part = {(0, 0): potential}
        for k in (2, 1, 3):
            part[k, 0] = band_shift(potential, k, 0, 0)
        part[0, 1] = band_shift(potential, 0, 1, 0)

        def contract(names, *extra):
            pieces = [w for name in names for w in (part[name], band_shift(part[name], 0, 0, 1))]
            return slab_call(names, fields, pieces, extra)

        part[2, 0], part[0, 1], fields = lax.optimization_barrier((part[2, 0], part[0, 1], fields))
        part[2, 1] = band_shift(part[2, 0], 0, 1, 0)
        for k in (1, 3):
            part[k, 1] = band_shift(part[0, 1], k, 0, 0)
        slab = contract(early)
        *got, slab = lax.optimization_barrier([part[name] for name in late] + [slab])
        part.update(zip(late, got))
        terms = contract(late, slab, amp)

    with jax.named_scope("ladder"):
        terms = lax.all_to_all(
            terms.reshape(GRID * BAND, XL, 128), ("grid", "band"), 0, 0, tiled=True
        )
        ladder = jnp.sum(terms.astype(F32), axis=0)
        return ladder.reshape(1, 16, ABLK)


def solution(mesh):
    in_specs = (
        P("band", "grid", None),
        P("band", "grid", None),
        P(None, "band", "grid"),
        P(),
        P(),
        P(("grid", "band"), None),
    )
    out_specs = P(None, ("grid", "band"), None)
    return jax.shard_map(
        per_device, mesh=mesh, in_specs=in_specs, out_specs=out_specs, check_vma=False
    )
```

```python
import functools
import math

import jax
import jax.numpy as jnp
import numpy as np
from jax import lax
from jax.experimental import pallas as pl
from jax.experimental.pallas import tpu as pltpu
from jax.sharding import PartitionSpec as P


N = 64
HALF = 32
ABLK = 64
GRID = 8
BAND = 16
XL = 8
SHARE = ABLK // BAND
PAIRS_Y = 32
F32 = jnp.float32
BF16 = jnp.bfloat16
VMEM_LIMIT = 16 * 1024 * 1024


@functools.cache
def tables():
    index = np.arange(N)
    phase = (index[:, None] * index[None, :]) % N
    angle = np.float32(2.0 * math.pi / N) * phase.astype(np.float32)
    cosine = np.cos(angle).astype(np.float32)
    sine = np.sin(angle).astype(np.float32)
    eye_x = np.eye(XL, dtype=np.float32)
    z_plain = np.concatenate([cosine[:HALF].T, -sine[:HALF].T], axis=1)
    z_turned = np.concatenate([z_plain[:, HALF:], -z_plain[:, :HALF]], axis=1)
    mz = np.zeros((SHARE, 2, N, 2, 2, SHARE, N), np.float32)
    for a in range(SHARE):
        for p in range(2):
            mz[a, p, :, 0, p, a, :] = z_plain
            mz[a, p, :, 1, p, a, :] = z_turned
    mzt = np.zeros((2, SHARE, N, SHARE, 2, N), np.float32)
    for a in range(SHARE):
        for p in range(2):
            mzt[p, a, :, a, p, :] = z_plain.T
    by_parity = np.stack([cosine, sine], axis=1).reshape(N, 2, PAIRS_Y, 2)
    ky = np.einsum("ktjp,xw->kxtpjw", by_parity, eye_x)
    signed = np.stack([cosine, -sine], axis=1).reshape(N, 2, PAIRS_Y, 2)
    kyt = np.einsum("ktjp,xw->pjxtkw", signed, eye_x)
    by_slab = np.stack([cosine, sine], axis=1).reshape(N, 2, GRID, XL)
    kx = np.einsum("ktgx,lm->lktgmx", by_slab, eye_x)
    signed_slab = np.stack([cosine, -sine], axis=1).reshape(N, 2, GRID, XL)
    kxt = np.einsum("ktgx,lm->gmxtlk", signed_slab, eye_x)
    turn = np.zeros((SHARE, 2, HALF, SHARE, 2, HALF), np.float32)
    for a in range(SHARE):
        turn[a, 1, :, a, 0, :] = np.eye(HALF)
        turn[a, 0, :, a, 1, :] = -np.eye(HALF)
    shapes = {
        "mz": (mz, 512, 1024),
        "mzt": (mzt, 512, 512),
        "ky": (ky, 512, 1024),
        "kyt": (kyt, 512, 1024),
        "kx": (kx, 512, 1024),
        "kxt": (kxt, 512, 1024),
        "turn": (turn, 256, 256),
    }
    return {n: v.reshape(r, c).astype(BF16) for n, (v, r, c) in shapes.items()}


def dot(a, b):
    return jnp.dot(a, b, preferred_element_type=F32)


def signed_freq(index):
    return (index + N // 2) % N - N // 2


def position():
    band = lax.axis_index("band")
    return band // 4, (band // 2) % 2, band % 2


def root_of(device):
    return device // 4, (device // 2) % 2, device % 2


def copies(sems, jobs):
    waits = []
    for slot, (target, choices) in enumerate(jobs):
        for condition, source in choices:
            move = pltpu.make_async_copy(source, target, sems.at[slot])
            if condition is None:
                move.start()
            else:
                pl.when(condition)(move.start)
        waits.append(pltpu.make_async_copy(target, target, sems.at[slot]))
    return waits


def through(bounce, sems, jobs, start=None):
    inner, row = [], 0
    for target, choices in jobs:
        inner.append((bounce.at[row : row + target.shape[0]], choices))
        row += target.shape[0]
    moves = copies(sems, inner)
    finish = start() if start else None
    out = []
    for slot, move in enumerate(moves):
        move.wait()
        target = jobs[slot][0]
        out.append(pltpu.make_async_copy(inner[slot][0], target, sems.at[len(jobs) + slot]))
        out[-1].start()
    if finish:
        out += finish()
    wait_all(out)


def added(marks, sems, groups):
    def start():
        moves, slot = [], 0
        for sources, _ in groups:
            part = [(marks.at[slot + i : slot + i + 1], [(None, v)]) for i, v in enumerate(sources)]
            moves.append((slot, copies(sems.at[slot : slot + len(part)], part)))
            slot += len(part)
        return functools.partial(finish, moves, slot)

    def finish(moves, slot):
        out = []
        for (first, waits), (sources, targets) in zip(moves, groups, strict=True):
            wait_all(waits)
            total = marks[first].astype(F32)
            for i in range(1, len(sources)):
                total += marks[first + i].astype(F32)
            marks[first] = total.astype(BF16)
            for target in targets:
                out.append(pltpu.make_async_copy(marks.at[first : first + 1], target, sems.at[slot]))
                out[-1].start()
                slot += 1
        return out

    return start


def wait_all(waits):
    for move in waits:
        move.wait()


class Roots:
    def __init__(self, ablock_ref, pairs_ref, fields, occupied):
        self.y, self.h, self.c = position()
        self.fields, self.occupied = fields, occupied
        start = ablock_ref[0] * ABLK
        self.first = start % fields.shape[0]
        devices = [start // fields.shape[0]]
        self.local = []
        for k in range(2):
            index = pairs_ref[0, k]
            devices.append(index // occupied.shape[0])
            self.local.append(index % occupied.shape[0])
        roots = [root_of(d) for d in devices]
        self.away = [(self.y - y + 4) % 4 for y, _, _ in roots]
        self.same_h = [h == self.h for _, h, _ in roots]
        self.same_c = [c == self.c for _, _, c in roots]

    def block(self, core, dy, h, count):
        start = self.first + 32 * core + 8 * ((self.y + dy) % 4) + 4 * h
        return self.fields.at[pl.ds(start, count)]

    def orbital(self, k):
        return self.occupied.at[pl.ds(self.local[k], 1)]


def core_a_body(ablock_ref, pairs_ref, kept_hbm, fields, occupied, out, bounce, marks, kept_ref, sems):
    at = Roots(ablock_ref, pairs_ref, fields, occupied)
    other, there = 1 - at.c, 1 - at.h
    sources = [at.block(other, dy, there, 4) for dy in (1, 3, 2)]
    jobs = [(out.at[4 * i : 4 * i + 4], [(None, v)]) for i, v in enumerate(sources)]
    jobs.append((out.at[12:13], [(None, at.orbital(0))]))

    def start():
        (wait,) = copies(sems.at[9:], [(kept_ref, [(None, kept_hbm)])])
        return functools.partial(finish, wait)

    def finish(wait):
        wait.wait()
        kept = kept_ref[...]
        in_x = (lax.broadcasted_iota(jnp.int32, (N, kept.shape[1]), 0) == kept // 16).astype(BF16)
        in_c = lax.broadcasted_iota(jnp.int32, (128, kept.shape[1]), 0) % 16 == kept % 16
        mask = lax.dot_general(
            in_x, in_c.astype(BF16), (((1,), (1,)), ((), ())), preferred_element_type=F32
        )
        row = lax.broadcasted_iota(jnp.int32, mask.shape, 0)
        lane = lax.broadcasted_iota(jnp.int32, mask.shape, 1)
        mask = jnp.where(row % XL == lane // 16, mask, 0.0)
        tile = jnp.sum(mask.reshape(XL, XL, 128), axis=1)
        band = lax.axis_index("band")
        tiles = [jnp.where(band == n, tile, 0.0) for n in range(2 * BAND)]
        marks[0] = jnp.concatenate(tiles, axis=1).astype(BF16)
        move = pltpu.make_async_copy(marks, out.at[13:], sems.at[8])
        move.start()
        return [move]

    through(bounce, sems, jobs, start)


def core_b_body(ablock_ref, pairs_ref, fields, occupied, out, bounce, sems):
    at = Roots(ablock_ref, pairs_ref, fields, occupied)
    other, here, there = 1 - at.c, at.h, 1 - at.h
    sources = [at.block(other, dy, h, 4) for dy, h in ((1, here), (3, here), (0, there), (2, here), (0, here))]
    jobs = [(out.at[4 * i : 4 * i + 4], [(None, v)]) for i, v in enumerate(sources)]
    jobs.append((out.at[20:], [(None, at.orbital(1))]))
    through(bounce, sems, jobs)


def first_a_body(
    ablock_ref, pairs_ref, fields, occupied, sent_a, got_a, up, down, across, bounce, marks, sems
):
    at = Roots(ablock_ref, pairs_ref, fields, occupied)
    mine, theirs = at.same_c[0], jnp.logical_not(at.same_c[0])
    jobs = []
    for i, (target, dy) in enumerate(((up, 1), (down, 3), (across, 2))):
        own = at.block(at.c, dy, 1 - at.h, 4)
        jobs.append((target.at[:4], [(mine, own), (theirs, got_a.at[4 * i : 4 * i + 4])]))
    mine, theirs = at.same_c[1], jnp.logical_not(at.same_c[1])
    for target in (up, down, across):
        jobs.append((target.at[4:5], [(mine, at.orbital(0)), (theirs, got_a.at[12:13])]))
    groups = [([sent_a.at[13:], got_a.at[13:]], [v.at[5:] for v in (up, down, across)])]
    through(bounce, sems, jobs, added(marks, sems.at[12:], groups))


def first_b_body(ablock_ref, pairs_ref, fields, occupied, got_b, up, down, across, bounce, sems):
    at = Roots(ablock_ref, pairs_ref, fields, occupied)
    mine, theirs = at.same_c[0], jnp.logical_not(at.same_c[0])
    jobs = []
    for i, (target, dy, h) in enumerate(((up, 1, at.h), (down, 3, at.h), (across, 0, 1 - at.h))):
        own = at.block(at.c, dy, h, 4)
        jobs.append((target.at[:4], [(mine, own), (theirs, got_b.at[4 * i : 4 * i + 4])]))
    mine, theirs = at.same_c[2], jnp.logical_not(at.same_c[2])
    for target in (up, down, across):
        jobs.append((target.at[4:], [(mine, at.orbital(1)), (theirs, got_b.at[20:])]))
    through(bounce, sems, jobs)


def second_a_body(
    ablock_ref,
    pairs_ref,
    fields,
    occupied,
    sent_a,
    got_a,
    got_b,
    crossed,
    below,
    above,
    far,
    turn,
    bounce,
    marks,
    sems,
):
    at = Roots(ablock_ref, pairs_ref, fields, occupied)
    not_ = jnp.logical_not
    jobs = []
    own_rows = (at.block(at.c, 2, at.h, 4), got_b.at[12:16], slice(0, 4))
    own_orbital = (at.orbital(0), got_a.at[12:13], slice(4, 5))
    for k, (own, core, part) in enumerate((own_rows, own_orbital)):
        same_h, same_c = at.same_h[k], at.same_c[k]
        choices = [(same_h & same_c, own), (same_h & not_(same_c), core), (not_(same_h), crossed.at[part])]
        jobs.append((far.at[part], choices))
        from_below = at.away[k] == 1
        jobs.append((turn.at[part], [(from_below, below.at[part]), (not_(from_below), above.at[part])]))
    groups = [
        ([sent_a.at[13:], got_a.at[13:], crossed.at[5:]], [far.at[5:]]),
        ([below.at[5:], above.at[5:]], [turn.at[5:]]),
    ]
    through(bounce, sems, jobs, added(marks, sems.at[8:], groups))


def second_b_body(
    ablock_ref,
    pairs_ref,
    fields,
    occupied,
    got_b,
    crossed,
    below,
    above,
    amp_hbm,
    far,
    turn,
    amp_out,
    bounce,
    amp_ref,
    sems,
):
    at = Roots(ablock_ref, pairs_ref, fields, occupied)
    not_ = jnp.logical_not
    same_h, same_c, from_below = at.same_h[2], at.same_c[2], at.away[2] == 1
    choices = [
        (same_h & same_c, at.orbital(1)),
        (same_h & not_(same_c), got_b.at[20:]),
        (not_(same_h), crossed.at[4:]),
    ]
    jobs = [(far, choices), (turn, [(from_below, below.at[4:]), (not_(from_below), above.at[4:])])]
    (amp_wait,) = copies(sems.at[4:], [(amp_ref, [(None, amp_hbm.at[0])])])
    through(bounce, sems, jobs)
    amp_wait.wait()
    row = lax.broadcasted_iota(jnp.int32, (128, 256), 0)
    col = lax.broadcasted_iota(jnp.int32, (128, 256), 1)
    over_c = (((1,), (1,)), ((), ()))
    parity = [
        lax.dot_general((col == 2 * row + p).astype(BF16), amp_ref[...], over_c, preferred_element_type=F32)
        for p in range(2)
    ]
    amp_out[...] = jnp.concatenate(parity, axis=1).astype(BF16)


def arrived(at, k, own, core, cross, far, below, above, turned):
    not_ = jnp.logical_not
    away, same_h, same_c = at.away[k], at.same_h[k], at.same_c[k]
    return [
        ((away == 0) & same_h & same_c, own),
        ((away == 0) & same_h & not_(same_c), core),
        ((away == 0) & not_(same_h), cross),
        (away == 2, far),
        ((away == 1) & same_h, below),
        ((away == 3) & same_h, above),
        ((away % 2 == 1) & not_(same_h), turned),
    ]


def forward_body(
    ablock_ref,
    pairs_ref,
    fields,
    occupied,
    got_a,
    got_b,
    crossed_a,
    below_a,
    above_a,
    crossed_b,
    below_b,
    above_b,
    far,
    turned,
    amp_hbm,
    mz_hbm,
    ky_hbm,
    out_hbm,
    u_ref,
    o_ref,
    mz_ref,
    ky_ref,
    out_ref,
    amp_ref,
    sems,
):
    at = Roots(ablock_ref, pairs_ref, fields, occupied)
    rows = [v.at[:4] for v in (crossed_b, far, below_b, above_b, turned)]
    orbital = [v.at[4:5] for v in (crossed_a, far, below_a, above_a, turned)]
    jobs = [
        (u_ref, arrived(at, 0, at.block(at.c, 0, at.h, 4), got_b.at[16:20], *rows)),
        (o_ref, arrived(at, 1, at.orbital(0), got_a.at[12:13], *orbital)),
    ]
    jobs += [(mz_ref, [(None, mz_hbm)]), (ky_ref, [(None, ky_hbm)]), (amp_ref, [(None, amp_hbm)])]
    u_wait, o_wait, mz_wait, ky_wait, amp_wait = copies(sems, jobs)
    u_wait.wait()
    o_wait.wait()
    orbital = o_ref[0].astype(F32)
    columns = []
    for a in range(SHARE):
        density = u_ref[a].astype(F32) * orbital
        columns.append(
            jnp.concatenate([density[:, 128 * j : 128 * (j + 1)] for j in range(PAIRS_Y)], axis=0)
        )
    density = jnp.concatenate(columns, axis=1).astype(BF16)
    mz_wait.wait()
    zfreq = dot(density, mz_ref[...]).astype(BF16)
    stacked = jnp.concatenate([zfreq[:, 256 * i : 256 * (i + 1)] for i in range(4)], axis=0)
    ky_wait.wait()
    amp_wait.wait()
    jobs = [(out_hbm.at[g, pl.ds(64, 128)], [(None, amp_ref)]) for g in range(GRID)]
    out_waits = copies(sems.at[5:], jobs)
    out_ref[...] = dot(ky_ref[...], stacked).astype(BF16)
    jobs = [(out_hbm.at[g, pl.ds(0, 64)], [(None, out_ref.at[pl.ds(64 * g, 64)])]) for g in range(GRID)]
    wait_all(out_waits + copies(sems.at[13:], jobs))


def middle_body(
    y_hbm, weight_ref, turn_hbm, kx_hbm, kxt_hbm, out_hbm, y_ref, turn_ref, kx_ref, kxt_ref, out_ref, sems
):
    jobs = [(y_ref, y_hbm.at[:, pl.ds(0, 64)]), (turn_ref, turn_hbm), (kx_ref, kx_hbm), (kxt_ref, kxt_hbm)]
    y_wait, turn_wait, kx_wait, kxt_wait = copies(sems, [(t, [(None, v)]) for t, v in jobs])
    weights = jnp.concatenate([weight_ref[...], weight_ref[...]], axis=1)
    y_wait.wait()
    turn_wait.wait()
    turn = turn_ref[...]
    yfreq = y_ref[...].reshape(512, 256)
    both = jnp.concatenate([yfreq, dot(yfreq, turn).astype(BF16)], axis=0)
    kx_wait.wait()
    potential = (dot(kx_ref[...], both) * weights).astype(BF16)
    both = jnp.concatenate([potential, dot(potential, turn).astype(BF16)], axis=0)
    kxt_wait.wait()
    out_ref[...] = dot(kxt_ref[...], both).astype(BF16)
    wait_all(copies(sems.at[4:], [(out_hbm, [(None, out_ref)])]))


def backward_body(
    ablock_ref,
    pairs_ref,
    fields,
    occupied,
    got_b,
    crossed,
    below,
    above,
    far,
    turned,
    turn_hbm,
    kyt_hbm,
    mzt_hbm,
    h_ref,
    out_ref,
    o_ref,
    turn_ref,
    kyt_ref,
    mzt_ref,
    sems,
):
    at = Roots(ablock_ref, pairs_ref, fields, occupied)
    rows = [v.at[4:] for v in (crossed, below, above)]
    own, core = at.orbital(1), got_b.at[20:]
    jobs = [
        (o_ref, arrived(at, 2, own, core, rows[0], far, rows[1], rows[2], turned)),
        (turn_ref, [(None, turn_hbm)]),
        (kyt_ref, [(None, kyt_hbm)]),
        (mzt_ref, [(None, mzt_hbm)]),
    ]
    o_wait, turn_wait, kyt_wait, mzt_wait = copies(sems, jobs)
    freq = h_ref[...]
    turn_wait.wait()
    both = jnp.concatenate([freq, dot(freq, turn_ref[...]).astype(BF16)], axis=0)
    kyt_wait.wait()
    zfreq = dot(kyt_ref[...], both).astype(BF16)
    zfreq = jnp.concatenate([zfreq[:256], zfreq[256:]], axis=1)
    mzt_wait.wait()
    value = dot(zfreq, mzt_ref[...])
    o_wait.wait()
    orbital = o_ref[0].astype(F32)
    for a in range(SHARE):
        rows = [value[8 * j : 8 * (j + 1), 128 * a : 128 * (a + 1)] for j in range(PAIRS_Y)]
        out_ref[a] = (jnp.concatenate(rows, axis=1) * orbital).astype(BF16)


def weight_body(sent_a, got_a, crossed, below, above, far, turned, out_ref, marks, sems):
    sources = [sent_a.at[13:], got_a.at[13:]] + [v.at[5:] for v in (crossed, below, above, far, turned)]
    wait_all(copies(sems, [(marks.at[i : i + 1], [(None, v)]) for i, v in enumerate(sources)]))
    total = sum(marks[i].astype(F32) for i in range(len(sources)))
    tiles = jnp.concatenate([total[:, 128 * n : 128 * (n + 1)] for n in range(BAND)], axis=0).astype(BF16)
    shape = (BAND * N, BAND * XL)
    row = lax.broadcasted_iota(jnp.int32, shape, 0)
    lane = lax.broadcasted_iota(jnp.int32, shape, 1)
    spread = dot((row // XL == lane).astype(BF16), tiles)
    spread = jnp.where(row % XL == lane // 16, spread, 0.0).astype(BF16)
    row = lax.broadcasted_iota(jnp.int32, (128, 128), 0)
    lane = lax.broadcasted_iota(jnp.int32, (128, 128), 1)
    spread = dot(spread, (row % 16 == lane % 16).astype(BF16))
    low = lax.broadcasted_iota(jnp.int32, (N, 128), 1) % HALF < 16
    blocks = [spread[N * n : N * (n + 1)] for n in range(BAND)]
    kept = jnp.concatenate([jnp.where(low, blocks[2 * m], blocks[2 * m + 1]) for m in range(XL)], axis=0)
    shape = (N * XL, 128)
    row = lax.broadcasted_iota(jnp.int32, shape, 0)
    lane = lax.broadcasted_iota(jnp.int32, shape, 1)
    freq_x = signed_freq(row % N)
    freq_y = signed_freq(lax.axis_index("grid") * XL + row // N)
    freq_z = lane % HALF
    squared = (freq_x * freq_x + freq_y * freq_y + freq_z * freq_z).astype(F32)
    out_ref[...] = kept / (float(N * N * N) * (squared + 1.0))


def copy_body(source, target, sems):
    wait_all(copies(sems, [(target, [(None, source)])]))


SMEM, VMEM, HBM = pltpu.SMEM, pltpu.VMEM, pltpu.HBM
PLANE = (XL, N * N)


def call(body, spaces, outs, out_spaces, scratch, args, dtype=BF16, flops=10**8):
    many = len(outs) > 1
    shapes = [jax.ShapeDtypeStruct(o, dtype) for o in outs]
    specs = [pl.BlockSpec(memory_space=m) for m in out_spaces]
    return pl.pallas_call(
        body,
        out_shape=shapes if many else shapes[0],
        in_specs=[pl.BlockSpec(memory_space=m) for m in spaces],
        out_specs=specs if many else specs[0],
        scratch_shapes=scratch,
        compiler_params=pltpu.CompilerParams(vmem_limit_bytes=VMEM_LIMIT),
        cost_estimate=pl.CostEstimate(flops=flops, bytes_accessed=2**20, transcendentals=0),
    )(*args)


def slab_body(last, names, u_ref, *refs):
    pieces = 2 * len(names)
    w_refs, extra = refs[:pieces], refs[pieces:-2]
    out_ref, total = refs[-2:]
    lanes = 2048
    for s in range(N * N // lanes):
        part = pl.ds(s * lanes, lanes)
        right = jnp.concatenate([w[:, part] for w in w_refs], axis=0)
        gram = lax.dot_general(u_ref[:, part], right, (((1,), (1,)), ((), ())), preferred_element_type=F32)
        if s == 0:
            total[...] = gram
        else:
            total[...] += gram
    gram = total[...]
    wide = gram.shape[1]
    row = lax.broadcasted_iota(jnp.int32, gram.shape, 0) % XL
    col = lax.broadcasted_iota(jnp.int32, gram.shape, 1) % XL
    gram = jnp.where(row == col, gram, 0.0)
    gram = jnp.sum(gram.reshape(gram.shape[0] // XL, XL, wide), axis=1)
    y, h, c = position()
    row = lax.broadcasted_iota(jnp.int32, (SHARE * XL, 128), 0) // XL
    lane = lax.broadcasted_iota(jnp.int32, (SHARE * XL, 128), 1) % ABLK
    pick = []
    for dy, dh in names:
        for dc in range(2):
            first = 32 * ((c + dc) % 2) + 8 * ((y - dy + 4) % 4) + 4 * ((h + dh) % 2)
            pick.append((lane == first + row).astype(F32))
    pick = jnp.concatenate(pick, axis=0)
    slab = jnp.dot(gram, pick, precision=lax.Precision.HIGHEST, preferred_element_type=F32)
    if extra:
        slab = slab + extra[0][...]
    if not last:
        out_ref[...] = slab
    else:
        lane = lax.broadcasted_iota(jnp.int32, slab.shape, 1)
        zero = jnp.zeros_like(slab)
        slab = jnp.concatenate(
            [jnp.where(lane < ABLK, slab, zero), jnp.where(lane < ABLK, zero, slab)], axis=0
        )
        high = slab.astype(BF16)
        low = (slab - high.astype(F32)).astype(BF16)
        amp = extra[1][:, pl.ds(64, 128)].reshape(1024, 256)
        out_ref[...] = (dot(amp, high) + dot(amp, low)).astype(BF16)


def slab_call(names, fields, parts, extra=()):
    last = len(extra) > 1
    tall = fields.shape[0]
    wide = sum(p.shape[0] for p in parts)
    out = (1024, 128) if last else (tall // XL, 128)
    args = (fields, *parts, *extra)
    return pl.pallas_call(
        functools.partial(slab_body, last, names),
        out_shape=jax.ShapeDtypeStruct(out, BF16 if last else F32),
        in_specs=[pl.BlockSpec(memory_space=VMEM)] * len(args),
        out_specs=pl.BlockSpec(memory_space=VMEM),
        scratch_shapes=[VMEM((tall, wide), F32)],
        compiler_params=pltpu.CompilerParams(vmem_limit_bytes=24 * 1024 * 1024),
        cost_estimate=pl.CostEstimate(
            flops=2 * tall * wide * N * N, bytes_accessed=2 * tall * N * N, transcendentals=0
        ),
    )(*args)


def band_shift(value, dy, dh, dc):
    pairs = []
    for y in range(4):
        for h in range(2):
            for c in range(2):
                pairs.append((4 * y + 2 * h + c, 4 * ((y + dy) % 4) + 2 * ((h + dh) % 2) + (c + dc) % 2))
    return lax.ppermute(value, "band", pairs)


def per_device(virtual_field, occupied_field, amplitudes, ablock, pairs, kept_cells):
    far_memory = lambda v: pltpu.with_memory_space_constraint(v, HBM)
    const = {n: far_memory(jnp.asarray(v)) for n, v in tables().items()}
    roots = (ablock, pairs, far_memory(virtual_field), far_memory(occupied_field))
    root_spaces = [SMEM, SMEM, pl.ANY, pl.ANY]

    with jax.named_scope("block_scatter"):
        sems = lambda n: [pltpu.SemaphoreType.DMA((n,))]
        rows = lambda n: (n,) + PLANE
        held = lambda n: VMEM(rows(n), BF16)
        hop = lambda body, spaces, out, scratch, *args, flops=10**8: call(
            body, spaces, out, [pl.ANY] * len(out), scratch, args, flops=flops
        )
        any_ = [pl.ANY]
        sent_a = hop(
            core_a_body,
            root_spaces[:2] + any_ * 3,
            [rows(14)],
            [held(13), held(1), VMEM(kept_cells.shape, jnp.int32)] + sems(10),
            *roots[:2],
            far_memory(kept_cells),
            *roots[2:],
        )
        got_a = band_shift(sent_a, 0, 0, 1)
        sent_b = call(
            core_b_body, root_spaces, [rows(21)], any_, [held(21)] + sems(12), roots, flops=5 * 10**9
        )
        up, down, across = hop(
            first_a_body,
            root_spaces + any_ * 2,
            [rows(6)] * 3,
            [held(15), held(2)] + sems(17),
            *roots,
            sent_a,
            got_a,
        )
        up, down, across, sent_b = lax.optimization_barrier((up, down, across, sent_b))
        below_a = band_shift(up, 1, 0, 0)
        above_a = band_shift(down, 3, 0, 0)
        crossed_a = band_shift(across, 0, 1, 0)
        got_b = band_shift(sent_b, 0, 0, 1)
        up, down, across = hop(
            first_b_body, root_spaces + any_, [rows(5)] * 3, [held(15)] + sems(12), *roots, got_b
        )
        below_b = band_shift(up, 1, 0, 0)
        above_b = band_shift(down, 3, 0, 0)
        crossed_b = band_shift(across, 0, 1, 0)
        crossed_a, below_a, above_a, _ = lax.optimization_barrier((crossed_a, below_a, above_a, (up, down, across)))
        far, turn = hop(
            second_a_body,
            root_spaces + any_ * 6,
            [rows(6)] * 2,
            [held(10), held(5)] + sems(15),
            *roots,
            sent_a,
            got_a,
            got_b,
            crossed_a,
            below_a,
            above_a,
            flops=10**10,
        )
        far_a = band_shift(far, 2, 0, 0)
        turned_a = band_shift(turn, 0, 1, 0)
        crossed_b, below_b, above_b, _ = lax.optimization_barrier((crossed_b, below_b, above_b, (far, turn)))
        far, turn, amp = call(
            second_b_body,
            root_spaces + any_ * 5,
            [rows(1), rows(1), (128, 256)],
            any_ * 2 + [VMEM],
            [held(2), VMEM((128, 256), BF16)] + sems(5),
            (*roots, got_b, crossed_b, below_b, above_b, far_memory(amplitudes)),
            flops=10**10,
        )
        far_b = band_shift(far, 2, 0, 0)
        turned_b = band_shift(turn, 0, 1, 0)
        far_a, turned_a, amp = lax.optimization_barrier((far_a, turned_a, amp))

    with jax.named_scope("transform"):
        big = VMEM((512, 1024), BF16)
        from_all = (GRID, 64 + 128, 256)
        freq = call(
            forward_body,
            root_spaces + any_ * 13,
            [from_all],
            any_,
            [held(SHARE), held(1), big, big, VMEM((512, 256), BF16), VMEM((128, 256), BF16)] + sems(21),
            roots
            + (got_a, got_b, crossed_a, below_a, above_a, crossed_b, below_b, above_b, far_a, turned_a)
            + (amp, const["mz"], const["ky"]),
            flops=2 * 10**10,
        )
        freq = lax.all_to_all(freq, "grid", 0, 0, tiled=True)
        amp = freq
        weights = call(
            weight_body,
            any_ * 7,
            [(N * XL, 128)],
            [VMEM],
            [held(7)] + sems(7),
            tuple(far_memory(v) for v in (sent_a, got_a, crossed_a, below_a, above_a, far_a, turned_a)),
            F32,
        )
        freq = call(
            middle_body,
            any_ + [VMEM] + any_ * 3,
            [(512, 256)],
            any_,
            [VMEM((GRID, 64, 256), BF16), VMEM((256, 256), BF16), big, big, VMEM((512, 256), BF16)] + sems(5),
            (freq, weights, const["turn"], const["kx"], const["kxt"]),
            flops=10**10,
        )
        freq = lax.all_to_all(freq, "grid", 0, 0, tiled=True)
        potential = call(
            backward_body,
            root_spaces + any_ * 9 + [VMEM],
            [(SHARE,) + PLANE],
            [VMEM],
            [held(1), VMEM((256, 256), BF16), big, VMEM((512, 512), BF16)] + sems(4),
            roots
            + tuple(far_memory(v) for v in (got_b, crossed_b, below_b, above_b, far_b, turned_b))
            + (const["turn"], const["kyt"], const["mzt"], freq),
        )

    with jax.named_scope("block_gather"):
        early, late = ((0, 0), (2, 0), (1, 0), (3, 0), (0, 1)), ((2, 1), (1, 1), (3, 1))
        shape = (virtual_field.shape[0] * XL, N * N)
        potential, fields = lax.optimization_barrier(
            (potential.reshape(SHARE * XL, N * N), virtual_field.reshape(shape))
        )
        fields = call(copy_body, [pl.ANY], [shape], [pl.ANY], sems(1), (far_memory(fields),))
        part = {(0, 0): potential}
        for k in (2, 1, 3):
            part[k, 0] = band_shift(potential, k, 0, 0)
        part[0, 1] = band_shift(potential, 0, 1, 0)

        def contract(names, *extra):
            pieces = [w for name in names for w in (part[name], band_shift(part[name], 0, 0, 1))]
            return slab_call(names, fields, pieces, extra)

        part[2, 0], part[0, 1], fields = lax.optimization_barrier((part[2, 0], part[0, 1], fields))
        part[2, 1] = band_shift(part[2, 0], 0, 1, 0)
        for k in (1, 3):
            part[k, 1] = band_shift(part[0, 1], k, 0, 0)
        slab = contract(early)
        *got, slab = lax.optimization_barrier([part[name] for name in late] + [slab])
        part.update(zip(late, got))
        terms = contract(late, slab, amp)

    with jax.named_scope("ladder"):
        terms = lax.all_to_all(
            terms.reshape(GRID * BAND, XL, 128), ("grid", "band"), 0, 0, tiled=True
        )
        ladder = jnp.sum(terms.astype(F32), axis=0)
        return ladder.reshape(1, 16, ABLK)


def solution(mesh):
    in_specs = (
        P("band", "grid", None),
        P("band", "grid", None),
        P(None, "band", "grid"),
        P(),
        P(),
        P(("grid", "band"), None),
    )
    out_specs = P(None, ("grid", "band"), None)
    return jax.shard_map(
        per_device, mesh=mesh, in_specs=in_specs, out_specs=out_specs, check_vma=False
    )
```

```python
import functools
import math

import jax
import jax.numpy as jnp
import numpy as np
from jax import lax
from jax.experimental import pallas as pl
from jax.experimental.pallas import tpu as pltpu
from jax.sharding import PartitionSpec as P


N = 64
HALF = 32
ABLK = 64
GRID = 8
BAND = 16
XL = 8
SHARE = ABLK // BAND
PAIRS_Y = 32
F32 = jnp.float32
BF16 = jnp.bfloat16
VMEM_LIMIT = 16 * 1024 * 1024


@functools.cache
def tables():
    index = np.arange(N)
    phase = (index[:, None] * index[None, :]) % N
    angle = np.float32(2.0 * math.pi / N) * phase.astype(np.float32)
    cosine = np.cos(angle).astype(np.float32)
    sine = np.sin(angle).astype(np.float32)
    eye_x = np.eye(XL, dtype=np.float32)
    z_plain = np.concatenate([cosine[:HALF].T, -sine[:HALF].T], axis=1)
    z_turned = np.concatenate([z_plain[:, HALF:], -z_plain[:, :HALF]], axis=1)
    mz = np.zeros((SHARE, 2, N, 2, 2, SHARE, N), np.float32)
    for a in range(SHARE):
        for p in range(2):
            mz[a, p, :, 0, p, a, :] = z_plain
            mz[a, p, :, 1, p, a, :] = z_turned
    mzt = np.zeros((2, SHARE, N, SHARE, 2, N), np.float32)
    for a in range(SHARE):
        for p in range(2):
            mzt[p, a, :, a, p, :] = z_plain.T
    by_parity = np.stack([cosine, sine], axis=1).reshape(N, 2, PAIRS_Y, 2)
    ky = np.einsum("ktjp,xw->kxtpjw", by_parity, eye_x)
    signed = np.stack([cosine, -sine], axis=1).reshape(N, 2, PAIRS_Y, 2)
    kyt = np.einsum("ktjp,xw->pjxtkw", signed, eye_x)
    by_slab = np.stack([cosine, sine], axis=1).reshape(N, 2, GRID, XL)
    kx = np.einsum("ktgx,lm->lktgmx", by_slab, eye_x)
    signed_slab = np.stack([cosine, -sine], axis=1).reshape(N, 2, GRID, XL)
    kxt = np.einsum("ktgx,lm->gmxtlk", signed_slab, eye_x)
    turn = np.zeros((SHARE, 2, HALF, SHARE, 2, HALF), np.float32)
    for a in range(SHARE):
        turn[a, 1, :, a, 0, :] = np.eye(HALF)
        turn[a, 0, :, a, 1, :] = -np.eye(HALF)
    shapes = {
        "mz": (mz, 512, 1024),
        "mzt": (mzt, 512, 512),
        "ky": (ky, 512, 1024),
        "kyt": (kyt, 512, 1024),
        "kx": (kx, 512, 1024),
        "kxt": (kxt, 512, 1024),
        "turn": (turn, 256, 256),
    }
    return {n: v.reshape(r, c).astype(BF16) for n, (v, r, c) in shapes.items()}


def dot(a, b):
    return jnp.dot(a, b, preferred_element_type=F32)


def signed_freq(index):
    return (index + N // 2) % N - N // 2


def position():
    band = lax.axis_index("band")
    return band // 4, (band // 2) % 2, band % 2


def root_of(device):
    return device // 4, (device // 2) % 2, device % 2


def copies(sems, jobs):
    waits = []
    for slot, (target, choices) in enumerate(jobs):
        for condition, source in choices:
            move = pltpu.make_async_copy(source, target, sems.at[slot])
            if condition is None:
                move.start()
            else:
                pl.when(condition)(move.start)
        waits.append(pltpu.make_async_copy(target, target, sems.at[slot]))
    return waits


def gather(sems, jobs, start=None):
    finish = start() if start else None
    moves = copies(sems, jobs)
    if finish:
        moves += finish()
    wait_all(moves)


def added(marks, sems, groups):
    def start():
        moves, slot = [], 0
        for sources, _ in groups:
            part = [(marks.at[slot + i : slot + i + 1], [(None, v)]) for i, v in enumerate(sources)]
            moves.append((slot, copies(sems.at[slot : slot + len(part)], part)))
            slot += len(part)
        return functools.partial(finish, moves, slot)

    def finish(moves, slot):
        out = []
        for (first, waits), (sources, targets) in zip(moves, groups, strict=True):
            wait_all(waits)
            total = marks[first].astype(F32)
            for i in range(1, len(sources)):
                total += marks[first + i].astype(F32)
            marks[first] = total.astype(BF16)
            for target in targets:
                out.append(pltpu.make_async_copy(marks.at[first : first + 1], target, sems.at[slot]))
                out[-1].start()
                slot += 1
        return out

    return start


def wait_all(waits):
    for move in waits:
        move.wait()


class Roots:
    def __init__(self, ablock_ref, pairs_ref, fields, occupied):
        self.y, self.h, self.c = position()
        self.fields, self.occupied = fields, occupied
        start = ablock_ref[0] * ABLK
        self.first = start % fields.shape[0]
        devices = [start // fields.shape[0]]
        self.local = []
        for k in range(2):
            index = pairs_ref[0, k]
            devices.append(index // occupied.shape[0])
            self.local.append(index % occupied.shape[0])
        roots = [root_of(d) for d in devices]
        self.away = [(self.y - y + 4) % 4 for y, _, _ in roots]
        self.same_h = [h == self.h for _, h, _ in roots]
        self.same_c = [c == self.c for _, _, c in roots]

    def block(self, core, dy, h, count):
        start = self.first + 32 * core + 8 * ((self.y + dy) % 4) + 4 * h
        return self.fields.at[pl.ds(start, count)]

    def orbital(self, k):
        return self.occupied.at[pl.ds(self.local[k], 1)]


def core_a_body(ablock_ref, pairs_ref, kept_hbm, fields, occupied, out, marks, kept_ref, sems):
    at = Roots(ablock_ref, pairs_ref, fields, occupied)
    other, there = 1 - at.c, 1 - at.h
    sources = [at.block(other, dy, there, 4) for dy in (1, 3, 2)]
    jobs = [(out.at[4 * i : 4 * i + 4], [(None, v)]) for i, v in enumerate(sources)]
    jobs.append((out.at[12:13], [(None, at.orbital(0))]))

    def start():
        (wait,) = copies(sems.at[9:], [(kept_ref, [(None, kept_hbm)])])
        return functools.partial(finish, wait)

    def finish(wait):
        wait.wait()
        kept = kept_ref[...]
        in_x = (lax.broadcasted_iota(jnp.int32, (N, kept.shape[1]), 0) == kept // 16).astype(BF16)
        in_c = lax.broadcasted_iota(jnp.int32, (128, kept.shape[1]), 0) % 16 == kept % 16
        mask = lax.dot_general(
            in_x, in_c.astype(BF16), (((1,), (1,)), ((), ())), preferred_element_type=F32
        )
        row = lax.broadcasted_iota(jnp.int32, mask.shape, 0)
        lane = lax.broadcasted_iota(jnp.int32, mask.shape, 1)
        mask = jnp.where(row % XL == lane // 16, mask, 0.0)
        tile = jnp.sum(mask.reshape(XL, XL, 128), axis=1)
        band = lax.axis_index("band")
        tiles = [jnp.where(band == n, tile, 0.0) for n in range(2 * BAND)]
        marks[0] = jnp.concatenate(tiles, axis=1).astype(BF16)
        move = pltpu.make_async_copy(marks, out.at[13:], sems.at[8])
        move.start()
        return [move]

    gather(sems, jobs, start)


def core_b_body(ablock_ref, pairs_ref, fields, occupied, amp_hbm, out, amp_out, amp_ref, sems):
    at = Roots(ablock_ref, pairs_ref, fields, occupied)
    other, here, there = 1 - at.c, at.h, 1 - at.h
    sources = [at.block(other, dy, h, 4) for dy, h in ((1, here), (3, here), (0, there), (2, here), (0, here))]
    jobs = [(out.at[4 * i : 4 * i + 4], [(None, v)]) for i, v in enumerate(sources)]
    jobs.append((out.at[20:], [(None, at.orbital(1))]))
    moves = copies(sems, jobs)
    (amp_wait,) = copies(sems.at[6:], [(amp_ref, [(None, amp_hbm.at[0])])])
    amp_wait.wait()
    row = lax.broadcasted_iota(jnp.int32, (128, 256), 0)
    col = lax.broadcasted_iota(jnp.int32, (128, 256), 1)
    over_c = (((1,), (1,)), ((), ()))
    parity = [
        lax.dot_general((col == 2 * row + p).astype(BF16), amp_ref[...], over_c, preferred_element_type=F32)
        for p in range(2)
    ]
    amp_out[...] = jnp.concatenate(parity, axis=1).astype(BF16)
    wait_all(moves)


def first_a_body(
    ablock_ref, pairs_ref, fields, occupied, sent_a, got_a, up, down, across, marks, sems
):
    at = Roots(ablock_ref, pairs_ref, fields, occupied)
    mine, theirs = at.same_c[0], jnp.logical_not(at.same_c[0])
    jobs = []
    for i, (target, dy) in enumerate(((up, 1), (down, 3), (across, 2))):
        own = at.block(at.c, dy, 1 - at.h, 4)
        jobs.append((target.at[:4], [(mine, own), (theirs, got_a.at[4 * i : 4 * i + 4])]))
    mine, theirs = at.same_c[1], jnp.logical_not(at.same_c[1])
    for target in (up, down, across):
        jobs.append((target.at[4:5], [(mine, at.orbital(0)), (theirs, got_a.at[12:13])]))
    groups = [([sent_a.at[13:], got_a.at[13:]], [v.at[5:] for v in (up, down, across)])]
    gather(sems, jobs, added(marks, sems.at[12:], groups))


def first_b_body(ablock_ref, pairs_ref, fields, occupied, got_b, up, down, across, sems):
    at = Roots(ablock_ref, pairs_ref, fields, occupied)
    mine, theirs = at.same_c[0], jnp.logical_not(at.same_c[0])
    jobs = []
    for i, (target, dy, h) in enumerate(((up, 1, at.h), (down, 3, at.h), (across, 0, 1 - at.h))):
        own = at.block(at.c, dy, h, 4)
        jobs.append((target.at[:4], [(mine, own), (theirs, got_b.at[4 * i : 4 * i + 4])]))
    mine, theirs = at.same_c[2], jnp.logical_not(at.same_c[2])
    for target in (up, down, across):
        jobs.append((target.at[4:], [(mine, at.orbital(1)), (theirs, got_b.at[20:])]))
    gather(sems, jobs)


def second_a_body(
    ablock_ref,
    pairs_ref,
    fields,
    occupied,
    sent_a,
    got_a,
    got_b,
    crossed,
    below,
    above,
    far,
    turn,
    marks,
    sems,
):
    at = Roots(ablock_ref, pairs_ref, fields, occupied)
    not_ = jnp.logical_not
    jobs = []
    own_rows = (at.block(at.c, 2, at.h, 4), got_b.at[12:16], slice(0, 4))
    own_orbital = (at.orbital(0), got_a.at[12:13], slice(4, 5))
    for k, (own, core, part) in enumerate((own_rows, own_orbital)):
        same_h, same_c = at.same_h[k], at.same_c[k]
        choices = [(same_h & same_c, own), (same_h & not_(same_c), core), (not_(same_h), crossed.at[part])]
        jobs.append((far.at[part], choices))
        from_below = at.away[k] == 1
        jobs.append((turn.at[part], [(from_below, below.at[part]), (not_(from_below), above.at[part])]))
    groups = [
        ([sent_a.at[13:], got_a.at[13:], crossed.at[5:]], [far.at[5:]]),
        ([below.at[5:], above.at[5:]], [turn.at[5:]]),
    ]
    gather(sems, jobs, added(marks, sems.at[8:], groups))


def arrived(at, k, own, core, cross, far, below, above, turned):
    not_ = jnp.logical_not
    away, same_h, same_c = at.away[k], at.same_h[k], at.same_c[k]
    return [
        ((away == 0) & same_h & same_c, own),
        ((away == 0) & same_h & not_(same_c), core),
        ((away == 0) & not_(same_h), cross),
        (away == 2, far),
        ((away == 1) & same_h, below),
        ((away == 3) & same_h, above),
        ((away % 2 == 1) & not_(same_h), turned),
    ]


def forward_body(
    ablock_ref,
    pairs_ref,
    fields,
    occupied,
    sent_a,
    got_a,
    got_b,
    crossed_a,
    below_a,
    above_a,
    crossed_b,
    below_b,
    above_b,
    far,
    turned,
    amp_hbm,
    mz_hbm,
    ky_hbm,
    out_hbm,
    tiles_ref,
    second_ref,
    far_ref,
    turn_ref,
    u_ref,
    o_ref,
    mz_ref,
    ky_ref,
    out_ref,
    amp_ref,
    marks,
    sems,
):
    at = Roots(ablock_ref, pairs_ref, fields, occupied)
    rows = [v.at[:4] for v in (crossed_b, far, below_b, above_b, turned)]
    orbital = [v.at[4:5] for v in (crossed_a, far, below_a, above_a, turned)]
    jobs = [
        (u_ref, arrived(at, 0, at.block(at.c, 0, at.h, 4), got_b.at[16:20], *rows)),
        (o_ref, arrived(at, 1, at.orbital(0), got_a.at[12:13], *orbital)),
    ]
    jobs += [(mz_ref, [(None, mz_hbm)]), (ky_ref, [(None, ky_hbm)]), (amp_ref, [(None, amp_hbm)])]
    u_wait, o_wait, mz_wait, ky_wait, amp_wait = copies(sems, jobs)
    sources = [sent_a.at[13:], got_a.at[13:]] + [v.at[5:] for v in (crossed_a, below_a, above_a, far, turned)]
    mark_waits = copies(sems.at[21:], [(marks.at[i : i + 1], [(None, v)]) for i, v in enumerate(sources)])
    own, core = at.orbital(1), got_b.at[20:]
    crossed, below, above = (v.at[4:] for v in (crossed_b, below_b, above_b))
    not_ = jnp.logical_not
    same_h, same_c, from_below = at.same_h[2], at.same_c[2], at.away[2] == 1
    jobs = [
        (second_ref, arrived(at, 2, own, core, crossed, own, below, above, own)),
        (far_ref, [(same_h & same_c, own), (same_h & not_(same_c), core), (not_(same_h), crossed)]),
        (turn_ref, [(from_below, below), (not_(from_below), above)]),
    ]
    second_waits = copies(sems.at[28:], jobs)
    u_wait.wait()
    o_wait.wait()
    orbital = o_ref[0].astype(F32)
    columns = []
    for a in range(SHARE):
        density = u_ref[a].astype(F32) * orbital
        columns.append(
            jnp.concatenate([density[:, 128 * j : 128 * (j + 1)] for j in range(PAIRS_Y)], axis=0)
        )
    density = jnp.concatenate(columns, axis=1).astype(BF16)
    wait_all(mark_waits)
    total = sum(marks[i].astype(F32) for i in range(len(sources)))
    tiles = jnp.concatenate([total[:, 128 * n : 128 * (n + 1)] for n in range(BAND)], axis=0)
    tiles_ref[...] = tiles.astype(BF16)
    mz_wait.wait()
    zfreq = dot(density, mz_ref[...]).astype(BF16)
    stacked = jnp.concatenate([zfreq[:, 256 * i : 256 * (i + 1)] for i in range(4)], axis=0)
    ky_wait.wait()
    amp_wait.wait()
    jobs = [(out_hbm.at[g, pl.ds(64, 128)], [(None, amp_ref)]) for g in range(GRID)]
    out_waits = copies(sems.at[5:], jobs)
    out_ref[...] = dot(ky_ref[...], stacked).astype(BF16)
    jobs = [(out_hbm.at[g, pl.ds(0, 64)], [(None, out_ref.at[pl.ds(64 * g, 64)])]) for g in range(GRID)]
    wait_all(out_waits + second_waits + copies(sems.at[13:], jobs))


def middle_body(
    y_hbm, weight_ref, turn_hbm, kx_hbm, kxt_hbm, out_hbm, y_ref, turn_ref, kx_ref, kxt_ref, out_ref, sems
):
    jobs = [(y_ref, y_hbm.at[:, pl.ds(0, 64)]), (turn_ref, turn_hbm), (kx_ref, kx_hbm), (kxt_ref, kxt_hbm)]
    y_wait, turn_wait, kx_wait, kxt_wait = copies(sems, [(t, [(None, v)]) for t, v in jobs])
    weights = jnp.concatenate([weight_ref[...], weight_ref[...]], axis=1)
    y_wait.wait()
    turn_wait.wait()
    turn = turn_ref[...]
    yfreq = y_ref[...].reshape(512, 256)
    both = jnp.concatenate([yfreq, dot(yfreq, turn).astype(BF16)], axis=0)
    kx_wait.wait()
    potential = (dot(kx_ref[...], both) * weights).astype(BF16)
    both = jnp.concatenate([potential, dot(potential, turn).astype(BF16)], axis=0)
    kxt_wait.wait()
    out_ref[...] = dot(kxt_ref[...], both).astype(BF16)
    wait_all(copies(sems.at[4:], [(out_hbm, [(None, out_ref)])]))


def backward_body(
    ablock_ref,
    pairs_ref,
    fields,
    occupied,
    second,
    far,
    turned,
    turn_hbm,
    kyt_hbm,
    mzt_hbm,
    h_ref,
    out_ref,
    o_ref,
    turn_ref,
    kyt_ref,
    mzt_ref,
    sems,
):
    at = Roots(ablock_ref, pairs_ref, fields, occupied)
    jobs = [
        (o_ref, arrived(at, 2, second, second, second, far, second, second, turned)),
        (turn_ref, [(None, turn_hbm)]),
        (kyt_ref, [(None, kyt_hbm)]),
        (mzt_ref, [(None, mzt_hbm)]),
    ]
    o_wait, turn_wait, kyt_wait, mzt_wait = copies(sems, jobs)
    freq = h_ref[...]
    turn_wait.wait()
    both = jnp.concatenate([freq, dot(freq, turn_ref[...]).astype(BF16)], axis=0)
    kyt_wait.wait()
    zfreq = dot(kyt_ref[...], both).astype(BF16)
    zfreq = jnp.concatenate([zfreq[:256], zfreq[256:]], axis=1)
    mzt_wait.wait()
    value = dot(zfreq, mzt_ref[...])
    o_wait.wait()
    orbital = o_ref[0].astype(F32)
    for a in range(SHARE):
        rows = [value[8 * j : 8 * (j + 1), 128 * a : 128 * (a + 1)] for j in range(PAIRS_Y)]
        out_ref[a] = (jnp.concatenate(rows, axis=1) * orbital).astype(BF16)


def weight_body(tiles_ref, out_ref):
    tiles = tiles_ref[...]
    shape = (BAND * N, BAND * XL)
    row = lax.broadcasted_iota(jnp.int32, shape, 0)
    lane = lax.broadcasted_iota(jnp.int32, shape, 1)
    spread = dot((row // XL == lane).astype(BF16), tiles)
    spread = jnp.where(row % XL == lane // 16, spread, 0.0).astype(BF16)
    row = lax.broadcasted_iota(jnp.int32, (128, 128), 0)
    lane = lax.broadcasted_iota(jnp.int32, (128, 128), 1)
    spread = dot(spread, (row % 16 == lane % 16).astype(BF16))
    low = lax.broadcasted_iota(jnp.int32, (N, 128), 1) % HALF < 16
    blocks = [spread[N * n : N * (n + 1)] for n in range(BAND)]
    kept = jnp.concatenate([jnp.where(low, blocks[2 * m], blocks[2 * m + 1]) for m in range(XL)], axis=0)
    shape = (N * XL, 128)
    row = lax.broadcasted_iota(jnp.int32, shape, 0)
    lane = lax.broadcasted_iota(jnp.int32, shape, 1)
    freq_x = signed_freq(row % N)
    freq_y = signed_freq(lax.axis_index("grid") * XL + row // N)
    freq_z = lane % HALF
    squared = (freq_x * freq_x + freq_y * freq_y + freq_z * freq_z).astype(F32)
    out_ref[...] = kept / (float(N * N * N) * (squared + 1.0))


def arrival_body(first, second, third, amp_ref, out_ref):
    out_ref[...] = amp_ref[...]


def copy_body(source, target, sems):
    wait_all(copies(sems, [(target, [(None, source)])]))


SMEM, VMEM, HBM = pltpu.SMEM, pltpu.VMEM, pltpu.HBM
PLANE = (XL, N * N)


def call(body, spaces, outs, out_spaces, scratch, args, dtype=BF16, flops=10**8):
    many = len(outs) > 1
    shapes = [jax.ShapeDtypeStruct(o, dtype) for o in outs]
    specs = [pl.BlockSpec(memory_space=m) for m in out_spaces]
    return pl.pallas_call(
        body,
        out_shape=shapes if many else shapes[0],
        in_specs=[pl.BlockSpec(memory_space=m) for m in spaces],
        out_specs=specs if many else specs[0],
        scratch_shapes=scratch,
        compiler_params=pltpu.CompilerParams(vmem_limit_bytes=VMEM_LIMIT),
        cost_estimate=pl.CostEstimate(flops=flops, bytes_accessed=2**20, transcendentals=0),
    )(*args)


def slab_body(last, names, u_ref, *refs):
    pieces = 2 * len(names)
    w_refs, extra = refs[:pieces], refs[pieces:-2]
    out_ref, total = refs[-2:]
    lanes = 2048
    for s in range(N * N // lanes):
        part = pl.ds(s * lanes, lanes)
        right = jnp.concatenate([w[:, part] for w in w_refs], axis=0)
        gram = lax.dot_general(u_ref[:, part], right, (((1,), (1,)), ((), ())), preferred_element_type=F32)
        if s == 0:
            total[...] = gram
        else:
            total[...] += gram
    gram = total[...]
    wide = gram.shape[1]
    row = lax.broadcasted_iota(jnp.int32, gram.shape, 0) % XL
    col = lax.broadcasted_iota(jnp.int32, gram.shape, 1) % XL
    gram = jnp.where(row == col, gram, 0.0)
    gram = jnp.sum(gram.reshape(gram.shape[0] // XL, XL, wide), axis=1)
    y, h, c = position()
    row = lax.broadcasted_iota(jnp.int32, (SHARE * XL, 128), 0) // XL
    lane = lax.broadcasted_iota(jnp.int32, (SHARE * XL, 128), 1) % ABLK
    pick = []
    for dy, dh in names:
        for dc in range(2):
            first = 32 * ((c + dc) % 2) + 8 * ((y - dy + 4) % 4) + 4 * ((h + dh) % 2)
            pick.append((lane == first + row).astype(F32))
    pick = jnp.concatenate(pick, axis=0)
    slab = jnp.dot(gram, pick, precision=lax.Precision.HIGHEST, preferred_element_type=F32)
    if extra:
        slab = slab + extra[0][...]
    if not last:
        out_ref[...] = slab
    else:
        lane = lax.broadcasted_iota(jnp.int32, slab.shape, 1)
        zero = jnp.zeros_like(slab)
        slab = jnp.concatenate(
            [jnp.where(lane < ABLK, slab, zero), jnp.where(lane < ABLK, zero, slab)], axis=0
        )
        high = slab.astype(BF16)
        low = (slab - high.astype(F32)).astype(BF16)
        amp = extra[1][:, pl.ds(64, 128)].reshape(1024, 256)
        out_ref[...] = (dot(amp, high) + dot(amp, low)).astype(BF16)


def slab_call(names, fields, parts, extra=()):
    last = len(extra) > 1
    tall = fields.shape[0]
    wide = sum(p.shape[0] for p in parts)
    out = (1024, 128) if last else (tall // XL, 128)
    args = (fields, *parts, *extra)
    return pl.pallas_call(
        functools.partial(slab_body, last, names),
        out_shape=jax.ShapeDtypeStruct(out, BF16 if last else F32),
        in_specs=[pl.BlockSpec(memory_space=VMEM)] * len(args),
        out_specs=pl.BlockSpec(memory_space=VMEM),
        scratch_shapes=[VMEM((tall, wide), F32)],
        compiler_params=pltpu.CompilerParams(vmem_limit_bytes=24 * 1024 * 1024),
        cost_estimate=pl.CostEstimate(
            flops=2 * tall * wide * N * N, bytes_accessed=2 * tall * N * N, transcendentals=0
        ),
    )(*args)


def band_shift(value, dy, dh, dc):
    pairs = []
    for y in range(4):
        for h in range(2):
            for c in range(2):
                pairs.append((4 * y + 2 * h + c, 4 * ((y + dy) % 4) + 2 * ((h + dh) % 2) + (c + dc) % 2))
    return lax.ppermute(value, "band", pairs)


def per_device(virtual_field, occupied_field, amplitudes, ablock, pairs, kept_cells):
    far_memory = lambda v: pltpu.with_memory_space_constraint(v, HBM)
    const = {n: far_memory(jnp.asarray(v)) for n, v in tables().items()}
    roots = (ablock, pairs, far_memory(virtual_field), far_memory(occupied_field))
    root_spaces = [SMEM, SMEM, pl.ANY, pl.ANY]

    with jax.named_scope("block_scatter"):
        sems = lambda n: [pltpu.SemaphoreType.DMA((n,))]
        rows = lambda n: (n,) + PLANE
        held = lambda n: VMEM(rows(n), BF16)
        hop = lambda body, spaces, out, scratch, *args, flops=10**8: call(
            body, spaces, out, [pl.ANY] * len(out), scratch, args, flops=flops
        )
        any_ = [pl.ANY]
        sent_a = hop(
            core_a_body,
            root_spaces[:2] + any_ * 3,
            [rows(14)],
            [held(1), VMEM(kept_cells.shape, jnp.int32)] + sems(10),
            *roots[:2],
            far_memory(kept_cells),
            *roots[2:],
        )
        got_a = band_shift(sent_a, 0, 0, 1)
        sent_b, amp = call(
            core_b_body,
            root_spaces + any_,
            [rows(21), (128, 256)],
            any_ + [VMEM],
            [VMEM((128, 256), BF16)] + sems(7),
            roots + (far_memory(amplitudes),),
            flops=5 * 10**9,
        )
        up, down, across = hop(
            first_a_body,
            root_spaces + any_ * 2,
            [rows(6)] * 3,
            [held(2)] + sems(17),
            *roots,
            sent_a,
            got_a,
        )
        up, down, across, sent_b = lax.optimization_barrier((up, down, across, sent_b))
        below_a = band_shift(up, 1, 0, 0)
        above_a = band_shift(down, 3, 0, 0)
        crossed_a = band_shift(across, 0, 1, 0)
        got_b = band_shift(sent_b, 0, 0, 1)
        up, down, across = hop(
            first_b_body, root_spaces + any_, [rows(5)] * 3, sems(6), *roots, got_b
        )
        below_b = band_shift(up, 1, 0, 0)
        above_b = band_shift(down, 3, 0, 0)
        crossed_b = band_shift(across, 0, 1, 0)
        crossed_a, below_a, above_a, _ = lax.optimization_barrier((crossed_a, below_a, above_a, (up, down, across)))
        far, turn = hop(
            second_a_body,
            root_spaces + any_ * 6,
            [rows(6)] * 2,
            [held(5)] + sems(15),
            *roots,
            sent_a,
            got_a,
            got_b,
            crossed_a,
            below_a,
            above_a,
            flops=10**10,
        )
        far_a = band_shift(far, 2, 0, 0)
        turned_a = band_shift(turn, 0, 1, 0)

        behind = (crossed_b, below_b, above_b, amp)
        amp = call(arrival_body, any_ * 3 + [VMEM], [(128, 256)], [VMEM], [], behind, flops=10**10)
        far_a, turned_a, amp = lax.optimization_barrier((far_a, turned_a, amp))

    with jax.named_scope("transform"):
        big = VMEM((512, 1024), BF16)
        from_all = (GRID, 64 + 128, 256)
        freq, tiles, second, far, turn = call(
            forward_body,
            root_spaces + any_ * 14,
            [from_all, (BAND * XL, 128)] + [rows(1)] * 3,
            any_ + [VMEM] * 4,
            [held(SHARE), held(1), big, big, VMEM((512, 256), BF16), VMEM((128, 256), BF16), held(7)] + sems(31),
            roots
            + (sent_a, got_a, got_b, crossed_a, below_a, above_a, crossed_b, below_b, above_b, far_a, turned_a)
            + (amp, const["mz"], const["ky"]),
            flops=2 * 10**10,
        )
        freq = lax.all_to_all(freq, "grid", 0, 0, tiled=True)
        amp = freq
        far_b = band_shift(far, 2, 0, 0)
        turned_b = band_shift(turn, 0, 1, 0)
        weights = call(
            weight_body,
            [VMEM],
            [(N * XL, 128)],
            [VMEM],
            [],
            (tiles,),
            F32,
        )
        freq = call(
            middle_body,
            any_ + [VMEM] + any_ * 3,
            [(512, 256)],
            any_,
            [VMEM((GRID, 64, 256), BF16), VMEM((256, 256), BF16), big, big, VMEM((512, 256), BF16)] + sems(5),
            (freq, weights, const["turn"], const["kx"], const["kxt"]),
            flops=10**10,
        )
        freq = lax.all_to_all(freq, "grid", 0, 0, tiled=True)
        potential = call(
            backward_body,
            root_spaces + any_ * 6 + [VMEM],
            [(SHARE,) + PLANE],
            [VMEM],
            [held(1), VMEM((256, 256), BF16), big, VMEM((512, 512), BF16)] + sems(4),
            roots
            + (second, far_b, turned_b)
            + (const["turn"], const["kyt"], const["mzt"], freq),
        )

    with jax.named_scope("block_gather"):
        early, late = ((0, 0), (2, 0), (1, 0), (3, 0), (0, 1)), ((2, 1), (1, 1), (3, 1))
        shape = (virtual_field.shape[0] * XL, N * N)
        potential, fields = lax.optimization_barrier(
            (potential.reshape(SHARE * XL, N * N), virtual_field.reshape(shape))
        )
        fields = call(copy_body, [pl.ANY], [shape], [pl.ANY], sems(1), (far_memory(fields),))
        part = {(0, 0): potential}
        for k in (2, 1, 3):
            part[k, 0] = band_shift(potential, k, 0, 0)
        part[0, 1] = band_shift(potential, 0, 1, 0)

        def contract(names, *extra):
            pieces = [w for name in names for w in (part[name], band_shift(part[name], 0, 0, 1))]
            return slab_call(names, fields, pieces, extra)

        part[2, 0], part[0, 1], fields = lax.optimization_barrier((part[2, 0], part[0, 1], fields))
        part[2, 1] = band_shift(part[2, 0], 0, 1, 0)
        for k in (1, 3):
            part[k, 1] = band_shift(part[0, 1], k, 0, 0)
        slab = contract(early)
        *got, slab = lax.optimization_barrier([part[name] for name in late] + [slab])
        part.update(zip(late, got))
        terms = contract(late, slab, amp)

    with jax.named_scope("ladder"):
        terms = lax.all_to_all(
            terms.reshape(GRID * BAND, XL, 128), ("grid", "band"), 0, 0, tiled=True
        )
        ladder = jnp.sum(terms.astype(F32), axis=0)
        return ladder.reshape(1, 16, ABLK)


def solution(mesh):
    in_specs = (
        P("band", "grid", None),
        P("band", "grid", None),
        P(None, "band", "grid"),
        P(),
        P(),
        P(("grid", "band"), None),
    )
    out_specs = P(None, ("grid", "band"), None)
    return jax.shard_map(
        per_device, mesh=mesh, in_specs=in_specs, out_specs=out_specs, check_vma=False
    )
```

```python
import functools
import math

import jax
import jax.numpy as jnp
import numpy as np
from jax import lax
from jax.experimental import pallas as pl
from jax.experimental.pallas import tpu as pltpu
from jax.sharding import PartitionSpec as P


N = 64
HALF = 32
ABLK = 64
GRID = 8
BAND = 16
XL = 8
SHARE = ABLK // BAND
PAIRS_Y = 32
F32 = jnp.float32
BF16 = jnp.bfloat16
VMEM_LIMIT = 16 * 1024 * 1024


@functools.cache
def tables():
    index = np.arange(N)
    phase = (index[:, None] * index[None, :]) % N
    angle = np.float32(2.0 * math.pi / N) * phase.astype(np.float32)
    cosine = np.cos(angle).astype(np.float32)
    sine = np.sin(angle).astype(np.float32)
    eye_x = np.eye(XL, dtype=np.float32)
    z_plain = np.concatenate([cosine[:HALF].T, -sine[:HALF].T], axis=1)
    z_turned = np.concatenate([z_plain[:, HALF:], -z_plain[:, :HALF]], axis=1)
    mz = np.zeros((SHARE, 2, N, 2, 2, SHARE, N), np.float32)
    for a in range(SHARE):
        for p in range(2):
            mz[a, p, :, 0, p, a, :] = z_plain
            mz[a, p, :, 1, p, a, :] = z_turned
    mzt = np.zeros((2, SHARE, N, SHARE, 2, N), np.float32)
    for a in range(SHARE):
        for p in range(2):
            mzt[p, a, :, a, p, :] = z_plain.T
    by_parity = np.stack([cosine, sine], axis=1).reshape(N, 2, PAIRS_Y, 2)
    ky = np.einsum("ktjp,xw->kxtpjw", by_parity, eye_x)
    signed = np.stack([cosine, -sine], axis=1).reshape(N, 2, PAIRS_Y, 2)
    kyt = np.einsum("ktjp,xw->pjxtkw", signed, eye_x)
    by_slab = np.stack([cosine, sine], axis=1).reshape(N, 2, GRID, XL)
    kx = np.einsum("ktgx,lm->lktgmx", by_slab, eye_x)
    signed_slab = np.stack([cosine, -sine], axis=1).reshape(N, 2, GRID, XL)
    kxt = np.einsum("ktgx,lm->gmxtlk", signed_slab, eye_x)
    turn = np.zeros((SHARE, 2, HALF, SHARE, 2, HALF), np.float32)
    for a in range(SHARE):
        turn[a, 1, :, a, 0, :] = np.eye(HALF)
        turn[a, 0, :, a, 1, :] = -np.eye(HALF)
    shapes = {
        "mz": (mz, 512, 1024),
        "mzt": (mzt, 512, 512),
        "ky": (ky, 512, 1024),
        "kyt": (kyt, 512, 1024),
        "kx": (kx, 512, 1024),
        "kxt": (kxt, 512, 1024),
        "turn": (turn, 256, 256),
    }
    return {n: v.reshape(r, c).astype(BF16) for n, (v, r, c) in shapes.items()}


def dot(a, b):
    return jnp.dot(a, b, preferred_element_type=F32)


def signed_freq(index):
    return (index + N // 2) % N - N // 2


def position():
    band = lax.axis_index("band")
    return band // 4, (band // 2) % 2, band % 2


def root_of(device):
    return device // 4, (device // 2) % 2, device % 2


def copies(sems, jobs):
    waits = []
    for slot, (target, choices) in enumerate(jobs):
        for condition, source in choices:
            move = pltpu.make_async_copy(source, target, sems.at[slot])
            if condition is None:
                move.start()
            else:
                pl.when(condition)(move.start)
        waits.append(pltpu.make_async_copy(target, target, sems.at[slot]))
    return waits


def gather(sems, jobs, start=None):
    finish = start() if start else None
    moves = copies(sems, jobs)
    if finish:
        moves += finish()
    wait_all(moves)


def wait_all(waits):
    for move in waits:
        move.wait()


class Roots:
    def __init__(self, ablock_ref, pairs_ref, fields, occupied):
        self.y, self.h, self.c = position()
        self.fields, self.occupied = fields, occupied
        start = ablock_ref[0] * ABLK
        self.first = start % fields.shape[0]
        devices = [start // fields.shape[0]]
        self.local = []
        for k in range(2):
            index = pairs_ref[0, k]
            devices.append(index // occupied.shape[0])
            self.local.append(index % occupied.shape[0])
        roots = [root_of(d) for d in devices]
        self.away = [(self.y - y + 4) % 4 for y, _, _ in roots]
        self.same_h = [h == self.h for _, h, _ in roots]
        self.same_c = [c == self.c for _, _, c in roots]

    def block(self, core, dy, h, count):
        start = self.first + 32 * core + 8 * ((self.y + dy) % 4) + 4 * h
        return self.fields.at[pl.ds(start, count)]

    def orbital(self, k):
        return self.occupied.at[pl.ds(self.local[k], 1)]


def core_a_body(ablock_ref, pairs_ref, kept_hbm, fields, occupied, out, marks, kept_ref, sems):
    at = Roots(ablock_ref, pairs_ref, fields, occupied)
    other, there = 1 - at.c, 1 - at.h
    sources = [at.block(other, dy, there, 4) for dy in (1, 3, 2)]
    jobs = [(plane(out, pl.ds(4 * i, 4)), [(None, v)]) for i, v in enumerate(sources)]
    jobs.append((plane(out, pl.ds(12, 1)), [(None, at.orbital(0))]))

    def start():
        (wait,) = copies(sems.at[9:], [(kept_ref, [(None, kept_hbm)])])
        return functools.partial(finish, wait)

    def finish(wait):
        wait.wait()
        kept = kept_ref[...]
        in_x = (lax.broadcasted_iota(jnp.int32, (N, kept.shape[1]), 0) == kept // 16).astype(BF16)
        in_c = lax.broadcasted_iota(jnp.int32, (128, kept.shape[1]), 0) % 16 == kept % 16
        mask = lax.dot_general(
            in_x, in_c.astype(BF16), (((1,), (1,)), ((), ())), preferred_element_type=F32
        )
        row = lax.broadcasted_iota(jnp.int32, mask.shape, 0)
        lane = lax.broadcasted_iota(jnp.int32, mask.shape, 1)
        mask = jnp.where(row % XL == lane // 16, mask, 0.0)
        marks[0] = jnp.sum(mask.reshape(XL, XL, 128), axis=1).astype(BF16)
        move = pltpu.make_async_copy(marks, marks_of(out, pl.ds(0, 1)), sems.at[8])
        move.start()
        return [move]

    gather(sems, jobs, start)


def core_b_body(ablock_ref, pairs_ref, fields, occupied, amp_hbm, out, amp_out, amp_ref, sems):
    at = Roots(ablock_ref, pairs_ref, fields, occupied)
    other, here, there = 1 - at.c, at.h, 1 - at.h
    sources = [at.block(other, dy, h, 4) for dy, h in ((1, here), (3, here), (0, there), (2, here), (0, here))]
    jobs = [(out.at[4 * i : 4 * i + 4], [(None, v)]) for i, v in enumerate(sources)]
    jobs.append((out.at[20:], [(None, at.orbital(1))]))
    moves = copies(sems, jobs)
    (amp_wait,) = copies(sems.at[6:], [(amp_ref, [(None, amp_hbm.at[0])])])
    amp_wait.wait()
    row = lax.broadcasted_iota(jnp.int32, (128, 256), 0)
    col = lax.broadcasted_iota(jnp.int32, (128, 256), 1)
    over_c = (((1,), (1,)), ((), ()))
    parity = [
        lax.dot_general((col == 2 * row + p).astype(BF16), amp_ref[...], over_c, preferred_element_type=F32)
        for p in range(2)
    ]
    amp_out[...] = jnp.concatenate(parity, axis=1).astype(BF16)
    wait_all(moves)


def own_marks(at, target, sent_a, got_a):
    return [
        (marks_of(target, pl.ds(at.c, 1)), [(None, marks_of(sent_a, pl.ds(0, 1)))]),
        (marks_of(target, pl.ds(1 - at.c, 1)), [(None, marks_of(got_a, pl.ds(0, 1)))]),
    ]


def first_a_body(ablock_ref, pairs_ref, fields, occupied, sent_a, got_a, up, down, across, sems):
    at = Roots(ablock_ref, pairs_ref, fields, occupied)
    mine, theirs = at.same_c[0], jnp.logical_not(at.same_c[0])
    jobs = []
    for i, (target, dy) in enumerate(((up, 1), (down, 3), (across, 2))):
        own = at.block(at.c, dy, 1 - at.h, 4)
        jobs.append((plane(target, pl.ds(0, 4)), [(mine, own), (theirs, plane(got_a, pl.ds(4 * i, 4)))]))
    mine, theirs = at.same_c[1], jnp.logical_not(at.same_c[1])
    for target in (up, down, across):
        partner = plane(got_a, pl.ds(12, 1))
        jobs.append((plane(target, pl.ds(4, 1)), [(mine, at.orbital(0)), (theirs, partner)]))
        jobs += own_marks(at, target, sent_a, got_a)
    gather(sems, jobs)


def first_b_body(ablock_ref, pairs_ref, fields, occupied, got_b, up, down, across, sems):
    at = Roots(ablock_ref, pairs_ref, fields, occupied)
    mine, theirs = at.same_c[0], jnp.logical_not(at.same_c[0])
    jobs = []
    for i, (target, dy, h) in enumerate(((up, 1, at.h), (down, 3, at.h), (across, 0, 1 - at.h))):
        own = at.block(at.c, dy, h, 4)
        jobs.append((target.at[:4], [(mine, own), (theirs, got_b.at[4 * i : 4 * i + 4])]))
    mine, theirs = at.same_c[2], jnp.logical_not(at.same_c[2])
    for target in (up, down, across):
        jobs.append((target.at[4:], [(mine, at.orbital(1)), (theirs, got_b.at[20:])]))
    gather(sems, jobs)


def second_a_body(
    ablock_ref, pairs_ref, fields, occupied, sent_a, got_a, got_b, crossed, below, above, far, turn, sems
):
    at = Roots(ablock_ref, pairs_ref, fields, occupied)
    not_ = jnp.logical_not
    jobs = []
    own_rows = (at.block(at.c, 2, at.h, 4), got_b.at[12:16], pl.ds(0, 4))
    own_orbital = (at.orbital(0), plane(got_a, pl.ds(12, 1)), pl.ds(4, 1))
    for k, (own, core, part) in enumerate((own_rows, own_orbital)):
        same_h, same_c = at.same_h[k], at.same_c[k]
        other = plane(crossed, part)
        choices = [(same_h & same_c, own), (same_h & not_(same_c), core), (not_(same_h), other)]
        jobs.append((plane(far, part), choices))
        from_below = at.away[k] == 1
        choices = [(from_below, plane(below, part)), (not_(from_below), plane(above, part))]
        jobs.append((plane(turn, part), choices))
    jobs += own_marks(at, far, sent_a, got_a)
    for target, first, source in ((far, 2, crossed), (turn, 0, below), (turn, 2, above)):
        jobs.append((marks_of(target, pl.ds(first, 2)), [(None, marks_of(source, pl.ds(0, 2)))]))
    gather(sems, jobs)


def arrived(at, k, own, core, cross, far, below, above, turned):
    not_ = jnp.logical_not
    away, same_h, same_c = at.away[k], at.same_h[k], at.same_c[k]
    return [
        ((away == 0) & same_h & same_c, own),
        ((away == 0) & same_h & not_(same_c), core),
        ((away == 0) & not_(same_h), cross),
        (away == 2, far),
        ((away == 1) & same_h, below),
        ((away == 3) & same_h, above),
        ((away % 2 == 1) & not_(same_h), turned),
    ]


def forward_body(
    ablock_ref,
    pairs_ref,
    fields,
    occupied,
    sent_a,
    got_a,
    got_b,
    crossed_a,
    below_a,
    above_a,
    crossed_b,
    below_b,
    above_b,
    far,
    turned,
    amp_hbm,
    mz_hbm,
    ky_hbm,
    out_hbm,
    tiles_ref,
    second_ref,
    far_ref,
    turn_ref,
    u_ref,
    o_ref,
    mz_ref,
    ky_ref,
    out_ref,
    amp_ref,
    sems,
):
    at = Roots(ablock_ref, pairs_ref, fields, occupied)
    rows = [crossed_b.at[:4], plane(far, pl.ds(0, 4)), below_b.at[:4], above_b.at[:4], plane(turned, pl.ds(0, 4))]
    orbital = [plane(v, pl.ds(4, 1)) for v in (crossed_a, far, below_a, above_a, turned)]
    jobs = [
        (u_ref, arrived(at, 0, at.block(at.c, 0, at.h, 4), got_b.at[16:20], *rows)),
        (o_ref, arrived(at, 1, at.orbital(0), plane(got_a, pl.ds(12, 1)), *orbital)),
    ]
    jobs += [(mz_ref, [(None, mz_hbm)]), (ky_ref, [(None, ky_hbm)]), (amp_ref, [(None, amp_hbm)])]
    u_wait, o_wait, mz_wait, ky_wait, amp_wait = copies(sems, jobs)
    device = lambda dy, dh, c: 4 * ((at.y + dy) % 4) + 2 * ((at.h + dh) % 2) + c
    jobs = [
        (tiles_ref.at[pl.ds(device(0, 0, at.c), 1)], [(None, marks_of(sent_a, pl.ds(0, 1)))]),
        (tiles_ref.at[pl.ds(device(0, 0, 1 - at.c), 1)], [(None, marks_of(got_a, pl.ds(0, 1)))]),
    ]
    pairs = [(0, 1, crossed_a, 0), (3, 0, below_a, 0), (1, 0, above_a, 0), (2, 0, far, 0), (2, 1, far, 2)]
    for dy, dh, source, first in pairs + [(3, 1, turned, 0), (1, 1, turned, 2)]:
        place = tiles_ref.at[pl.ds(device(dy, dh, 0), 2)]
        jobs.append((place, [(None, marks_of(source, pl.ds(first, 2)))]))
    mark_waits = copies(sems.at[21:], jobs)
    own, core = at.orbital(1), got_b.at[20:]
    crossed, below, above = (v.at[4:] for v in (crossed_b, below_b, above_b))
    not_ = jnp.logical_not
    same_h, same_c, from_below = at.same_h[2], at.same_c[2], at.away[2] == 1
    jobs = [
        (second_ref, arrived(at, 2, own, core, crossed, own, below, above, own)),
        (far_ref, [(same_h & same_c, own), (same_h & not_(same_c), core), (not_(same_h), crossed)]),
        (turn_ref, [(from_below, below), (not_(from_below), above)]),
    ]
    second_waits = copies(sems.at[30:], jobs)
    u_wait.wait()
    o_wait.wait()
    orbital = o_ref[0].astype(F32)
    columns = []
    for a in range(SHARE):
        density = u_ref[a].astype(F32) * orbital
        columns.append(
            jnp.concatenate([density[:, 128 * j : 128 * (j + 1)] for j in range(PAIRS_Y)], axis=0)
        )
    density = jnp.concatenate(columns, axis=1).astype(BF16)
    mz_wait.wait()
    zfreq = dot(density, mz_ref[...]).astype(BF16)
    stacked = jnp.concatenate([zfreq[:, 256 * i : 256 * (i + 1)] for i in range(4)], axis=0)
    ky_wait.wait()
    amp_wait.wait()
    jobs = [(out_hbm.at[g, pl.ds(64, 128)], [(None, amp_ref)]) for g in range(GRID)]
    out_waits = copies(sems.at[5:], jobs)
    out_ref[...] = dot(ky_ref[...], stacked).astype(BF16)
    jobs = [(out_hbm.at[g, pl.ds(0, 64)], [(None, out_ref.at[pl.ds(64 * g, 64)])]) for g in range(GRID)]
    wait_all(out_waits + mark_waits + second_waits + copies(sems.at[13:], jobs))


def middle_body(
    y_hbm, weight_ref, turn_hbm, kx_hbm, kxt_hbm, out_hbm, y_ref, turn_ref, kx_ref, kxt_ref, out_ref, sems
):
    jobs = [(y_ref, y_hbm.at[:, pl.ds(0, 64)]), (turn_ref, turn_hbm), (kx_ref, kx_hbm), (kxt_ref, kxt_hbm)]
    y_wait, turn_wait, kx_wait, kxt_wait = copies(sems, [(t, [(None, v)]) for t, v in jobs])
    weights = jnp.concatenate([weight_ref[...], weight_ref[...]], axis=1)
    y_wait.wait()
    turn_wait.wait()
    turn = turn_ref[...]
    yfreq = y_ref[...].reshape(512, 256)
    both = jnp.concatenate([yfreq, dot(yfreq, turn).astype(BF16)], axis=0)
    kx_wait.wait()
    potential = (dot(kx_ref[...], both) * weights).astype(BF16)
    both = jnp.concatenate([potential, dot(potential, turn).astype(BF16)], axis=0)
    kxt_wait.wait()
    out_ref[...] = dot(kxt_ref[...], both).astype(BF16)
    wait_all(copies(sems.at[4:], [(out_hbm, [(None, out_ref)])]))


def backward_body(
    ablock_ref,
    pairs_ref,
    fields,
    occupied,
    second,
    far,
    turned,
    turn_hbm,
    kyt_hbm,
    mzt_hbm,
    h_ref,
    out_ref,
    o_ref,
    turn_ref,
    kyt_ref,
    mzt_ref,
    sems,
):
    at = Roots(ablock_ref, pairs_ref, fields, occupied)
    jobs = [
        (o_ref, arrived(at, 2, second, second, second, far, second, second, turned)),
        (turn_ref, [(None, turn_hbm)]),
        (kyt_ref, [(None, kyt_hbm)]),
        (mzt_ref, [(None, mzt_hbm)]),
    ]
    o_wait, turn_wait, kyt_wait, mzt_wait = copies(sems, jobs)
    freq = h_ref[...]
    turn_wait.wait()
    both = jnp.concatenate([freq, dot(freq, turn_ref[...]).astype(BF16)], axis=0)
    kyt_wait.wait()
    zfreq = dot(kyt_ref[...], both).astype(BF16)
    zfreq = jnp.concatenate([zfreq[:256], zfreq[256:]], axis=1)
    mzt_wait.wait()
    value = dot(zfreq, mzt_ref[...])
    o_wait.wait()
    orbital = o_ref[0].astype(F32)
    for a in range(SHARE):
        rows = [value[8 * j : 8 * (j + 1), 128 * a : 128 * (a + 1)] for j in range(PAIRS_Y)]
        out_ref[a] = (jnp.concatenate(rows, axis=1) * orbital).astype(BF16)


def weight_body(tiles_ref, out_ref):
    tiles = tiles_ref[...].astype(F32).reshape(BAND * XL, 128).astype(BF16)
    shape = (BAND * N, BAND * XL)
    row = lax.broadcasted_iota(jnp.int32, shape, 0)
    lane = lax.broadcasted_iota(jnp.int32, shape, 1)
    spread = dot((row // XL == lane).astype(BF16), tiles)
    spread = jnp.where(row % XL == lane // 16, spread, 0.0).astype(BF16)
    row = lax.broadcasted_iota(jnp.int32, (128, 128), 0)
    lane = lax.broadcasted_iota(jnp.int32, (128, 128), 1)
    spread = dot(spread, (row % 16 == lane % 16).astype(BF16))
    low = lax.broadcasted_iota(jnp.int32, (N, 128), 1) % HALF < 16
    blocks = [spread[N * n : N * (n + 1)] for n in range(BAND)]
    kept = jnp.concatenate([jnp.where(low, blocks[2 * m], blocks[2 * m + 1]) for m in range(XL)], axis=0)
    shape = (N * XL, 128)
    row = lax.broadcasted_iota(jnp.int32, shape, 0)
    lane = lax.broadcasted_iota(jnp.int32, shape, 1)
    freq_x = signed_freq(row % N)
    freq_y = signed_freq(lax.axis_index("grid") * XL + row // N)
    freq_z = lane % HALF
    squared = (freq_x * freq_x + freq_y * freq_y + freq_z * freq_z).astype(F32)
    out_ref[...] = kept / (float(N * N * N) * (squared + 1.0))


def arrival_body(first, second, third, amp_ref, out_ref):
    out_ref[...] = amp_ref[...]


def copy_body(source, target, sems):
    wait_all(copies(sems, [(target, [(None, source)])]))


SMEM, VMEM, HBM = pltpu.SMEM, pltpu.VMEM, pltpu.HBM
PLANE = (XL, N * N)
LONG = (XL, N * N + 128)
GRIDPOINTS, MARKS = pl.ds(0, N * N), pl.ds(N * N, 128)


def plane(ref, *index):
    return ref.at[*index, :, GRIDPOINTS]


def marks_of(ref, *index):
    return ref.at[*index, :, MARKS]


def call(body, spaces, outs, out_spaces, scratch, args, dtype=BF16, flops=10**8):
    many = len(outs) > 1
    shapes = [jax.ShapeDtypeStruct(o, dtype) for o in outs]
    specs = [pl.BlockSpec(memory_space=m) for m in out_spaces]
    return pl.pallas_call(
        body,
        out_shape=shapes if many else shapes[0],
        in_specs=[pl.BlockSpec(memory_space=m) for m in spaces],
        out_specs=specs if many else specs[0],
        scratch_shapes=scratch,
        compiler_params=pltpu.CompilerParams(vmem_limit_bytes=VMEM_LIMIT),
        cost_estimate=pl.CostEstimate(flops=flops, bytes_accessed=2**20, transcendentals=0),
    )(*args)


def slab_body(last, names, u_ref, *refs):
    pieces = 2 * len(names)
    w_refs, extra = refs[:pieces], refs[pieces:-2]
    out_ref, total = refs[-2:]
    lanes = 2048
    for s in range(N * N // lanes):
        part = pl.ds(s * lanes, lanes)
        right = jnp.concatenate([w[:, part] for w in w_refs], axis=0)
        gram = lax.dot_general(u_ref[:, part], right, (((1,), (1,)), ((), ())), preferred_element_type=F32)
        if s == 0:
            total[...] = gram
        else:
            total[...] += gram
    gram = total[...]
    wide = gram.shape[1]
    row = lax.broadcasted_iota(jnp.int32, gram.shape, 0) % XL
    col = lax.broadcasted_iota(jnp.int32, gram.shape, 1) % XL
    gram = jnp.where(row == col, gram, 0.0)
    gram = jnp.sum(gram.reshape(gram.shape[0] // XL, XL, wide), axis=1)
    y, h, c = position()
    row = lax.broadcasted_iota(jnp.int32, (SHARE * XL, 128), 0) // XL
    lane = lax.broadcasted_iota(jnp.int32, (SHARE * XL, 128), 1) % ABLK
    pick = []
    for dy, dh in names:
        for dc in range(2):
            first = 32 * ((c + dc) % 2) + 8 * ((y - dy + 4) % 4) + 4 * ((h + dh) % 2)
            pick.append((lane == first + row).astype(F32))
    pick = jnp.concatenate(pick, axis=0)
    slab = jnp.dot(gram, pick, precision=lax.Precision.HIGHEST, preferred_element_type=F32)
    if extra:
        slab = slab + extra[0][...]
    if not last:
        out_ref[...] = slab
    else:
        lane = lax.broadcasted_iota(jnp.int32, slab.shape, 1)
        zero = jnp.zeros_like(slab)
        slab = jnp.concatenate(
            [jnp.where(lane < ABLK, slab, zero), jnp.where(lane < ABLK, zero, slab)], axis=0
        )
        high = slab.astype(BF16)
        low = (slab - high.astype(F32)).astype(BF16)
        amp = extra[1][:, pl.ds(64, 128)].reshape(1024, 256)
        out_ref[...] = (dot(amp, high) + dot(amp, low)).astype(BF16)


def slab_call(names, fields, parts, extra=()):
    last = len(extra) > 1
    tall = fields.shape[0]
    wide = sum(p.shape[0] for p in parts)
    out = (1024, 128) if last else (tall // XL, 128)
    args = (fields, *parts, *extra)
    return pl.pallas_call(
        functools.partial(slab_body, last, names),
        out_shape=jax.ShapeDtypeStruct(out, BF16 if last else F32),
        in_specs=[pl.BlockSpec(memory_space=VMEM)] * len(args),
        out_specs=pl.BlockSpec(memory_space=VMEM),
        scratch_shapes=[VMEM((tall, wide), F32)],
        compiler_params=pltpu.CompilerParams(vmem_limit_bytes=24 * 1024 * 1024),
        cost_estimate=pl.CostEstimate(
            flops=2 * tall * wide * N * N, bytes_accessed=2 * tall * N * N, transcendentals=0
        ),
    )(*args)


def band_shift(value, dy, dh, dc):
    pairs = []
    for y in range(4):
        for h in range(2):
            for c in range(2):
                pairs.append((4 * y + 2 * h + c, 4 * ((y + dy) % 4) + 2 * ((h + dh) % 2) + (c + dc) % 2))
    return lax.ppermute(value, "band", pairs)


def per_device(virtual_field, occupied_field, amplitudes, ablock, pairs, kept_cells):
    far_memory = lambda v: pltpu.with_memory_space_constraint(v, HBM)
    const = {n: far_memory(jnp.asarray(v)) for n, v in tables().items()}
    roots = (ablock, pairs, far_memory(virtual_field), far_memory(occupied_field))
    root_spaces = [SMEM, SMEM, pl.ANY, pl.ANY]

    with jax.named_scope("block_scatter"):
        sems = lambda n: [pltpu.SemaphoreType.DMA((n,))]
        rows = lambda n: (n,) + PLANE
        held = lambda n: VMEM(rows(n), BF16)
        hop = lambda body, spaces, out, scratch, *args, flops=10**8: call(
            body, spaces, out, [pl.ANY] * len(out), scratch, args, flops=flops
        )
        any_ = [pl.ANY]
        sent_a = hop(
            core_a_body,
            root_spaces[:2] + any_ * 3,
            [(13,) + LONG],
            [VMEM((1, XL, 128), BF16), VMEM(kept_cells.shape, jnp.int32)] + sems(10),
            *roots[:2],
            far_memory(kept_cells),
            *roots[2:],
        )
        got_a = band_shift(sent_a, 0, 0, 1)
        sent_b, amp = call(
            core_b_body,
            root_spaces + any_,
            [rows(21), (128, 256)],
            any_ + [VMEM],
            [VMEM((128, 256), BF16)] + sems(7),
            roots + (far_memory(amplitudes),),
            flops=5 * 10**9,
        )
        up, down, across = hop(
            first_a_body,
            root_spaces + any_ * 2,
            [(5,) + LONG] * 3,
            sems(12),
            *roots,
            sent_a,
            got_a,
        )
        up, down, across, sent_b = lax.optimization_barrier((up, down, across, sent_b))
        below_a = band_shift(up, 1, 0, 0)
        above_a = band_shift(down, 3, 0, 0)
        crossed_a = band_shift(across, 0, 1, 0)
        got_b = band_shift(sent_b, 0, 0, 1)
        up, down, across = hop(
            first_b_body, root_spaces + any_, [rows(5)] * 3, sems(6), *roots, got_b
        )
        below_b = band_shift(up, 1, 0, 0)
        above_b = band_shift(down, 3, 0, 0)
        crossed_b = band_shift(across, 0, 1, 0)
        crossed_a, below_a, above_a, _ = lax.optimization_barrier((crossed_a, below_a, above_a, (up, down, across)))
        far, turn = hop(
            second_a_body,
            root_spaces + any_ * 6,
            [(5,) + LONG] * 2,
            sems(9),
            *roots,
            sent_a,
            got_a,
            got_b,
            crossed_a,
            below_a,
            above_a,
            flops=10**10,
        )
        far_a = band_shift(far, 2, 0, 0)
        turned_a = band_shift(turn, 0, 1, 0)

        behind = (crossed_b, below_b, above_b, amp)
        amp = call(arrival_body, any_ * 3 + [VMEM], [(128, 256)], [VMEM], [], behind, flops=10**10)
        far_a, turned_a, amp = lax.optimization_barrier((far_a, turned_a, amp))

    with jax.named_scope("transform"):
        big = VMEM((512, 1024), BF16)
        from_all = (GRID, 64 + 128, 256)
        freq, tiles, second, far, turn = call(
            forward_body,
            root_spaces + any_ * 14,
            [from_all, (BAND, XL, 128)] + [rows(1)] * 3,
            any_ + [VMEM] * 4,
            [held(SHARE), held(1), big, big, VMEM((512, 256), BF16), VMEM((128, 256), BF16)] + sems(33),
            roots
            + (sent_a, got_a, got_b, crossed_a, below_a, above_a, crossed_b, below_b, above_b, far_a, turned_a)
            + (amp, const["mz"], const["ky"]),
            flops=2 * 10**10,
        )
        freq = lax.all_to_all(freq, "grid", 0, 0, tiled=True)
        amp = freq
        far_b = band_shift(far, 2, 0, 0)
        turned_b = band_shift(turn, 0, 1, 0)
        weights = call(
            weight_body,
            [VMEM],
            [(N * XL, 128)],
            [VMEM],
            [],
            (tiles,),
            F32,
        )
        freq = call(
            middle_body,
            any_ + [VMEM] + any_ * 3,
            [(512, 256)],
            any_,
            [VMEM((GRID, 64, 256), BF16), VMEM((256, 256), BF16), big, big, VMEM((512, 256), BF16)] + sems(5),
            (freq, weights, const["turn"], const["kx"], const["kxt"]),
            flops=10**10,
        )
        freq = lax.all_to_all(freq, "grid", 0, 0, tiled=True)
        potential = call(
            backward_body,
            root_spaces + any_ * 6 + [VMEM],
            [(SHARE,) + PLANE],
            [VMEM],
            [held(1), VMEM((256, 256), BF16), big, VMEM((512, 512), BF16)] + sems(4),
            roots
            + (second, far_b, turned_b)
            + (const["turn"], const["kyt"], const["mzt"], freq),
        )

    with jax.named_scope("block_gather"):
        early, late = ((0, 0), (2, 0), (1, 0), (3, 0), (0, 1)), ((2, 1), (1, 1), (3, 1))
        shape = (virtual_field.shape[0] * XL, N * N)
        potential, fields = lax.optimization_barrier(
            (potential.reshape(SHARE * XL, N * N), virtual_field.reshape(shape))
        )
        fields = call(copy_body, [pl.ANY], [shape], [pl.ANY], sems(1), (far_memory(fields),))
        part = {(0, 0): potential}
        for k in (2, 1, 3):
            part[k, 0] = band_shift(potential, k, 0, 0)
        part[0, 1] = band_shift(potential, 0, 1, 0)

        def contract(names, *extra):
            pieces = [w for name in names for w in (part[name], band_shift(part[name], 0, 0, 1))]
            return slab_call(names, fields, pieces, extra)

        part[2, 0], part[0, 1], fields = lax.optimization_barrier((part[2, 0], part[0, 1], fields))
        part[2, 1] = band_shift(part[2, 0], 0, 1, 0)
        for k in (1, 3):
            part[k, 1] = band_shift(part[0, 1], k, 0, 0)
        slab = contract(early)
        *got, slab = lax.optimization_barrier([part[name] for name in late] + [slab])
        part.update(zip(late, got))
        terms = contract(late, slab, amp)

    with jax.named_scope("ladder"):
        terms = lax.all_to_all(
            terms.reshape(GRID * BAND, XL, 128), ("grid", "band"), 0, 0, tiled=True
        )
        ladder = jnp.sum(terms.astype(F32), axis=0)
        return ladder.reshape(1, 16, ABLK)


def solution(mesh):
    in_specs = (
        P("band", "grid", None),
        P("band", "grid", None),
        P(None, "band", "grid"),
        P(),
        P(),
        P(("grid", "band"), None),
    )
    out_specs = P(None, ("grid", "band"), None)
    return jax.shard_map(
        per_device, mesh=mesh, in_specs=in_specs, out_specs=out_specs, check_vma=False
    )
```

```python
import functools
import math

import jax
import jax.numpy as jnp
import numpy as np
from jax import lax
from jax.experimental import pallas as pl
from jax.experimental.pallas import tpu as pltpu
from jax.sharding import PartitionSpec as P


N = 64
HALF = 32
ABLK = 64
GRID = 8
BAND = 16
XL = 8
SHARE = ABLK // BAND
PAIRS_Y = 32
F32 = jnp.float32
BF16 = jnp.bfloat16
VMEM_LIMIT = 16 * 1024 * 1024


@functools.cache
def tables():
    index = np.arange(N)
    phase = (index[:, None] * index[None, :]) % N
    angle = np.float32(2.0 * math.pi / N) * phase.astype(np.float32)
    cosine = np.cos(angle).astype(np.float32)
    sine = np.sin(angle).astype(np.float32)
    eye_x = np.eye(XL, dtype=np.float32)
    z_plain = np.concatenate([cosine[:HALF].T, -sine[:HALF].T], axis=1)
    z_turned = np.concatenate([z_plain[:, HALF:], -z_plain[:, :HALF]], axis=1)
    mz = np.zeros((SHARE, 2, N, 2, 2, SHARE, N), np.float32)
    for a in range(SHARE):
        for p in range(2):
            mz[a, p, :, 0, p, a, :] = z_plain
            mz[a, p, :, 1, p, a, :] = z_turned
    mzt = np.zeros((2, SHARE, N, SHARE, 2, N), np.float32)
    for a in range(SHARE):
        for p in range(2):
            mzt[p, a, :, a, p, :] = z_plain.T
    by_parity = np.stack([cosine, sine], axis=1).reshape(N, 2, PAIRS_Y, 2)
    ky = np.einsum("ktjp,xw->kxtpjw", by_parity, eye_x)
    signed = np.stack([cosine, -sine], axis=1).reshape(N, 2, PAIRS_Y, 2)
    kyt = np.einsum("ktjp,xw->pjxtkw", signed, eye_x)
    by_slab = np.stack([cosine, sine], axis=1).reshape(N, 2, GRID, XL)
    kx = np.einsum("ktgx,lm->lktgmx", by_slab, eye_x)
    signed_slab = np.stack([cosine, -sine], axis=1).reshape(N, 2, GRID, XL)
    kxt = np.einsum("ktgx,lm->gmxtlk", signed_slab, eye_x)
    turn = np.zeros((SHARE, 2, HALF, SHARE, 2, HALF), np.float32)
    for a in range(SHARE):
        turn[a, 1, :, a, 0, :] = np.eye(HALF)
        turn[a, 0, :, a, 1, :] = -np.eye(HALF)
    shapes = {
        "mz": (mz, 512, 1024),
        "mzt": (mzt, 512, 512),
        "ky": (ky, 512, 1024),
        "kyt": (kyt, 512, 1024),
        "kx": (kx, 512, 1024),
        "kxt": (kxt, 512, 1024),
        "turn": (turn, 256, 256),
    }
    return {n: v.reshape(r, c).astype(BF16) for n, (v, r, c) in shapes.items()}


def dot(a, b):
    return jnp.dot(a, b, preferred_element_type=F32)


def signed_freq(index):
    return (index + N // 2) % N - N // 2


def position():
    band = lax.axis_index("band")
    return band // 4, (band // 2) % 2, band % 2


def root_of(device):
    return device // 4, (device // 2) % 2, device % 2


def copies(sems, jobs):
    waits = []
    for slot, (target, choices) in enumerate(jobs):
        for condition, source in choices:
            move = pltpu.make_async_copy(source, target, sems.at[slot])
            if condition is None:
                move.start()
            else:
                pl.when(condition)(move.start)
        waits.append(pltpu.make_async_copy(target, target, sems.at[slot]))
    return waits


def gather(sems, jobs, start=None):
    finish = start() if start else None
    moves = copies(sems, jobs)
    if finish:
        moves += finish()
    wait_all(moves)


def wait_all(waits):
    for move in waits:
        move.wait()


class Roots:
    def __init__(self, ablock_ref, pairs_ref, fields, occupied):
        self.y, self.h, self.c = position()
        self.fields, self.occupied = fields, occupied
        start = ablock_ref[0] * ABLK
        self.first = start % fields.shape[0]
        devices = [start // fields.shape[0]]
        self.local = []
        for k in range(2 if pairs_ref is not None else 0):
            index = pairs_ref[0, k]
            devices.append(index // occupied.shape[0])
            self.local.append(index % occupied.shape[0])
        roots = [root_of(d) for d in devices]
        self.away = [(self.y - y + 4) % 4 for y, _, _ in roots]
        self.same_h = [h == self.h for _, h, _ in roots]
        self.same_c = [c == self.c for _, _, c in roots]

    def block(self, core, dy, h, count):
        start = self.first + 32 * core + 8 * ((self.y + dy) % 4) + 4 * h
        return self.fields.at[pl.ds(start, count)]

    def orbital(self, k):
        return self.occupied.at[pl.ds(self.local[k], 1)]


def core_a_body(ablock_ref, pairs_hbm, kept_hbm, fields, occupied, out, marks, kept_ref, pairs_ref, sems):
    (pairs_wait,) = copies(sems.at[10:], [(pairs_ref, [(None, pairs_hbm)])])
    at = Roots(ablock_ref, None, fields, occupied)
    other, there = 1 - at.c, 1 - at.h
    sources = [at.block(other, dy, there, 4) for dy in (1, 3, 2)]
    jobs = [(plane(out, pl.ds(4 * i, 4)), [(None, v)]) for i, v in enumerate(sources)]

    def start():
        (wait,) = copies(sems.at[9:], [(kept_ref, [(None, kept_hbm)])])
        return functools.partial(finish, wait)

    def finish(wait):
        wait.wait()
        kept = kept_ref[...]
        in_x = (lax.broadcasted_iota(jnp.int32, (N, kept.shape[1]), 0) == kept // 16).astype(BF16)
        in_c = lax.broadcasted_iota(jnp.int32, (128, kept.shape[1]), 0) % 16 == kept % 16
        mask = lax.dot_general(
            in_x, in_c.astype(BF16), (((1,), (1,)), ((), ())), preferred_element_type=F32
        )
        row = lax.broadcasted_iota(jnp.int32, mask.shape, 0)
        lane = lax.broadcasted_iota(jnp.int32, mask.shape, 1)
        mask = jnp.where(row % XL == lane // 16, mask, 0.0)
        marks[0] = jnp.sum(mask.reshape(XL, XL, 128), axis=1).astype(BF16)
        move = pltpu.make_async_copy(marks, marks_of(out, pl.ds(0, 1)), sems.at[8])
        move.start()
        pairs_wait.wait()
        orbital = occupied.at[pl.ds(pairs_ref[0, 0] % occupied.shape[0], 1)]
        return [move] + copies(sems.at[3:], [(plane(out, pl.ds(12, 1)), [(None, orbital)])])

    gather(sems, jobs, start)


def core_b_body(ablock_ref, pairs_ref, fields, occupied, amp_hbm, out, amp_out, amp_ref, sems):
    at = Roots(ablock_ref, pairs_ref, fields, occupied)
    other, here, there = 1 - at.c, at.h, 1 - at.h
    sources = [at.block(other, dy, h, 4) for dy, h in ((1, here), (3, here), (0, there), (2, here), (0, here))]
    jobs = [(out.at[4 * i : 4 * i + 4], [(None, v)]) for i, v in enumerate(sources)]
    jobs.append((out.at[20:], [(None, at.orbital(1))]))
    moves = copies(sems, jobs)
    (amp_wait,) = copies(sems.at[6:], [(amp_ref, [(None, amp_hbm.at[0])])])
    amp_wait.wait()
    row = lax.broadcasted_iota(jnp.int32, (128, 256), 0)
    col = lax.broadcasted_iota(jnp.int32, (128, 256), 1)
    over_c = (((1,), (1,)), ((), ()))
    parity = [
        lax.dot_general((col == 2 * row + p).astype(BF16), amp_ref[...], over_c, preferred_element_type=F32)
        for p in range(2)
    ]
    amp_out[...] = jnp.concatenate(parity, axis=1).astype(BF16)
    wait_all(moves)


def own_marks(at, target, sent_a, got_a):
    return [
        (marks_of(target, pl.ds(at.c, 1)), [(None, marks_of(sent_a, pl.ds(0, 1)))]),
        (marks_of(target, pl.ds(1 - at.c, 1)), [(None, marks_of(got_a, pl.ds(0, 1)))]),
    ]


def first_a_body(ablock_ref, pairs_ref, fields, occupied, sent_a, got_a, up, down, across, sems):
    at = Roots(ablock_ref, pairs_ref, fields, occupied)
    mine, theirs = at.same_c[0], jnp.logical_not(at.same_c[0])
    jobs = []
    for i, (target, dy) in enumerate(((up, 1), (down, 3), (across, 2))):
        own = at.block(at.c, dy, 1 - at.h, 4)
        jobs.append((plane(target, pl.ds(0, 4)), [(mine, own), (theirs, plane(got_a, pl.ds(4 * i, 4)))]))
    mine, theirs = at.same_c[1], jnp.logical_not(at.same_c[1])
    for target in (up, down, across):
        partner = plane(got_a, pl.ds(12, 1))
        jobs.append((plane(target, pl.ds(4, 1)), [(mine, at.orbital(0)), (theirs, partner)]))
        jobs += own_marks(at, target, sent_a, got_a)
    gather(sems, jobs)


def first_b_body(ablock_ref, pairs_ref, fields, occupied, got_b, up, down, across, sems):
    at = Roots(ablock_ref, pairs_ref, fields, occupied)
    mine, theirs = at.same_c[0], jnp.logical_not(at.same_c[0])
    jobs = []
    for i, (target, dy, h) in enumerate(((up, 1, at.h), (down, 3, at.h), (across, 0, 1 - at.h))):
        own = at.block(at.c, dy, h, 4)
        jobs.append((target.at[:4], [(mine, own), (theirs, got_b.at[4 * i : 4 * i + 4])]))
    mine, theirs = at.same_c[2], jnp.logical_not(at.same_c[2])
    for target in (up, down, across):
        jobs.append((target.at[4:], [(mine, at.orbital(1)), (theirs, got_b.at[20:])]))
    gather(sems, jobs)


def second_a_body(
    ablock_ref, pairs_ref, fields, occupied, sent_a, got_a, got_b, crossed, below, above, far, turn, sems
):
    at = Roots(ablock_ref, pairs_ref, fields, occupied)
    not_ = jnp.logical_not
    jobs = []
    own_rows = (at.block(at.c, 2, at.h, 4), got_b.at[12:16], pl.ds(0, 4))
    own_orbital = (at.orbital(0), plane(got_a, pl.ds(12, 1)), pl.ds(4, 1))
    for k, (own, core, part) in enumerate((own_rows, own_orbital)):
        same_h, same_c = at.same_h[k], at.same_c[k]
        other = plane(crossed, part)
        choices = [(same_h & same_c, own), (same_h & not_(same_c), core), (not_(same_h), other)]
        jobs.append((plane(far, part), choices))
        from_below = at.away[k] == 1
        choices = [(from_below, plane(below, part)), (not_(from_below), plane(above, part))]
        jobs.append((plane(turn, part), choices))
    jobs += own_marks(at, far, sent_a, got_a)
    for target, first, source in ((far, 2, crossed), (turn, 0, below), (turn, 2, above)):
        jobs.append((marks_of(target, pl.ds(first, 2)), [(None, marks_of(source, pl.ds(0, 2)))]))
    gather(sems, jobs)


def arrived(at, k, own, core, cross, far, below, above, turned):
    not_ = jnp.logical_not
    away, same_h, same_c = at.away[k], at.same_h[k], at.same_c[k]
    return [
        ((away == 0) & same_h & same_c, own),
        ((away == 0) & same_h & not_(same_c), core),
        ((away == 0) & not_(same_h), cross),
        (away == 2, far),
        ((away == 1) & same_h, below),
        ((away == 3) & same_h, above),
        ((away % 2 == 1) & not_(same_h), turned),
    ]


def forward_body(
    ablock_ref,
    pairs_ref,
    fields,
    occupied,
    sent_a,
    got_a,
    got_b,
    crossed_a,
    below_a,
    above_a,
    crossed_b,
    below_b,
    above_b,
    far,
    turned,
    amp_hbm,
    mz_hbm,
    ky_hbm,
    out_hbm,
    tiles_ref,
    second_ref,
    far_ref,
    turn_ref,
    u_ref,
    o_ref,
    mz_ref,
    ky_ref,
    out_ref,
    amp_ref,
    sems,
):
    at = Roots(ablock_ref, pairs_ref, fields, occupied)
    rows = [crossed_b.at[:4], plane(far, pl.ds(0, 4)), below_b.at[:4], above_b.at[:4], plane(turned, pl.ds(0, 4))]
    orbital = [plane(v, pl.ds(4, 1)) for v in (crossed_a, far, below_a, above_a, turned)]
    jobs = [
        (u_ref, arrived(at, 0, at.block(at.c, 0, at.h, 4), got_b.at[16:20], *rows)),
        (o_ref, arrived(at, 1, at.orbital(0), plane(got_a, pl.ds(12, 1)), *orbital)),
    ]
    jobs += [(mz_ref, [(None, mz_hbm)]), (ky_ref, [(None, ky_hbm)]), (amp_ref, [(None, amp_hbm)])]
    u_wait, o_wait, mz_wait, ky_wait, amp_wait = copies(sems, jobs)
    device = lambda dy, dh, c: 4 * ((at.y + dy) % 4) + 2 * ((at.h + dh) % 2) + c
    jobs = [
        (tiles_ref.at[pl.ds(device(0, 0, at.c), 1)], [(None, marks_of(sent_a, pl.ds(0, 1)))]),
        (tiles_ref.at[pl.ds(device(0, 0, 1 - at.c), 1)], [(None, marks_of(got_a, pl.ds(0, 1)))]),
    ]
    pairs = [(0, 1, crossed_a, 0), (3, 0, below_a, 0), (1, 0, above_a, 0), (2, 0, far, 0), (2, 1, far, 2)]
    for dy, dh, source, first in pairs + [(3, 1, turned, 0), (1, 1, turned, 2)]:
        place = tiles_ref.at[pl.ds(device(dy, dh, 0), 2)]
        jobs.append((place, [(None, marks_of(source, pl.ds(first, 2)))]))
    mark_waits = copies(sems.at[21:], jobs)
    own, core = at.orbital(1), got_b.at[20:]
    crossed, below, above = (v.at[4:] for v in (crossed_b, below_b, above_b))
    not_ = jnp.logical_not
    same_h, same_c, from_below = at.same_h[2], at.same_c[2], at.away[2] == 1
    jobs = [
        (second_ref, arrived(at, 2, own, core, crossed, own, below, above, own)),
        (far_ref, [(same_h & same_c, own), (same_h & not_(same_c), core), (not_(same_h), crossed)]),
        (turn_ref, [(from_below, below), (not_(from_below), above)]),
    ]
    second_waits = copies(sems.at[30:], jobs)
    u_wait.wait()
    o_wait.wait()
    orbital = o_ref[0].astype(F32)
    columns = []
    for a in range(SHARE):
        density = u_ref[a].astype(F32) * orbital
        columns.append(
            jnp.concatenate([density[:, 128 * j : 128 * (j + 1)] for j in range(PAIRS_Y)], axis=0)
        )
    density = jnp.concatenate(columns, axis=1).astype(BF16)
    mz_wait.wait()
    zfreq = dot(density, mz_ref[...]).astype(BF16)
    stacked = jnp.concatenate([zfreq[:, 256 * i : 256 * (i + 1)] for i in range(4)], axis=0)
    ky_wait.wait()
    amp_wait.wait()
    jobs = [(out_hbm.at[g, pl.ds(64, 128)], [(None, amp_ref)]) for g in range(GRID)]
    out_waits = copies(sems.at[5:], jobs)
    out_ref[...] = dot(ky_ref[...], stacked).astype(BF16)
    jobs = [(out_hbm.at[g, pl.ds(0, 64)], [(None, out_ref.at[pl.ds(64 * g, 64)])]) for g in range(GRID)]
    wait_all(out_waits + mark_waits + second_waits + copies(sems.at[13:], jobs))


def middle_body(
    y_hbm, weight_ref, turn_hbm, kx_hbm, kxt_hbm, out_hbm, y_ref, turn_ref, kx_ref, kxt_ref, out_ref, sems
):
    jobs = [(y_ref, y_hbm.at[:, pl.ds(0, 64)]), (turn_ref, turn_hbm), (kx_ref, kx_hbm), (kxt_ref, kxt_hbm)]
    y_wait, turn_wait, kx_wait, kxt_wait = copies(sems, [(t, [(None, v)]) for t, v in jobs])
    weights = jnp.concatenate([weight_ref[...], weight_ref[...]], axis=1)
    y_wait.wait()
    turn_wait.wait()
    turn = turn_ref[...]
    yfreq = y_ref[...].reshape(512, 256)
    both = jnp.concatenate([yfreq, dot(yfreq, turn).astype(BF16)], axis=0)
    kx_wait.wait()
    potential = (dot(kx_ref[...], both) * weights).astype(BF16)
    both = jnp.concatenate([potential, dot(potential, turn).astype(BF16)], axis=0)
    kxt_wait.wait()
    out_ref[...] = dot(kxt_ref[...], both).astype(BF16)
    wait_all(copies(sems.at[4:], [(out_hbm, [(None, out_ref)])]))


def backward_body(
    ablock_ref,
    pairs_ref,
    fields,
    occupied,
    second,
    far,
    turned,
    turn_hbm,
    kyt_hbm,
    mzt_hbm,
    h_ref,
    out_ref,
    o_ref,
    turn_ref,
    kyt_ref,
    mzt_ref,
    sems,
):
    at = Roots(ablock_ref, pairs_ref, fields, occupied)
    jobs = [
        (o_ref, arrived(at, 2, second, second, second, far, second, second, turned)),
        (turn_ref, [(None, turn_hbm)]),
        (kyt_ref, [(None, kyt_hbm)]),
        (mzt_ref, [(None, mzt_hbm)]),
    ]
    o_wait, turn_wait, kyt_wait, mzt_wait = copies(sems, jobs)
    freq = h_ref[...]
    turn_wait.wait()
    both = jnp.concatenate([freq, dot(freq, turn_ref[...]).astype(BF16)], axis=0)
    kyt_wait.wait()
    zfreq = dot(kyt_ref[...], both).astype(BF16)
    zfreq = jnp.concatenate([zfreq[:256], zfreq[256:]], axis=1)
    mzt_wait.wait()
    value = dot(zfreq, mzt_ref[...])
    o_wait.wait()
    orbital = o_ref[0].astype(F32)
    for a in range(SHARE):
        rows = [value[8 * j : 8 * (j + 1), 128 * a : 128 * (a + 1)] for j in range(PAIRS_Y)]
        out_ref[a] = (jnp.concatenate(rows, axis=1) * orbital).astype(BF16)


def weight_body(tiles_ref, out_ref):
    tiles = tiles_ref[...].astype(F32).reshape(BAND * XL, 128).astype(BF16)
    shape = (BAND * N, BAND * XL)
    row = lax.broadcasted_iota(jnp.int32, shape, 0)
    lane = lax.broadcasted_iota(jnp.int32, shape, 1)
    spread = dot((row // XL == lane).astype(BF16), tiles)
    spread = jnp.where(row % XL == lane // 16, spread, 0.0).astype(BF16)
    row = lax.broadcasted_iota(jnp.int32, (128, 128), 0)
    lane = lax.broadcasted_iota(jnp.int32, (128, 128), 1)
    spread = dot(spread, (row % 16 == lane % 16).astype(BF16))
    low = lax.broadcasted_iota(jnp.int32, (N, 128), 1) % HALF < 16
    blocks = [spread[N * n : N * (n + 1)] for n in range(BAND)]
    kept = jnp.concatenate([jnp.where(low, blocks[2 * m], blocks[2 * m + 1]) for m in range(XL)], axis=0)
    shape = (N * XL, 128)
    row = lax.broadcasted_iota(jnp.int32, shape, 0)
    lane = lax.broadcasted_iota(jnp.int32, shape, 1)
    freq_x = signed_freq(row % N)
    freq_y = signed_freq(lax.axis_index("grid") * XL + row // N)
    freq_z = lane % HALF
    squared = (freq_x * freq_x + freq_y * freq_y + freq_z * freq_z).astype(F32)
    out_ref[...] = kept / (float(N * N * N) * (squared + 1.0))


def arrival_body(first, second, third, amp_ref, out_ref):
    out_ref[...] = amp_ref[...]


def copy_body(source, target, sems):
    wait_all(copies(sems, [(target, [(None, source)])]))


SMEM, VMEM, HBM = pltpu.SMEM, pltpu.VMEM, pltpu.HBM
PLANE = (XL, N * N)
LONG = (XL, N * N + 128)
GRIDPOINTS, MARKS = pl.ds(0, N * N), pl.ds(N * N, 128)


def plane(ref, *index):
    return ref.at[*index, :, GRIDPOINTS]


def marks_of(ref, *index):
    return ref.at[*index, :, MARKS]


def call(body, spaces, outs, out_spaces, scratch, args, dtype=BF16, flops=10**8):
    many = len(outs) > 1
    shapes = [jax.ShapeDtypeStruct(o, dtype) for o in outs]
    specs = [pl.BlockSpec(memory_space=m) for m in out_spaces]
    return pl.pallas_call(
        body,
        out_shape=shapes if many else shapes[0],
        in_specs=[pl.BlockSpec(memory_space=m) for m in spaces],
        out_specs=specs if many else specs[0],
        scratch_shapes=scratch,
        compiler_params=pltpu.CompilerParams(vmem_limit_bytes=VMEM_LIMIT),
        cost_estimate=pl.CostEstimate(flops=flops, bytes_accessed=2**20, transcendentals=0),
    )(*args)


def slab_body(last, names, u_ref, *refs):
    pieces = 2 * len(names)
    w_refs, extra = refs[:pieces], refs[pieces:-2]
    out_ref, total = refs[-2:]
    lanes = 2048
    for s in range(N * N // lanes):
        part = pl.ds(s * lanes, lanes)
        right = jnp.concatenate([w[:, part] for w in w_refs], axis=0)
        gram = lax.dot_general(u_ref[:, part], right, (((1,), (1,)), ((), ())), preferred_element_type=F32)
        if s == 0:
            total[...] = gram
        else:
            total[...] += gram
    gram = total[...]
    wide = gram.shape[1]
    row = lax.broadcasted_iota(jnp.int32, gram.shape, 0) % XL
    col = lax.broadcasted_iota(jnp.int32, gram.shape, 1) % XL
    gram = jnp.where(row == col, gram, 0.0)
    gram = jnp.sum(gram.reshape(gram.shape[0] // XL, XL, wide), axis=1)
    y, h, c = position()
    row = lax.broadcasted_iota(jnp.int32, (SHARE * XL, 128), 0) // XL
    lane = lax.broadcasted_iota(jnp.int32, (SHARE * XL, 128), 1) % ABLK
    pick = []
    for dy, dh in names:
        for dc in range(2):
            first = 32 * ((c + dc) % 2) + 8 * ((y - dy + 4) % 4) + 4 * ((h + dh) % 2)
            pick.append((lane == first + row).astype(F32))
    pick = jnp.concatenate(pick, axis=0)
    slab = jnp.dot(gram, pick, precision=lax.Precision.HIGHEST, preferred_element_type=F32)
    if extra:
        slab = slab + extra[0][...]
    if not last:
        out_ref[...] = slab
    else:
        lane = lax.broadcasted_iota(jnp.int32, slab.shape, 1)
        zero = jnp.zeros_like(slab)
        slab = jnp.concatenate(
            [jnp.where(lane < ABLK, slab, zero), jnp.where(lane < ABLK, zero, slab)], axis=0
        )
        high = slab.astype(BF16)
        low = (slab - high.astype(F32)).astype(BF16)
        amp = extra[1][:, pl.ds(64, 128)].reshape(1024, 256)
        out_ref[...] = (dot(amp, high) + dot(amp, low)).astype(BF16)


def slab_call(names, fields, parts, extra=()):
    last = len(extra) > 1
    tall = fields.shape[0]
    wide = sum(p.shape[0] for p in parts)
    out = (1024, 128) if last else (tall // XL, 128)
    args = (fields, *parts, *extra)
    return pl.pallas_call(
        functools.partial(slab_body, last, names),
        out_shape=jax.ShapeDtypeStruct(out, BF16 if last else F32),
        in_specs=[pl.BlockSpec(memory_space=VMEM)] * len(args),
        out_specs=pl.BlockSpec(memory_space=VMEM),
        scratch_shapes=[VMEM((tall, wide), F32)],
        compiler_params=pltpu.CompilerParams(vmem_limit_bytes=24 * 1024 * 1024),
        cost_estimate=pl.CostEstimate(
            flops=2 * tall * wide * N * N, bytes_accessed=2 * tall * N * N, transcendentals=0
        ),
    )(*args)


def band_shift(value, dy, dh, dc):
    pairs = []
    for y in range(4):
        for h in range(2):
            for c in range(2):
                pairs.append((4 * y + 2 * h + c, 4 * ((y + dy) % 4) + 2 * ((h + dh) % 2) + (c + dc) % 2))
    return lax.ppermute(value, "band", pairs)


def per_device(virtual_field, occupied_field, amplitudes, ablock, pairs, kept_cells):
    far_memory = lambda v: pltpu.with_memory_space_constraint(v, HBM)
    const = {n: far_memory(jnp.asarray(v)) for n, v in tables().items()}
    roots = (ablock, pairs, far_memory(virtual_field), far_memory(occupied_field))
    root_spaces = [SMEM, SMEM, pl.ANY, pl.ANY]

    with jax.named_scope("block_scatter"):
        sems = lambda n: [pltpu.SemaphoreType.DMA((n,))]
        rows = lambda n: (n,) + PLANE
        held = lambda n: VMEM(rows(n), BF16)
        hop = lambda body, spaces, out, scratch, *args, flops=10**8: call(
            body, spaces, out, [pl.ANY] * len(out), scratch, args, flops=flops
        )
        any_ = [pl.ANY]
        sent_a = hop(
            core_a_body,
            [SMEM] + any_ * 4,
            [(13,) + LONG],
            [VMEM((1, XL, 128), BF16), VMEM(kept_cells.shape, jnp.int32), SMEM((1, 2), jnp.int32)] + sems(11),
            ablock,
            far_memory(pairs),
            far_memory(kept_cells),
            *roots[2:],
        )
        got_a = band_shift(sent_a, 0, 0, 1)
        sent_b, amp = call(
            core_b_body,
            root_spaces + any_,
            [rows(21), (128, 256)],
            any_ + [VMEM],
            [VMEM((128, 256), BF16)] + sems(7),
            roots + (far_memory(amplitudes),),
            flops=5 * 10**9,
        )
        up, down, across = hop(
            first_a_body,
            root_spaces + any_ * 2,
            [(5,) + LONG] * 3,
            sems(12),
            *roots,
            sent_a,
            got_a,
        )
        up, down, across, sent_b = lax.optimization_barrier((up, down, across, sent_b))
        below_a = band_shift(up, 1, 0, 0)
        above_a = band_shift(down, 3, 0, 0)
        crossed_a = band_shift(across, 0, 1, 0)
        got_b = band_shift(sent_b, 0, 0, 1)
        up, down, across = hop(
            first_b_body, root_spaces + any_, [rows(5)] * 3, sems(6), *roots, got_b
        )
        below_b = band_shift(up, 1, 0, 0)
        above_b = band_shift(down, 3, 0, 0)
        crossed_b = band_shift(across, 0, 1, 0)
        crossed_a, below_a, above_a, _ = lax.optimization_barrier((crossed_a, below_a, above_a, (up, down, across)))
        far, turn = hop(
            second_a_body,
            root_spaces + any_ * 6,
            [(5,) + LONG] * 2,
            sems(9),
            *roots,
            sent_a,
            got_a,
            got_b,
            crossed_a,
            below_a,
            above_a,
            flops=10**10,
        )
        far_a = band_shift(far, 2, 0, 0)
        turned_a = band_shift(turn, 0, 1, 0)

        behind = (crossed_b, below_b, above_b, amp)
        amp = call(arrival_body, any_ * 3 + [VMEM], [(128, 256)], [VMEM], [], behind, flops=10**10)
        far_a, turned_a, amp = lax.optimization_barrier((far_a, turned_a, amp))

    with jax.named_scope("transform"):
        big = VMEM((512, 1024), BF16)
        from_all = (GRID, 64 + 128, 256)
        freq, tiles, second, far, turn = call(
            forward_body,
            root_spaces + any_ * 14,
            [from_all, (BAND, XL, 128)] + [rows(1)] * 3,
            any_ + [VMEM] * 4,
            [held(SHARE), held(1), big, big, VMEM((512, 256), BF16), VMEM((128, 256), BF16)] + sems(33),
            roots
            + (sent_a, got_a, got_b, crossed_a, below_a, above_a, crossed_b, below_b, above_b, far_a, turned_a)
            + (amp, const["mz"], const["ky"]),
            flops=2 * 10**10,
        )
        freq = lax.all_to_all(freq, "grid", 0, 0, tiled=True)
        amp = freq
        far_b = band_shift(far, 2, 0, 0)
        turned_b = band_shift(turn, 0, 1, 0)
        weights = call(
            weight_body,
            [VMEM],
            [(N * XL, 128)],
            [VMEM],
            [],
            (tiles,),
            F32,
        )
        freq = call(
            middle_body,
            any_ + [VMEM] + any_ * 3,
            [(512, 256)],
            any_,
            [VMEM((GRID, 64, 256), BF16), VMEM((256, 256), BF16), big, big, VMEM((512, 256), BF16)] + sems(5),
            (freq, weights, const["turn"], const["kx"], const["kxt"]),
            flops=10**10,
        )
        freq = lax.all_to_all(freq, "grid", 0, 0, tiled=True)
        potential = call(
            backward_body,
            root_spaces + any_ * 6 + [VMEM],
            [(SHARE,) + PLANE],
            [VMEM],
            [held(1), VMEM((256, 256), BF16), big, VMEM((512, 512), BF16)] + sems(4),
            roots
            + (second, far_b, turned_b)
            + (const["turn"], const["kyt"], const["mzt"], freq),
        )

    with jax.named_scope("block_gather"):
        early, late = ((0, 0), (2, 0), (1, 0), (3, 0), (0, 1)), ((2, 1), (1, 1), (3, 1))
        shape = (virtual_field.shape[0] * XL, N * N)
        potential, fields = lax.optimization_barrier(
            (potential.reshape(SHARE * XL, N * N), virtual_field.reshape(shape))
        )
        fields = call(copy_body, [pl.ANY], [shape], [pl.ANY], sems(1), (far_memory(fields),))
        part = {(0, 0): potential}
        for k in (2, 1, 3):
            part[k, 0] = band_shift(potential, k, 0, 0)
        part[0, 1] = band_shift(potential, 0, 1, 0)

        def contract(names, *extra):
            pieces = [w for name in names for w in (part[name], band_shift(part[name], 0, 0, 1))]
            return slab_call(names, fields, pieces, extra)

        part[2, 0], part[0, 1], fields = lax.optimization_barrier((part[2, 0], part[0, 1], fields))
        part[2, 1] = band_shift(part[2, 0], 0, 1, 0)
        for k in (1, 3):
            part[k, 1] = band_shift(part[0, 1], k, 0, 0)
        slab = contract(early)
        *got, slab = lax.optimization_barrier([part[name] for name in late] + [slab])
        part.update(zip(late, got))
        terms = contract(late, slab, amp)

    with jax.named_scope("ladder"):
        terms = lax.all_to_all(
            terms.reshape(GRID * BAND, XL, 128), ("grid", "band"), 0, 0, tiled=True
        )
        ladder = jnp.sum(terms.astype(F32), axis=0)
        return ladder.reshape(1, 16, ABLK)


def solution(mesh):
    in_specs = (
        P("band", "grid", None),
        P("band", "grid", None),
        P(None, "band", "grid"),
        P(),
        P(),
        P(("grid", "band"), None),
    )
    out_specs = P(None, ("grid", "band"), None)
    return jax.shard_map(
        per_device, mesh=mesh, in_specs=in_specs, out_specs=out_specs, check_vma=False
    )
```

```python
import functools
import math

import jax
import jax.numpy as jnp
import numpy as np
from jax import lax
from jax.experimental import pallas as pl
from jax.experimental.pallas import tpu as pltpu
from jax.sharding import PartitionSpec as P


N = 64
HALF = 32
ABLK = 64
GRID = 8
BAND = 16
XL = 8
SHARE = ABLK // BAND
PAIRS_Y = 32
F32 = jnp.float32
BF16 = jnp.bfloat16
VMEM_LIMIT = 16 * 1024 * 1024


@functools.cache
def tables():
    index = np.arange(N)
    phase = (index[:, None] * index[None, :]) % N
    angle = np.float32(2.0 * math.pi / N) * phase.astype(np.float32)
    cosine = np.cos(angle).astype(np.float32)
    sine = np.sin(angle).astype(np.float32)
    eye_x = np.eye(XL, dtype=np.float32)
    z_plain = np.concatenate([cosine[:HALF].T, -sine[:HALF].T], axis=1)
    z_turned = np.concatenate([z_plain[:, HALF:], -z_plain[:, :HALF]], axis=1)
    mz = np.zeros((SHARE, 2, N, 2, 2, SHARE, N), np.float32)
    for a in range(SHARE):
        for p in range(2):
            mz[a, p, :, 0, p, a, :] = z_plain
            mz[a, p, :, 1, p, a, :] = z_turned
    mzt = np.zeros((2, SHARE, N, SHARE, 2, N), np.float32)
    for a in range(SHARE):
        for p in range(2):
            mzt[p, a, :, a, p, :] = z_plain.T
    by_parity = np.stack([cosine, sine], axis=1).reshape(N, 2, PAIRS_Y, 2)
    ky = np.einsum("ktjp,xw->kxtpjw", by_parity, eye_x)
    signed = np.stack([cosine, -sine], axis=1).reshape(N, 2, PAIRS_Y, 2)
    kyt = np.einsum("ktjp,xw->pjxtkw", signed, eye_x)
    by_slab = np.stack([cosine, sine], axis=1).reshape(N, 2, GRID, XL)
    kx = np.einsum("ktgx,lm->lktgmx", by_slab, eye_x)
    signed_slab = np.stack([cosine, -sine], axis=1).reshape(N, 2, GRID, XL)
    kxt = np.einsum("ktgx,lm->gmxtlk", signed_slab, eye_x)
    turn = np.zeros((SHARE, 2, HALF, SHARE, 2, HALF), np.float32)
    for a in range(SHARE):
        turn[a, 1, :, a, 0, :] = np.eye(HALF)
        turn[a, 0, :, a, 1, :] = -np.eye(HALF)
    shapes = {
        "mz": (mz, 512, 1024),
        "mzt": (mzt, 512, 512),
        "ky": (ky, 512, 1024),
        "kyt": (kyt, 512, 1024),
        "kx": (kx, 512, 1024),
        "kxt": (kxt, 512, 1024),
        "turn": (turn, 256, 256),
    }
    return {n: v.reshape(r, c).astype(BF16) for n, (v, r, c) in shapes.items()}


def dot(a, b):
    return jnp.dot(a, b, preferred_element_type=F32)


def signed_freq(index):
    return (index + N // 2) % N - N // 2


def position():
    band = lax.axis_index("band")
    return band // 4, (band // 2) % 2, band % 2


def root_of(device):
    return device // 4, (device // 2) % 2, device % 2


def copies(sems, jobs):
    waits = []
    for slot, (target, choices) in enumerate(jobs):
        for condition, source in choices:
            move = pltpu.make_async_copy(source, target, sems.at[slot])
            if condition is None:
                move.start()
            else:
                pl.when(condition)(move.start)
        waits.append(pltpu.make_async_copy(target, target, sems.at[slot]))
    return waits


def gather(sems, jobs, start=None):
    finish = start() if start else None
    moves = copies(sems, jobs)
    if finish:
        moves += finish()
    wait_all(moves)


def wait_all(waits):
    for move in waits:
        move.wait()


class Roots:
    def __init__(self, ablock_ref, pairs_ref, fields, occupied):
        self.y, self.h, self.c = position()
        self.fields, self.occupied = fields, occupied
        start = ablock_ref[0] * ABLK
        self.first = start % fields.shape[0]
        devices = [start // fields.shape[0]]
        self.local = []
        for k in range(2 if pairs_ref is not None else 0):
            index = pairs_ref[0, k]
            devices.append(index // occupied.shape[0])
            self.local.append(index % occupied.shape[0])
        roots = [root_of(d) for d in devices]
        self.away = [(self.y - y + 4) % 4 for y, _, _ in roots]
        self.same_h = [h == self.h for _, h, _ in roots]
        self.same_c = [c == self.c for _, _, c in roots]

    def block(self, core, dy, h, count):
        start = self.first + 32 * core + 8 * ((self.y + dy) % 4) + 4 * h
        return self.fields.at[pl.ds(start, count)]

    def orbital(self, k):
        return self.occupied.at[pl.ds(self.local[k], 1)]


def core_a_body(ablock_ref, pairs_hbm, kept_hbm, fields, occupied, out, marks, kept_ref, pairs_ref, sems):
    (pairs_wait,) = copies(sems.at[10:], [(pairs_ref, [(None, pairs_hbm)])])
    at = Roots(ablock_ref, None, fields, occupied)
    other, there = 1 - at.c, 1 - at.h
    sources = [at.block(other, dy, there, 4) for dy in (1, 3, 2)]
    jobs = [(plane(out, pl.ds(4 * i, 4)), [(None, v)]) for i, v in enumerate(sources)]

    def start():
        (wait,) = copies(sems.at[9:], [(kept_ref, [(None, kept_hbm)])])
        return functools.partial(finish, wait)

    def finish(wait):
        wait.wait()
        kept = kept_ref[...]
        in_x = (lax.broadcasted_iota(jnp.int32, (N, kept.shape[1]), 0) == kept // 16).astype(BF16)
        in_c = lax.broadcasted_iota(jnp.int32, (128, kept.shape[1]), 0) % 16 == kept % 16
        mask = lax.dot_general(
            in_x, in_c.astype(BF16), (((1,), (1,)), ((), ())), preferred_element_type=F32
        )
        row = lax.broadcasted_iota(jnp.int32, mask.shape, 0)
        lane = lax.broadcasted_iota(jnp.int32, mask.shape, 1)
        mask = jnp.where(row % XL == lane // 16, mask, 0.0)
        marks[0] = jnp.sum(mask.reshape(XL, XL, 128), axis=1).astype(BF16)
        move = pltpu.make_async_copy(marks, marks_of(out, pl.ds(0, 1)), sems.at[8])
        move.start()
        pairs_wait.wait()
        orbital = occupied.at[pl.ds(pairs_ref[0, 0] % occupied.shape[0], 1)]
        return [move] + copies(sems.at[3:], [(plane(out, pl.ds(12, 1)), [(None, orbital)])])

    gather(sems, jobs, start)


def core_b_body(ablock_ref, pairs_ref, fields, occupied, amp_hbm, out, amp_out, amp_ref, sems):
    at = Roots(ablock_ref, pairs_ref, fields, occupied)
    other, here, there = 1 - at.c, at.h, 1 - at.h
    sources = [at.block(other, dy, h, 4) for dy, h in ((1, here), (3, here), (0, there), (2, here), (0, here))]
    jobs = [(out.at[4 * i : 4 * i + 4], [(None, v)]) for i, v in enumerate(sources)]
    jobs.append((out.at[20:], [(None, at.orbital(1))]))
    moves = copies(sems, jobs)
    (amp_wait,) = copies(sems.at[6:], [(amp_ref, [(None, amp_hbm.at[0])])])
    amp_wait.wait()
    row = lax.broadcasted_iota(jnp.int32, (128, 256), 0)
    col = lax.broadcasted_iota(jnp.int32, (128, 256), 1)
    over_c = (((1,), (1,)), ((), ()))
    parity = [
        lax.dot_general((col == 2 * row + p).astype(BF16), amp_ref[...], over_c, preferred_element_type=F32)
        for p in range(2)
    ]
    amp_out[...] = jnp.concatenate(parity, axis=1).astype(BF16)
    wait_all(moves)


def own_marks(at, target, sent_a, got_a):
    return [
        (marks_of(target, pl.ds(at.c, 1)), [(None, marks_of(sent_a, pl.ds(0, 1)))]),
        (marks_of(target, pl.ds(1 - at.c, 1)), [(None, marks_of(got_a, pl.ds(0, 1)))]),
    ]


def first_a_body(ablock_ref, pairs_ref, fields, occupied, sent_a, got_a, up, down, across, sems):
    at = Roots(ablock_ref, pairs_ref, fields, occupied)
    mine, theirs = at.same_c[0], jnp.logical_not(at.same_c[0])
    jobs = []
    for i, (target, dy) in enumerate(((up, 1), (down, 3), (across, 2))):
        own = at.block(at.c, dy, 1 - at.h, 4)
        jobs.append((plane(target, pl.ds(0, 4)), [(mine, own), (theirs, plane(got_a, pl.ds(4 * i, 4)))]))
    mine, theirs = at.same_c[1], jnp.logical_not(at.same_c[1])
    for target in (up, down, across):
        partner = plane(got_a, pl.ds(12, 1))
        jobs.append((plane(target, pl.ds(4, 1)), [(mine, at.orbital(0)), (theirs, partner)]))
        jobs += own_marks(at, target, sent_a, got_a)
    gather(sems, jobs)


def first_b_body(ablock_ref, pairs_ref, fields, occupied, got_b, up, down, across, sems):
    at = Roots(ablock_ref, pairs_ref, fields, occupied)
    mine, theirs = at.same_c[0], jnp.logical_not(at.same_c[0])
    jobs = []
    for i, (target, dy, h) in enumerate(((up, 1, at.h), (down, 3, at.h), (across, 0, 1 - at.h))):
        own = at.block(at.c, dy, h, 4)
        jobs.append((target.at[:4], [(mine, own), (theirs, got_b.at[4 * i : 4 * i + 4])]))
    mine, theirs = at.same_c[2], jnp.logical_not(at.same_c[2])
    for target in (up, down, across):
        jobs.append((target.at[4:], [(mine, at.orbital(1)), (theirs, got_b.at[20:])]))
    gather(sems, jobs)


def second_a_body(
    ablock_ref, pairs_ref, fields, occupied, sent_a, got_a, got_b, crossed, below, above, far, turn, sems
):
    at = Roots(ablock_ref, pairs_ref, fields, occupied)
    not_ = jnp.logical_not
    jobs = []
    own_rows = (at.block(at.c, 2, at.h, 4), got_b.at[12:16], pl.ds(0, 4))
    own_orbital = (at.orbital(0), plane(got_a, pl.ds(12, 1)), pl.ds(4, 1))
    for k, (own, core, part) in enumerate((own_rows, own_orbital)):
        same_h, same_c = at.same_h[k], at.same_c[k]
        other = plane(crossed, part)
        choices = [(same_h & same_c, own), (same_h & not_(same_c), core), (not_(same_h), other)]
        jobs.append((plane(far, part), choices))
        from_below = at.away[k] == 1
        choices = [(from_below, plane(below, part)), (not_(from_below), plane(above, part))]
        jobs.append((plane(turn, part), choices))
    jobs += own_marks(at, far, sent_a, got_a)
    for target, first, source in ((far, 2, crossed), (turn, 0, below), (turn, 2, above)):
        jobs.append((marks_of(target, pl.ds(first, 2)), [(None, marks_of(source, pl.ds(0, 2)))]))
    gather(sems, jobs)


def arrived(at, k, own, core, cross, far, below, above, turned):
    not_ = jnp.logical_not
    away, same_h, same_c = at.away[k], at.same_h[k], at.same_c[k]
    return [
        ((away == 0) & same_h & same_c, own),
        ((away == 0) & same_h & not_(same_c), core),
        ((away == 0) & not_(same_h), cross),
        (away == 2, far),
        ((away == 1) & same_h, below),
        ((away == 3) & same_h, above),
        ((away % 2 == 1) & not_(same_h), turned),
    ]


def forward_body(
    ablock_ref,
    pairs_ref,
    fields,
    occupied,
    sent_a,
    got_a,
    got_b,
    crossed_a,
    below_a,
    above_a,
    crossed_b,
    below_b,
    above_b,
    far,
    turned,
    amp_hbm,
    mz_hbm,
    ky_hbm,
    out_hbm,
    tiles_ref,
    second_ref,
    far_ref,
    turn_ref,
    u_ref,
    o_ref,
    mz_ref,
    ky_ref,
    out_ref,
    amp_ref,
    sems,
):
    at = Roots(ablock_ref, pairs_ref, fields, occupied)
    rows = [crossed_b.at[:4], plane(far, pl.ds(0, 4)), below_b.at[:4], above_b.at[:4], plane(turned, pl.ds(0, 4))]
    orbital = [plane(v, pl.ds(4, 1)) for v in (crossed_a, far, below_a, above_a, turned)]
    jobs = [
        (u_ref, arrived(at, 0, at.block(at.c, 0, at.h, 4), got_b.at[16:20], *rows)),
        (o_ref, arrived(at, 1, at.orbital(0), plane(got_a, pl.ds(12, 1)), *orbital)),
    ]
    jobs += [(mz_ref, [(None, mz_hbm)]), (ky_ref, [(None, ky_hbm)]), (amp_ref, [(None, amp_hbm)])]
    u_wait, o_wait, mz_wait, ky_wait, amp_wait = copies(sems, jobs)
    device = lambda dy, dh, c: 4 * ((at.y + dy) % 4) + 2 * ((at.h + dh) % 2) + c
    jobs = [
        (tiles_ref.at[pl.ds(device(0, 0, at.c), 1)], [(None, marks_of(sent_a, pl.ds(0, 1)))]),
        (tiles_ref.at[pl.ds(device(0, 0, 1 - at.c), 1)], [(None, marks_of(got_a, pl.ds(0, 1)))]),
    ]
    pairs = [(0, 1, crossed_a, 0), (3, 0, below_a, 0), (1, 0, above_a, 0), (2, 0, far, 0), (2, 1, far, 2)]
    for dy, dh, source, first in pairs + [(3, 1, turned, 0), (1, 1, turned, 2)]:
        place = tiles_ref.at[pl.ds(device(dy, dh, 0), 2)]
        jobs.append((place, [(None, marks_of(source, pl.ds(first, 2)))]))
    mark_waits = copies(sems.at[21:], jobs)
    own, core = at.orbital(1), got_b.at[20:]
    crossed, below, above = (v.at[4:] for v in (crossed_b, below_b, above_b))
    not_ = jnp.logical_not
    same_h, same_c, from_below = at.same_h[2], at.same_c[2], at.away[2] == 1
    jobs = [
        (second_ref, arrived(at, 2, own, core, crossed, own, below, above, own)),
        (far_ref, [(same_h & same_c, own), (same_h & not_(same_c), core), (not_(same_h), crossed)]),
        (turn_ref, [(from_below, below), (not_(from_below), above)]),
    ]
    second_waits = copies(sems.at[30:], jobs)
    u_wait.wait()
    o_wait.wait()
    orbital = o_ref[0].astype(F32)
    columns = []
    for a in range(SHARE):
        density = u_ref[a].astype(F32) * orbital
        columns.append(
            jnp.concatenate([density[:, 128 * j : 128 * (j + 1)] for j in range(PAIRS_Y)], axis=0)
        )
    density = jnp.concatenate(columns, axis=1).astype(BF16)
    mz_wait.wait()
    zfreq = dot(density, mz_ref[...]).astype(BF16)
    stacked = jnp.concatenate([zfreq[:, 256 * i : 256 * (i + 1)] for i in range(4)], axis=0)
    ky_wait.wait()
    amp_wait.wait()
    jobs = [(out_hbm.at[g, pl.ds(64, 128)], [(None, amp_ref)]) for g in range(GRID)]
    out_waits = copies(sems.at[5:], jobs)
    out_ref[...] = dot(ky_ref[...], stacked).astype(BF16)
    jobs = [(out_hbm.at[g, pl.ds(0, 64)], [(None, out_ref.at[pl.ds(64 * g, 64)])]) for g in range(GRID)]
    wait_all(out_waits + mark_waits + second_waits + copies(sems.at[13:], jobs))


def middle_body(
    y_hbm, weight_ref, turn_hbm, kx_hbm, kxt_hbm, out_hbm, y_ref, turn_ref, kx_ref, kxt_ref, out_ref, sems
):
    jobs = [(y_ref, y_hbm.at[:, pl.ds(0, 64)]), (turn_ref, turn_hbm), (kx_ref, kx_hbm), (kxt_ref, kxt_hbm)]
    y_wait, turn_wait, kx_wait, kxt_wait = copies(sems, [(t, [(None, v)]) for t, v in jobs])
    weights = jnp.concatenate([weight_ref[...], weight_ref[...]], axis=1)
    y_wait.wait()
    turn_wait.wait()
    turn = turn_ref[...]
    yfreq = y_ref[...].reshape(512, 256)
    both = jnp.concatenate([yfreq, dot(yfreq, turn).astype(BF16)], axis=0)
    kx_wait.wait()
    potential = (dot(kx_ref[...], both) * weights).astype(BF16)
    both = jnp.concatenate([potential, dot(potential, turn).astype(BF16)], axis=0)
    kxt_wait.wait()
    out_ref[...] = dot(kxt_ref[...], both).astype(BF16)
    wait_all(copies(sems.at[4:], [(out_hbm, [(None, out_ref)])]))


def backward_body(
    ablock_ref,
    pairs_ref,
    fields,
    occupied,
    second,
    far,
    turned,
    turn_hbm,
    kyt_hbm,
    mzt_hbm,
    h_ref,
    out_ref,
    o_ref,
    turn_ref,
    kyt_ref,
    mzt_ref,
    sems,
):
    at = Roots(ablock_ref, pairs_ref, fields, occupied)
    jobs = [
        (o_ref, arrived(at, 2, second, second, second, far, second, second, turned)),
        (turn_ref, [(None, turn_hbm)]),
        (kyt_ref, [(None, kyt_hbm)]),
        (mzt_ref, [(None, mzt_hbm)]),
    ]
    o_wait, turn_wait, kyt_wait, mzt_wait = copies(sems, jobs)
    freq = h_ref[...]
    turn_wait.wait()
    both = jnp.concatenate([freq, dot(freq, turn_ref[...]).astype(BF16)], axis=0)
    kyt_wait.wait()
    zfreq = dot(kyt_ref[...], both).astype(BF16)
    zfreq = jnp.concatenate([zfreq[:256], zfreq[256:]], axis=1)
    mzt_wait.wait()
    value = dot(zfreq, mzt_ref[...])
    o_wait.wait()
    orbital = o_ref[0].astype(F32)
    for a in range(SHARE):
        rows = [value[8 * j : 8 * (j + 1), 128 * a : 128 * (a + 1)] for j in range(PAIRS_Y)]
        out_ref[a] = (jnp.concatenate(rows, axis=1) * orbital).astype(BF16)


def weight_body(tiles_ref, out_ref):
    tiles = tiles_ref[...].astype(F32).reshape(BAND * XL, 128).astype(BF16)
    shape = (BAND * N, BAND * XL)
    row = lax.broadcasted_iota(jnp.int32, shape, 0)
    lane = lax.broadcasted_iota(jnp.int32, shape, 1)
    spread = dot((row // XL == lane).astype(BF16), tiles)
    spread = jnp.where(row % XL == lane // 16, spread, 0.0).astype(BF16)
    row = lax.broadcasted_iota(jnp.int32, (128, 128), 0)
    lane = lax.broadcasted_iota(jnp.int32, (128, 128), 1)
    spread = dot(spread, (row % 16 == lane % 16).astype(BF16))
    low = lax.broadcasted_iota(jnp.int32, (N, 128), 1) % HALF < 16
    blocks = [spread[N * n : N * (n + 1)] for n in range(BAND)]
    kept = jnp.concatenate([jnp.where(low, blocks[2 * m], blocks[2 * m + 1]) for m in range(XL)], axis=0)
    shape = (N * XL, 128)
    row = lax.broadcasted_iota(jnp.int32, shape, 0)
    lane = lax.broadcasted_iota(jnp.int32, shape, 1)
    freq_x = signed_freq(row % N)
    freq_y = signed_freq(lax.axis_index("grid") * XL + row // N)
    freq_z = lane % HALF
    squared = (freq_x * freq_x + freq_y * freq_y + freq_z * freq_z).astype(F32)
    out_ref[...] = kept / (float(N * N * N) * (squared + 1.0))


def arrival_body(first, second, third, amp_ref, out_ref):
    out_ref[...] = amp_ref[...]


def copy_body(source, target, sems):
    wait_all(copies(sems, [(target, [(None, source)])]))


SMEM, VMEM, HBM = pltpu.SMEM, pltpu.VMEM, pltpu.HBM
PLANE = (XL, N * N)
LONG = (XL, N * N + 128)
GRIDPOINTS, MARKS = pl.ds(0, N * N), pl.ds(N * N, 128)


def plane(ref, *index):
    return ref.at[*index, :, GRIDPOINTS]


def marks_of(ref, *index):
    return ref.at[*index, :, MARKS]


def call(body, spaces, outs, out_spaces, scratch, args, dtype=BF16, flops=10**8):
    many = len(outs) > 1
    shapes = [jax.ShapeDtypeStruct(o, dtype) for o in outs]
    specs = [pl.BlockSpec(memory_space=m) for m in out_spaces]
    return pl.pallas_call(
        body,
        out_shape=shapes if many else shapes[0],
        in_specs=[pl.BlockSpec(memory_space=m) for m in spaces],
        out_specs=specs if many else specs[0],
        scratch_shapes=scratch,
        compiler_params=pltpu.CompilerParams(vmem_limit_bytes=VMEM_LIMIT),
        cost_estimate=pl.CostEstimate(flops=flops, bytes_accessed=2**20, transcendentals=0),
    )(*args)


def slab_body(last, names, u_ref, *refs):
    pieces = 2 * len(names)
    w_refs, extra = refs[:pieces], refs[pieces:-2]
    out_ref, total = refs[-2:]
    right = jnp.concatenate([w[...] for w in w_refs], axis=0)
    total[...] = lax.dot_general(u_ref[...], right, (((1,), (1,)), ((), ())), preferred_element_type=F32)
    gram = total[...]
    wide = gram.shape[1]
    row = lax.broadcasted_iota(jnp.int32, gram.shape, 0) % XL
    col = lax.broadcasted_iota(jnp.int32, gram.shape, 1) % XL
    gram = jnp.where(row == col, gram, 0.0)
    gram = jnp.sum(gram.reshape(gram.shape[0] // XL, XL, wide), axis=1)
    y, h, c = position()
    row = lax.broadcasted_iota(jnp.int32, (SHARE * XL, 128), 0) // XL
    lane = lax.broadcasted_iota(jnp.int32, (SHARE * XL, 128), 1) % ABLK
    pick = []
    for dy, dh in names:
        for dc in range(2):
            first = 32 * ((c + dc) % 2) + 8 * ((y - dy + 4) % 4) + 4 * ((h + dh) % 2)
            pick.append((lane == first + row).astype(BF16))
    pick = jnp.concatenate(pick, axis=0)
    high = gram.astype(BF16)
    rest = gram - high.astype(F32)
    middle = rest.astype(BF16)
    slab = dot(high, pick) + dot(middle, pick) + dot((rest - middle.astype(F32)).astype(BF16), pick)
    if extra:
        slab = slab + extra[0][...]
    if not last:
        out_ref[...] = slab
    else:
        lane = lax.broadcasted_iota(jnp.int32, slab.shape, 1)
        zero = jnp.zeros_like(slab)
        slab = jnp.concatenate(
            [jnp.where(lane < ABLK, slab, zero), jnp.where(lane < ABLK, zero, slab)], axis=0
        )
        high = slab.astype(BF16)
        low = (slab - high.astype(F32)).astype(BF16)
        amp = extra[1][:, pl.ds(64, 128)].reshape(1024, 256)
        out_ref[...] = (dot(amp, high) + dot(amp, low)).astype(BF16)


def slab_call(names, fields, parts, extra=()):
    last = len(extra) > 1
    tall = fields.shape[0]
    wide = sum(p.shape[0] for p in parts)
    out = (1024, 128) if last else (tall // XL, 128)
    args = (fields, *parts, *extra)
    return pl.pallas_call(
        functools.partial(slab_body, last, names),
        out_shape=jax.ShapeDtypeStruct(out, BF16 if last else F32),
        in_specs=[pl.BlockSpec(memory_space=VMEM)] * len(args),
        out_specs=pl.BlockSpec(memory_space=VMEM),
        scratch_shapes=[VMEM((tall, wide), F32)],
        compiler_params=pltpu.CompilerParams(vmem_limit_bytes=24 * 1024 * 1024),
        cost_estimate=pl.CostEstimate(
            flops=2 * tall * wide * N * N, bytes_accessed=2 * tall * N * N, transcendentals=0
        ),
    )(*args)


def band_shift(value, dy, dh, dc):
    pairs = []
    for y in range(4):
        for h in range(2):
            for c in range(2):
                pairs.append((4 * y + 2 * h + c, 4 * ((y + dy) % 4) + 2 * ((h + dh) % 2) + (c + dc) % 2))
    return lax.ppermute(value, "band", pairs)


def per_device(virtual_field, occupied_field, amplitudes, ablock, pairs, kept_cells):
    far_memory = lambda v: pltpu.with_memory_space_constraint(v, HBM)
    const = {n: far_memory(jnp.asarray(v)) for n, v in tables().items()}
    roots = (ablock, pairs, far_memory(virtual_field), far_memory(occupied_field))
    root_spaces = [SMEM, SMEM, pl.ANY, pl.ANY]

    with jax.named_scope("block_scatter"):
        sems = lambda n: [pltpu.SemaphoreType.DMA((n,))]
        rows = lambda n: (n,) + PLANE
        held = lambda n: VMEM(rows(n), BF16)
        hop = lambda body, spaces, out, scratch, *args, flops=10**8: call(
            body, spaces, out, [pl.ANY] * len(out), scratch, args, flops=flops
        )
        any_ = [pl.ANY]
        sent_a = hop(
            core_a_body,
            [SMEM] + any_ * 4,
            [(13,) + LONG],
            [VMEM((1, XL, 128), BF16), VMEM(kept_cells.shape, jnp.int32), SMEM((1, 2), jnp.int32)] + sems(11),
            ablock,
            far_memory(pairs),
            far_memory(kept_cells),
            *roots[2:],
        )
        got_a = band_shift(sent_a, 0, 0, 1)
        sent_b, amp = call(
            core_b_body,
            root_spaces + any_,
            [rows(21), (128, 256)],
            any_ + [VMEM],
            [VMEM((128, 256), BF16)] + sems(7),
            roots + (far_memory(amplitudes),),
            flops=5 * 10**9,
        )
        up, down, across = hop(
            first_a_body,
            root_spaces + any_ * 2,
            [(5,) + LONG] * 3,
            sems(12),
            *roots,
            sent_a,
            got_a,
        )
        up, down, across, sent_b = lax.optimization_barrier((up, down, across, sent_b))
        below_a = band_shift(up, 1, 0, 0)
        above_a = band_shift(down, 3, 0, 0)
        crossed_a = band_shift(across, 0, 1, 0)
        got_b = band_shift(sent_b, 0, 0, 1)
        up, down, across = hop(
            first_b_body, root_spaces + any_, [rows(5)] * 3, sems(6), *roots, got_b
        )
        below_b = band_shift(up, 1, 0, 0)
        above_b = band_shift(down, 3, 0, 0)
        crossed_b = band_shift(across, 0, 1, 0)
        crossed_a, below_a, above_a, _ = lax.optimization_barrier((crossed_a, below_a, above_a, (up, down, across)))
        far, turn = hop(
            second_a_body,
            root_spaces + any_ * 6,
            [(5,) + LONG] * 2,
            sems(9),
            *roots,
            sent_a,
            got_a,
            got_b,
            crossed_a,
            below_a,
            above_a,
            flops=10**10,
        )
        far_a = band_shift(far, 2, 0, 0)
        turned_a = band_shift(turn, 0, 1, 0)

        behind = (crossed_b, below_b, above_b, amp)
        amp = call(arrival_body, any_ * 3 + [VMEM], [(128, 256)], [VMEM], [], behind, flops=10**10)
        far_a, turned_a, amp = lax.optimization_barrier((far_a, turned_a, amp))

    with jax.named_scope("transform"):
        big = VMEM((512, 1024), BF16)
        from_all = (GRID, 64 + 128, 256)
        freq, tiles, second, far, turn = call(
            forward_body,
            root_spaces + any_ * 14,
            [from_all, (BAND, XL, 128)] + [rows(1)] * 3,
            any_ + [VMEM] * 4,
            [held(SHARE), held(1), big, big, VMEM((512, 256), BF16), VMEM((128, 256), BF16)] + sems(33),
            roots
            + (sent_a, got_a, got_b, crossed_a, below_a, above_a, crossed_b, below_b, above_b, far_a, turned_a)
            + (amp, const["mz"], const["ky"]),
            flops=2 * 10**10,
        )
        freq = lax.all_to_all(freq, "grid", 0, 0, tiled=True)
        amp = freq
        far_b = band_shift(far, 2, 0, 0)
        turned_b = band_shift(turn, 0, 1, 0)
        weights = call(
            weight_body,
            [VMEM],
            [(N * XL, 128)],
            [VMEM],
            [],
            (tiles,),
            F32,
        )
        freq = call(
            middle_body,
            any_ + [VMEM] + any_ * 3,
            [(512, 256)],
            any_,
            [VMEM((GRID, 64, 256), BF16), VMEM((256, 256), BF16), big, big, VMEM((512, 256), BF16)] + sems(5),
            (freq, weights, const["turn"], const["kx"], const["kxt"]),
            flops=10**10,
        )
        freq = lax.all_to_all(freq, "grid", 0, 0, tiled=True)
        potential = call(
            backward_body,
            root_spaces + any_ * 6 + [VMEM],
            [(SHARE,) + PLANE],
            [VMEM],
            [held(1), VMEM((256, 256), BF16), big, VMEM((512, 512), BF16)] + sems(4),
            roots
            + (second, far_b, turned_b)
            + (const["turn"], const["kyt"], const["mzt"], freq),
        )

    with jax.named_scope("block_gather"):
        early, late = ((0, 0), (2, 0), (1, 0), (3, 0), (0, 1)), ((2, 1), (1, 1), (3, 1))
        shape = (virtual_field.shape[0] * XL, N * N)
        potential, fields = lax.optimization_barrier(
            (potential.reshape(SHARE * XL, N * N), virtual_field.reshape(shape))
        )
        fields = call(copy_body, [pl.ANY], [shape], [pl.ANY], sems(1), (far_memory(fields),))
        part = {(0, 0): potential}
        for k in (2, 1, 3):
            part[k, 0] = band_shift(potential, k, 0, 0)
        part[0, 1] = band_shift(potential, 0, 1, 0)

        def contract(names, *extra):
            pieces = [w for name in names for w in (part[name], band_shift(part[name], 0, 0, 1))]
            return slab_call(names, fields, pieces, extra)

        part[2, 0], part[0, 1], fields = lax.optimization_barrier((part[2, 0], part[0, 1], fields))
        part[2, 1] = band_shift(part[2, 0], 0, 1, 0)
        for k in (1, 3):
            part[k, 1] = band_shift(part[0, 1], k, 0, 0)
        slab = contract(early)
        *got, slab = lax.optimization_barrier([part[name] for name in late] + [slab])
        part.update(zip(late, got))
        terms = contract(late, slab, amp)

    with jax.named_scope("ladder"):
        terms = lax.all_to_all(
            terms.reshape(GRID * BAND, XL, 128), ("grid", "band"), 0, 0, tiled=True
        )
        ladder = jnp.sum(terms.astype(F32), axis=0)
        return ladder.reshape(1, 16, ABLK)


def solution(mesh):
    in_specs = (
        P("band", "grid", None),
        P("band", "grid", None),
        P(None, "band", "grid"),
        P(),
        P(),
        P(("grid", "band"), None),
    )
    out_specs = P(None, ("grid", "band"), None)
    return jax.shard_map(
        per_device, mesh=mesh, in_specs=in_specs, out_specs=out_specs, check_vma=False
    )
```

```python
import functools
import math

import jax
import jax.numpy as jnp
import numpy as np
from jax import lax
from jax.experimental import pallas as pl
from jax.experimental.pallas import tpu as pltpu
from jax.sharding import PartitionSpec as P


N = 64
HALF = 32
ABLK = 64
GRID = 8
BAND = 16
XL = 8
SHARE = ABLK // BAND
PAIRS_Y = 32
F32 = jnp.float32
BF16 = jnp.bfloat16
VMEM_LIMIT = 16 * 1024 * 1024


@functools.cache
def tables():
    index = np.arange(N)
    phase = (index[:, None] * index[None, :]) % N
    angle = np.float32(2.0 * math.pi / N) * phase.astype(np.float32)
    cosine = np.cos(angle).astype(np.float32)
    sine = np.sin(angle).astype(np.float32)
    eye_x = np.eye(XL, dtype=np.float32)
    z_plain = np.concatenate([cosine[:HALF].T, -sine[:HALF].T], axis=1)
    z_turned = np.concatenate([z_plain[:, HALF:], -z_plain[:, :HALF]], axis=1)
    mz = np.zeros((SHARE, 2, N, 2, 2, SHARE, N), np.float32)
    for a in range(SHARE):
        for p in range(2):
            mz[a, p, :, 0, p, a, :] = z_plain
            mz[a, p, :, 1, p, a, :] = z_turned
    mzt = np.zeros((2, SHARE, N, SHARE, 2, N), np.float32)
    for a in range(SHARE):
        for p in range(2):
            mzt[p, a, :, a, p, :] = z_plain.T
    by_parity = np.stack([cosine, sine], axis=1).reshape(N, 2, PAIRS_Y, 2)
    ky = np.einsum("ktjp,xw->kxtpjw", by_parity, eye_x)
    signed = np.stack([cosine, -sine], axis=1).reshape(N, 2, PAIRS_Y, 2)
    kyt = np.einsum("ktjp,xw->pjxtkw", signed, eye_x)
    by_slab = np.stack([cosine, sine], axis=1).reshape(N, 2, GRID, XL)
    kx = np.einsum("ktgx,lm->lktgmx", by_slab, eye_x)
    signed_slab = np.stack([cosine, -sine], axis=1).reshape(N, 2, GRID, XL)
    kxt = np.einsum("ktgx,lm->gmxtlk", signed_slab, eye_x)
    turn = np.zeros((SHARE, 2, HALF, SHARE, 2, HALF), np.float32)
    for a in range(SHARE):
        turn[a, 1, :, a, 0, :] = np.eye(HALF)
        turn[a, 0, :, a, 1, :] = -np.eye(HALF)
    shapes = {
        "mz": (mz, 512, 1024),
        "mzt": (mzt, 512, 512),
        "ky": (ky, 512, 1024),
        "kyt": (kyt, 512, 1024),
        "kx": (kx, 512, 1024),
        "kxt": (kxt, 512, 1024),
        "turn": (turn, 256, 256),
    }
    return {n: v.reshape(r, c).astype(BF16) for n, (v, r, c) in shapes.items()}


def dot(a, b):
    return jnp.dot(a, b, preferred_element_type=F32)


def signed_freq(index):
    return (index + N // 2) % N - N // 2


def position():
    band = lax.axis_index("band")
    return band // 4, (band // 2) % 2, band % 2


def root_of(device):
    return device // 4, (device // 2) % 2, device % 2


def copies(sems, jobs):
    waits = []
    for slot, (target, choices) in enumerate(jobs):
        for condition, source in choices:
            move = pltpu.make_async_copy(source, target, sems.at[slot])
            if condition is None:
                move.start()
            else:
                pl.when(condition)(move.start)
        waits.append(pltpu.make_async_copy(target, target, sems.at[slot]))
    return waits


def gather(sems, jobs, start=None):
    finish = start() if start else None
    moves = copies(sems, jobs)
    if finish:
        moves += finish()
    wait_all(moves)


def wait_all(waits):
    for move in waits:
        move.wait()


class Roots:
    def __init__(self, ablock_ref, pairs_ref, fields, occupied):
        self.y, self.h, self.c = position()
        self.fields, self.occupied = fields, occupied
        start = ablock_ref[0] * ABLK
        self.first = start % fields.shape[0]
        devices = [start // fields.shape[0]]
        self.local = []
        for k in range(2 if pairs_ref is not None else 0):
            index = pairs_ref[0, k]
            devices.append(index // occupied.shape[0])
            self.local.append(index % occupied.shape[0])
        roots = [root_of(d) for d in devices]
        self.away = [(self.y - y + 4) % 4 for y, _, _ in roots]
        self.same_h = [h == self.h for _, h, _ in roots]
        self.same_c = [c == self.c for _, _, c in roots]

    def block(self, core, dy, h, count):
        start = self.first + 32 * core + 8 * ((self.y + dy) % 4) + 4 * h
        return self.fields.at[pl.ds(start, count)]

    def orbital(self, k):
        return self.occupied.at[pl.ds(self.local[k], 1)]


def core_a_body(ablock_ref, pairs_hbm, kept_hbm, fields, occupied, out, marks, kept_ref, pairs_ref, sems):
    (pairs_wait,) = copies(sems.at[10:], [(pairs_ref, [(None, pairs_hbm)])])
    at = Roots(ablock_ref, None, fields, occupied)
    other, there = 1 - at.c, 1 - at.h
    sources = [at.block(other, dy, there, 4) for dy in (1, 3, 2)]
    jobs = [(plane(out, pl.ds(4 * i, 4)), [(None, v)]) for i, v in enumerate(sources)]

    def start():
        (wait,) = copies(sems.at[9:], [(kept_ref, [(None, kept_hbm)])])
        return functools.partial(finish, wait)

    def finish(wait):
        wait.wait()
        kept = kept_ref[...]
        in_x = (lax.broadcasted_iota(jnp.int32, (N, kept.shape[1]), 0) == kept // 16).astype(BF16)
        in_c = lax.broadcasted_iota(jnp.int32, (128, kept.shape[1]), 0) % 16 == kept % 16
        mask = lax.dot_general(
            in_x, in_c.astype(BF16), (((1,), (1,)), ((), ())), preferred_element_type=F32
        )
        row = lax.broadcasted_iota(jnp.int32, mask.shape, 0)
        lane = lax.broadcasted_iota(jnp.int32, mask.shape, 1)
        mask = jnp.where(row % XL == lane // 16, mask, 0.0)
        marks[0] = jnp.sum(mask.reshape(XL, XL, 128), axis=1).astype(BF16)
        move = pltpu.make_async_copy(marks, marks_of(out, pl.ds(0, 1)), sems.at[8])
        move.start()
        pairs_wait.wait()
        orbital = occupied.at[pl.ds(pairs_ref[0, 0] % occupied.shape[0], 1)]
        return [move] + copies(sems.at[3:], [(plane(out, pl.ds(12, 1)), [(None, orbital)])])

    gather(sems, jobs, start)


def core_b_body(ablock_ref, pairs_ref, fields, occupied, amp_hbm, out, amp_out, amp_ref, sems):
    at = Roots(ablock_ref, pairs_ref, fields, occupied)
    other, here, there = 1 - at.c, at.h, 1 - at.h
    sources = [at.block(other, dy, h, 4) for dy, h in ((1, here), (3, here), (0, there), (2, here), (0, here))]
    jobs = [(out.at[4 * i : 4 * i + 4], [(None, v)]) for i, v in enumerate(sources)]
    jobs.append((out.at[20:], [(None, at.orbital(1))]))
    moves = copies(sems, jobs)
    (amp_wait,) = copies(sems.at[6:], [(amp_ref, [(None, amp_hbm.at[0])])])
    amp_wait.wait()
    row = lax.broadcasted_iota(jnp.int32, (128, 256), 0)
    col = lax.broadcasted_iota(jnp.int32, (128, 256), 1)
    over_c = (((1,), (1,)), ((), ()))
    parity = [
        lax.dot_general((col == 2 * row + p).astype(BF16), amp_ref[...], over_c, preferred_element_type=F32)
        for p in range(2)
    ]
    amp_out[...] = jnp.concatenate(parity, axis=1).astype(BF16)
    wait_all(moves)


def own_marks(at, target, sent_a, got_a):
    return [
        (marks_of(target, pl.ds(at.c, 1)), [(None, marks_of(sent_a, pl.ds(0, 1)))]),
        (marks_of(target, pl.ds(1 - at.c, 1)), [(None, marks_of(got_a, pl.ds(0, 1)))]),
    ]


def first_a_body(ablock_ref, pairs_ref, fields, occupied, sent_a, got_a, up, down, across, sems):
    at = Roots(ablock_ref, pairs_ref, fields, occupied)
    mine, theirs = at.same_c[0], jnp.logical_not(at.same_c[0])
    jobs = []
    for i, (target, dy) in enumerate(((up, 1), (down, 3), (across, 2))):
        own = at.block(at.c, dy, 1 - at.h, 4)
        jobs.append((plane(target, pl.ds(0, 4)), [(mine, own), (theirs, plane(got_a, pl.ds(4 * i, 4)))]))
    mine, theirs = at.same_c[1], jnp.logical_not(at.same_c[1])
    for target in (up, down, across):
        partner = plane(got_a, pl.ds(12, 1))
        jobs.append((plane(target, pl.ds(4, 1)), [(mine, at.orbital(0)), (theirs, partner)]))
        jobs += own_marks(at, target, sent_a, got_a)
    gather(sems, jobs)


def first_b_body(ablock_ref, pairs_ref, fields, occupied, got_b, up, down, across, sems):
    at = Roots(ablock_ref, pairs_ref, fields, occupied)
    mine, theirs = at.same_c[0], jnp.logical_not(at.same_c[0])
    jobs = []
    for i, (target, dy, h) in enumerate(((up, 1, at.h), (down, 3, at.h), (across, 0, 1 - at.h))):
        own = at.block(at.c, dy, h, 4)
        jobs.append((target.at[:4], [(mine, own), (theirs, got_b.at[4 * i : 4 * i + 4])]))
    mine, theirs = at.same_c[2], jnp.logical_not(at.same_c[2])
    for target in (up, down, across):
        jobs.append((target.at[4:], [(mine, at.orbital(1)), (theirs, got_b.at[20:])]))
    gather(sems, jobs)


def second_a_body(
    ablock_ref, pairs_ref, fields, occupied, sent_a, got_a, got_b, crossed, below, above, far, turn, sems
):
    at = Roots(ablock_ref, pairs_ref, fields, occupied)
    not_ = jnp.logical_not
    jobs = []
    own_rows = (at.block(at.c, 2, at.h, 4), got_b.at[12:16], pl.ds(0, 4))
    own_orbital = (at.orbital(0), plane(got_a, pl.ds(12, 1)), pl.ds(4, 1))
    for k, (own, core, part) in enumerate((own_rows, own_orbital)):
        same_h, same_c = at.same_h[k], at.same_c[k]
        other = plane(crossed, part)
        choices = [(same_h & same_c, own), (same_h & not_(same_c), core), (not_(same_h), other)]
        jobs.append((plane(far, part), choices))
        from_below = at.away[k] == 1
        choices = [(from_below, plane(below, part)), (not_(from_below), plane(above, part))]
        jobs.append((plane(turn, part), choices))
    jobs += own_marks(at, far, sent_a, got_a)
    for target, first, source in ((far, 2, crossed), (turn, 0, below), (turn, 2, above)):
        jobs.append((marks_of(target, pl.ds(first, 2)), [(None, marks_of(source, pl.ds(0, 2)))]))
    gather(sems, jobs)


def arrived(at, k, own, core, cross, far, below, above, turned):
    not_ = jnp.logical_not
    away, same_h, same_c = at.away[k], at.same_h[k], at.same_c[k]
    return [
        ((away == 0) & same_h & same_c, own),
        ((away == 0) & same_h & not_(same_c), core),
        ((away == 0) & not_(same_h), cross),
        (away == 2, far),
        ((away == 1) & same_h, below),
        ((away == 3) & same_h, above),
        ((away % 2 == 1) & not_(same_h), turned),
    ]


def forward_body(
    ablock_ref,
    pairs_ref,
    fields,
    occupied,
    sent_a,
    got_a,
    got_b,
    crossed_a,
    below_a,
    above_a,
    crossed_b,
    below_b,
    above_b,
    far,
    turned,
    amp_hbm,
    mz_hbm,
    ky_hbm,
    out_hbm,
    tiles_ref,
    second_ref,
    far_ref,
    turn_ref,
    u_ref,
    o_ref,
    mz_ref,
    ky_ref,
    out_ref,
    amp_ref,
    sems,
):
    at = Roots(ablock_ref, pairs_ref, fields, occupied)
    rows = [crossed_b.at[:4], plane(far, pl.ds(0, 4)), below_b.at[:4], above_b.at[:4], plane(turned, pl.ds(0, 4))]
    orbital = [plane(v, pl.ds(4, 1)) for v in (crossed_a, far, below_a, above_a, turned)]
    jobs = [
        (u_ref, arrived(at, 0, at.block(at.c, 0, at.h, 4), got_b.at[16:20], *rows)),
        (o_ref, arrived(at, 1, at.orbital(0), plane(got_a, pl.ds(12, 1)), *orbital)),
    ]
    jobs += [(mz_ref, [(None, mz_hbm)]), (ky_ref, [(None, ky_hbm)]), (amp_ref, [(None, amp_hbm)])]
    u_wait, o_wait, mz_wait, ky_wait, amp_wait = copies(sems, jobs)
    device = lambda dy, dh, c: 4 * ((at.y + dy) % 4) + 2 * ((at.h + dh) % 2) + c
    jobs = [
        (tiles_ref.at[pl.ds(device(0, 0, at.c), 1)], [(None, marks_of(sent_a, pl.ds(0, 1)))]),
        (tiles_ref.at[pl.ds(device(0, 0, 1 - at.c), 1)], [(None, marks_of(got_a, pl.ds(0, 1)))]),
    ]
    pairs = [(0, 1, crossed_a, 0), (3, 0, below_a, 0), (1, 0, above_a, 0), (2, 0, far, 0), (2, 1, far, 2)]
    for dy, dh, source, first in pairs + [(3, 1, turned, 0), (1, 1, turned, 2)]:
        place = tiles_ref.at[pl.ds(device(dy, dh, 0), 2)]
        jobs.append((place, [(None, marks_of(source, pl.ds(first, 2)))]))
    mark_waits = copies(sems.at[21:], jobs)
    own, core = at.orbital(1), got_b.at[20:]
    crossed, below, above = (v.at[4:] for v in (crossed_b, below_b, above_b))
    not_ = jnp.logical_not
    same_h, same_c, from_below = at.same_h[2], at.same_c[2], at.away[2] == 1
    jobs = [
        (second_ref, arrived(at, 2, own, core, crossed, own, below, above, own)),
        (far_ref, [(same_h & same_c, own), (same_h & not_(same_c), core), (not_(same_h), crossed)]),
        (turn_ref, [(from_below, below), (not_(from_below), above)]),
    ]
    second_waits = copies(sems.at[30:], jobs)
    u_wait.wait()
    o_wait.wait()
    orbital = o_ref[0].astype(F32)
    columns = []
    for a in range(SHARE):
        density = u_ref[a].astype(F32) * orbital
        columns.append(
            jnp.concatenate([density[:, 128 * j : 128 * (j + 1)] for j in range(PAIRS_Y)], axis=0)
        )
    density = jnp.concatenate(columns, axis=1).astype(BF16)
    mz_wait.wait()
    zfreq = dot(density, mz_ref[...]).astype(BF16)
    stacked = jnp.concatenate([zfreq[:, 256 * i : 256 * (i + 1)] for i in range(4)], axis=0)
    ky_wait.wait()
    amp_wait.wait()
    jobs = [(out_hbm.at[g, pl.ds(64, 128)], [(None, amp_ref)]) for g in range(GRID)]
    out_waits = copies(sems.at[5:], jobs)
    out_ref[...] = dot(ky_ref[...], stacked).astype(BF16)
    jobs = [(out_hbm.at[g, pl.ds(0, 64)], [(None, out_ref.at[pl.ds(64 * g, 64)])]) for g in range(GRID)]
    wait_all(out_waits + mark_waits + second_waits + copies(sems.at[13:], jobs))


def middle_body(
    y_hbm, weight_ref, turn_hbm, kx_hbm, kxt_hbm, out_hbm, y_ref, turn_ref, kx_ref, kxt_ref, out_ref, sems
):
    jobs = [(y_ref, y_hbm.at[:, pl.ds(0, 64)]), (turn_ref, turn_hbm), (kx_ref, kx_hbm), (kxt_ref, kxt_hbm)]
    y_wait, turn_wait, kx_wait, kxt_wait = copies(sems, [(t, [(None, v)]) for t, v in jobs])
    weights = jnp.concatenate([weight_ref[...], weight_ref[...]], axis=1)
    y_wait.wait()
    turn_wait.wait()
    turn = turn_ref[...]
    yfreq = y_ref[...].reshape(512, 256)
    both = jnp.concatenate([yfreq, dot(yfreq, turn).astype(BF16)], axis=0)
    kx_wait.wait()
    potential = (dot(kx_ref[...], both) * weights).astype(BF16)
    both = jnp.concatenate([potential, dot(potential, turn).astype(BF16)], axis=0)
    kxt_wait.wait()
    out_ref[...] = dot(kxt_ref[...], both).astype(BF16)
    wait_all(copies(sems.at[4:], [(out_hbm, [(None, out_ref)])]))


def backward_body(
    ablock_ref,
    pairs_ref,
    fields,
    occupied,
    second,
    far,
    turned,
    turn_hbm,
    kyt_hbm,
    mzt_hbm,
    h_ref,
    out_ref,
    o_ref,
    turn_ref,
    kyt_ref,
    mzt_ref,
    sems,
):
    at = Roots(ablock_ref, pairs_ref, fields, occupied)
    jobs = [
        (o_ref, arrived(at, 2, second, second, second, far, second, second, turned)),
        (turn_ref, [(None, turn_hbm)]),
        (kyt_ref, [(None, kyt_hbm)]),
        (mzt_ref, [(None, mzt_hbm)]),
    ]
    o_wait, turn_wait, kyt_wait, mzt_wait = copies(sems, jobs)
    freq = h_ref[...]
    turn_wait.wait()
    both = jnp.concatenate([freq, dot(freq, turn_ref[...]).astype(BF16)], axis=0)
    kyt_wait.wait()
    zfreq = dot(kyt_ref[...], both).astype(BF16)
    zfreq = jnp.concatenate([zfreq[:256], zfreq[256:]], axis=1)
    mzt_wait.wait()
    value = dot(zfreq, mzt_ref[...])
    o_wait.wait()
    orbital = o_ref[0].astype(F32)
    for a in range(SHARE):
        rows = [value[8 * j : 8 * (j + 1), 128 * a : 128 * (a + 1)] for j in range(PAIRS_Y)]
        out_ref[a] = (jnp.concatenate(rows, axis=1) * orbital).astype(BF16)


def weight_body(tiles_ref, out_ref):
    tiles = tiles_ref[...].astype(F32).reshape(BAND * XL, 128).astype(BF16)
    shape = (BAND * N, BAND * XL)
    row = lax.broadcasted_iota(jnp.int32, shape, 0)
    lane = lax.broadcasted_iota(jnp.int32, shape, 1)
    spread = dot((row // XL == lane).astype(BF16), tiles)
    spread = jnp.where(row % XL == lane // 16, spread, 0.0).astype(BF16)
    row = lax.broadcasted_iota(jnp.int32, (128, 128), 0)
    lane = lax.broadcasted_iota(jnp.int32, (128, 128), 1)
    spread = dot(spread, (row % 16 == lane % 16).astype(BF16))
    low = lax.broadcasted_iota(jnp.int32, (N, 128), 1) % HALF < 16
    blocks = [spread[N * n : N * (n + 1)] for n in range(BAND)]
    kept = jnp.concatenate([jnp.where(low, blocks[2 * m], blocks[2 * m + 1]) for m in range(XL)], axis=0)
    shape = (N * XL, 128)
    row = lax.broadcasted_iota(jnp.int32, shape, 0)
    lane = lax.broadcasted_iota(jnp.int32, shape, 1)
    freq_x = signed_freq(row % N)
    freq_y = signed_freq(lax.axis_index("grid") * XL + row // N)
    freq_z = lane % HALF
    squared = (freq_x * freq_x + freq_y * freq_y + freq_z * freq_z).astype(F32)
    out_ref[...] = kept / (float(N * N * N) * (squared + 1.0))


def arrival_body(first, second, third, amp_ref, out_ref):
    out_ref[...] = amp_ref[...]


def copy_body(source, target, sems):
    wait_all(copies(sems, [(target, [(None, source)])]))


SMEM, VMEM, HBM = pltpu.SMEM, pltpu.VMEM, pltpu.HBM
PLANE = (XL, N * N)
LONG = (XL, N * N + 128)
GRIDPOINTS, MARKS = pl.ds(0, N * N), pl.ds(N * N, 128)


def plane(ref, *index):
    return ref.at[*index, :, GRIDPOINTS]


def marks_of(ref, *index):
    return ref.at[*index, :, MARKS]


def call(body, spaces, outs, out_spaces, scratch, args, dtype=BF16, flops=10**8):
    many = len(outs) > 1
    shapes = [jax.ShapeDtypeStruct(o, dtype) for o in outs]
    specs = [pl.BlockSpec(memory_space=m) for m in out_spaces]
    return pl.pallas_call(
        body,
        out_shape=shapes if many else shapes[0],
        in_specs=[pl.BlockSpec(memory_space=m) for m in spaces],
        out_specs=specs if many else specs[0],
        scratch_shapes=scratch,
        compiler_params=pltpu.CompilerParams(vmem_limit_bytes=VMEM_LIMIT),
        cost_estimate=pl.CostEstimate(flops=flops, bytes_accessed=2**20, transcendentals=0),
    )(*args)


def slab_body(last, names, u_ref, *refs):
    pieces = 2 * len(names)
    w_refs, extra = refs[:pieces], refs[pieces:-2]
    out_ref, total = refs[-2:]
    right = jnp.concatenate([w[...] for w in w_refs], axis=0)
    total[...] = lax.dot_general(u_ref[...], right, (((1,), (1,)), ((), ())), preferred_element_type=F32)
    gram = total[...]
    wide = gram.shape[1]
    row = lax.broadcasted_iota(jnp.int32, gram.shape, 0) % XL
    col = lax.broadcasted_iota(jnp.int32, gram.shape, 1) % XL
    gram = jnp.where(row == col, gram, 0.0)
    gram = jnp.sum(gram.reshape(gram.shape[0] // XL, XL, wide), axis=1)
    y, h, c = position()
    row = lax.broadcasted_iota(jnp.int32, (SHARE * XL, 128), 0) // XL
    lane = lax.broadcasted_iota(jnp.int32, (SHARE * XL, 128), 1) % ABLK
    pick = []
    for dy, dh in names:
        for dc in range(2):
            first = 32 * ((c + dc) % 2) + 8 * ((y - dy + 4) % 4) + 4 * ((h + dh) % 2)
            pick.append((lane == first + row).astype(BF16))
    pick = jnp.concatenate(pick, axis=0)
    high = gram.astype(BF16)
    rest = gram - high.astype(F32)
    middle = rest.astype(BF16)
    slab = dot(high, pick) + dot(middle, pick) + dot((rest - middle.astype(F32)).astype(BF16), pick)
    if extra:
        slab = slab + extra[0][...]
    if not last:
        out_ref[...] = slab
    else:
        lane = lax.broadcasted_iota(jnp.int32, slab.shape, 1)
        zero = jnp.zeros_like(slab)
        slab = jnp.concatenate(
            [jnp.where(lane < ABLK, slab, zero), jnp.where(lane < ABLK, zero, slab)], axis=0
        )
        high = slab.astype(BF16)
        low = (slab - high.astype(F32)).astype(BF16)
        amp = extra[1][:, pl.ds(64, 128)].reshape(1024, 256)
        out_ref[...] = (dot(amp, high) + dot(amp, low)).astype(BF16)


def slab_call(names, fields, parts, extra=()):
    last = len(extra) > 1
    tall = fields.shape[0]
    wide = sum(p.shape[0] for p in parts)
    out = (1024, 128) if last else (tall // XL, 128)
    args = (fields, *parts, *extra)
    return pl.pallas_call(
        functools.partial(slab_body, last, names),
        out_shape=jax.ShapeDtypeStruct(out, BF16 if last else F32),
        in_specs=[pl.BlockSpec(memory_space=VMEM)] * len(args),
        out_specs=pl.BlockSpec(memory_space=VMEM),
        scratch_shapes=[VMEM((tall, wide), F32)],
        compiler_params=pltpu.CompilerParams(vmem_limit_bytes=24 * 1024 * 1024),
        cost_estimate=pl.CostEstimate(
            flops=2 * tall * wide * N * N, bytes_accessed=2 * tall * N * N, transcendentals=0
        ),
    )(*args)


def band_shift(value, dy, dh, dc):
    pairs = []
    for y in range(4):
        for h in range(2):
            for c in range(2):
                pairs.append((4 * y + 2 * h + c, 4 * ((y + dy) % 4) + 2 * ((h + dh) % 2) + (c + dc) % 2))
    return lax.ppermute(value, "band", pairs)


def per_device(virtual_field, occupied_field, amplitudes, ablock, pairs, kept_cells):
    far_memory = lambda v: pltpu.with_memory_space_constraint(v, HBM)
    const = {n: far_memory(jnp.asarray(v)) for n, v in tables().items()}
    roots = (ablock, pairs, far_memory(virtual_field), far_memory(occupied_field))
    root_spaces = [SMEM, SMEM, pl.ANY, pl.ANY]

    with jax.named_scope("block_scatter"):
        sems = lambda n: [pltpu.SemaphoreType.DMA((n,))]
        rows = lambda n: (n,) + PLANE
        held = lambda n: VMEM(rows(n), BF16)
        hop = lambda body, spaces, out, scratch, *args, flops=10**8: call(
            body, spaces, out, [pl.ANY] * len(out), scratch, args, flops=flops
        )
        any_ = [pl.ANY]
        sent_a = hop(
            core_a_body,
            [SMEM] + any_ * 4,
            [(13,) + LONG],
            [VMEM((1, XL, 128), BF16), VMEM(kept_cells.shape, jnp.int32), SMEM((1, 2), jnp.int32)] + sems(11),
            ablock,
            far_memory(pairs),
            far_memory(kept_cells),
            *roots[2:],
        )
        got_a = band_shift(sent_a, 0, 0, 1)
        sent_b, amp = call(
            core_b_body,
            root_spaces + any_,
            [rows(21), (128, 256)],
            any_ + [VMEM],
            [VMEM((128, 256), BF16)] + sems(7),
            roots + (far_memory(amplitudes),),
            flops=5 * 10**9,
        )
        up, down, across = hop(
            first_a_body,
            root_spaces + any_ * 2,
            [(5,) + LONG] * 3,
            sems(12),
            *roots,
            sent_a,
            got_a,
        )
        up, down, across, sent_b = lax.optimization_barrier((up, down, across, sent_b))
        below_a = band_shift(up, 1, 0, 0)
        above_a = band_shift(down, 3, 0, 0)
        crossed_a = band_shift(across, 0, 1, 0)
        got_b = band_shift(sent_b, 0, 0, 1)
        up, down, across = hop(
            first_b_body, root_spaces + any_, [rows(5)] * 3, sems(6), *roots, got_b
        )
        below_b = band_shift(up, 1, 0, 0)
        above_b = band_shift(down, 3, 0, 0)
        crossed_b = band_shift(across, 0, 1, 0)
        crossed_a, below_a, above_a, _ = lax.optimization_barrier((crossed_a, below_a, above_a, (up, down, across)))
        far, turn = hop(
            second_a_body,
            root_spaces + any_ * 6,
            [(5,) + LONG] * 2,
            sems(9),
            *roots,
            sent_a,
            got_a,
            got_b,
            crossed_a,
            below_a,
            above_a,
            flops=10**10,
        )
        far_a = band_shift(far, 2, 0, 0)
        turned_a = band_shift(turn, 0, 1, 0)

        behind = (crossed_b, below_b, above_b, amp)
        amp = call(arrival_body, any_ * 3 + [VMEM], [(128, 256)], [VMEM], [], behind, flops=10**10)
        far_a, turned_a, amp = lax.optimization_barrier((far_a, turned_a, amp))

    with jax.named_scope("transform"):
        big = VMEM((512, 1024), BF16)
        from_all = (GRID, 64 + 128, 256)
        freq, tiles, second, far, turn = call(
            forward_body,
            root_spaces + any_ * 14,
            [from_all, (BAND, XL, 128)] + [rows(1)] * 3,
            any_ + [VMEM] * 4,
            [held(SHARE), held(1), big, big, VMEM((512, 256), BF16), VMEM((128, 256), BF16)] + sems(33),
            roots
            + (sent_a, got_a, got_b, crossed_a, below_a, above_a, crossed_b, below_b, above_b, far_a, turned_a)
            + (amp, const["mz"], const["ky"]),
            flops=2 * 10**10,
        )
        freq = lax.all_to_all(freq, "grid", 0, 0, tiled=True)
        amp = freq
        far_b = band_shift(far, 2, 0, 0)
        turned_b = band_shift(turn, 0, 1, 0)
        weights = call(
            weight_body,
            [VMEM],
            [(N * XL, 128)],
            [VMEM],
            [],
            (tiles,),
            F32,
        )
        freq = call(
            middle_body,
            any_ + [VMEM] + any_ * 3,
            [(512, 256)],
            any_,
            [VMEM((GRID, 64, 256), BF16), VMEM((256, 256), BF16), big, big, VMEM((512, 256), BF16)] + sems(5),
            (freq, weights, const["turn"], const["kx"], const["kxt"]),
            flops=10**10,
        )
        freq = lax.all_to_all(freq, "grid", 0, 0, tiled=True)
        potential = call(
            backward_body,
            root_spaces + any_ * 6 + [VMEM],
            [(SHARE,) + PLANE],
            [VMEM],
            [held(1), VMEM((256, 256), BF16), big, VMEM((512, 512), BF16)] + sems(4),
            roots
            + (second, far_b, turned_b)
            + (const["turn"], const["kyt"], const["mzt"], freq),
        )

    with jax.named_scope("block_gather"):
        early, late = ((0, 0), (2, 0), (1, 0), (3, 0), (0, 1)), ((2, 1), (1, 1), (3, 1))
        shape = (virtual_field.shape[0] * XL, N * N)
        potential, fields = lax.optimization_barrier(
            (potential.reshape(SHARE * XL, N * N), virtual_field.reshape(shape))
        )
        fields = call(copy_body, [pl.ANY], [shape], [pl.ANY], sems(1), (far_memory(fields),))
        part = {(0, 0): potential}
        part[0, 1] = band_shift(potential, 0, 1, 0)
        for k in (2, 1, 3):
            part[k, 0] = band_shift(potential, k, 0, 0)

        def contract(names, *extra):
            pieces = [w for name in names for w in (part[name], band_shift(part[name], 0, 0, 1))]
            return slab_call(names, fields, pieces, extra)

        part[2, 0], part[0, 1], fields = lax.optimization_barrier((part[2, 0], part[0, 1], fields))
        part[2, 1] = band_shift(part[2, 0], 0, 1, 0)
        for k in (1, 3):
            part[k, 1] = band_shift(part[0, 1], k, 0, 0)
        slab = contract(early)
        *got, slab = lax.optimization_barrier([part[name] for name in late] + [slab])
        part.update(zip(late, got))
        terms = contract(late, slab, amp)

    with jax.named_scope("ladder"):
        terms = lax.all_to_all(
            terms.reshape(GRID * BAND, XL, 128), ("grid", "band"), 0, 0, tiled=True
        )
        ladder = jnp.sum(terms.astype(F32), axis=0)
        return ladder.reshape(1, 16, ABLK)


def solution(mesh):
    in_specs = (
        P("band", "grid", None),
        P("band", "grid", None),
        P(None, "band", "grid"),
        P(),
        P(),
        P(("grid", "band"), None),
    )
    out_specs = P(None, ("grid", "band"), None)
    return jax.shard_map(
        per_device, mesh=mesh, in_specs=in_specs, out_specs=out_specs, check_vma=False
    )
```
